32 devices in a mesh: lon: 16 (over z, y, x), lat: 2 (over core).
Axes of the slice: x: 2, y: 2, z: 4, core: 2. Of those that a mesh axis runs over, the one named last changes fastest.
Arguments:
- inputs: bfloat16 [16, 512, 256], P('lat', 'lon'), may hold values from -6 to 6
- psi_raw: float32 [4, 16, 3, 257], P(None, 'lat'), may hold values from -6 to 6
- widths: int32 [16], P('lat'), may hold values from 1 to 4, as said below
- w_group: bfloat16 [4, 4, 256], replicated, may hold values from -1.5 to 1.5
- w_mix: bfloat16 [256, 256], replicated, may hold values from -0.375 to 0.375
- grad_out: bfloat16 [16, 512, 256], P('lat', 'lon'), may hold values from -6 to 6
Outputs:
- outputs: bfloat16 [16, 512, 256], P('lat', 'lon')
- grad_in: bfloat16 [16, 512, 256], P('lat', 'lon')
The draws below stay inside these ranges and needn't reach their ends.
Inputs may be any that keep to these rules, and one draw needn't show every extreme that they name: `widths`: let d be a row's distance to the nearer pole (min(i, 15 - i)). A row's width is at most min(4, max(1, 2 * 4 // (d + 1)) + 1); the row nearest each pole has width 4.
All inputs are finite; a program needn't handle non-finite values.
Results may differ from the reference program's by a relative error of at most 0.011.
Values may be sent and summed in bfloat16 or wider, within the bound.
No kernel may reach another device: no remote copies, remote signals or barrier semaphores. Data moves between devices by JAX's collectives and lax.ppermute only.
A program may use at most 192 MiB of HBM per device.

```python
from functools import partial
import jax
import jax.numpy as jnp
from jax import lax

C = 256
K = 4
GROUP = 4
SMAX = 4
LON_DEV = 32
TAPS = 257
NLAT = 16
NLON = 512


def draw_widths(key, part):
    row_index = jnp.arange(NLAT, dtype=jnp.int32)
    distance = jnp.minimum(row_index, NLAT - 1 - row_index)
    bound = jnp.minimum(SMAX, jnp.maximum(1, 2 * SMAX // (distance + 1)) + 1)
    chosen = jax.random.randint(key, (NLAT,), 0, 1 << 20, dtype=jnp.int32)
    drawn = 1 + chosen % bound
    return jnp.where(distance == 0, SMAX, drawn).astype(jnp.int32)


def level_of(key, extent, cuts, low, high):
    def one(dim, blocks):
        draws = jax.random.uniform(jax.random.fold_in(jax.random.fold_in(key, 6), dim), (blocks,), jnp.float32, low / len(cuts), high / len(cuts))
        return jnp.repeat(jnp.exp(draws), extent[dim] // blocks).reshape((-1,) + (1,) * (len(extent) - dim - 1))

    factor_of = one(*cuts[0])
    for cut in cuts[1:]:
        factor_of = factor_of * one(*cut)
    return factor_of


def gaussian(key, dims, scale, most, shards=(), kind=jnp.bfloat16):
    values = jax.random.normal(key, dims, jnp.float32) * scale
    if len(shards) > 0:
        values = level_of(key, dims, shards, -0.22, 0.18) * values
    return jnp.clip(values, min=-most, max=most).astype(kind)


def setup_inputs(seed: int = 0) -> dict:
    seeds = jax.random.split(jax.random.key(seed), 7)
    return {
        "inputs": gaussian(seeds[0], (NLAT, NLON, C), 1.0, 6.0, ((0, 2), (1, 16))),
        "psi_raw": gaussian(seeds[1], (K, NLAT, 3, TAPS), 1.0, 6.0, ((1, 2),), jnp.float32),
        "widths": draw_widths(jax.random.fold_in(seeds[6], 71), 0),
        "w_group": gaussian(seeds[3], (K, GROUP, C), (K * GROUP) ** -0.5, 1.5),
        "w_mix": gaussian(seeds[4], (C, C), C ** -0.5, 0.375),
        "grad_out": gaussian(seeds[5], (NLAT, NLON, C), 1.0, 6.0, ((0, 2), (1, 16))),
    }


def masked_filter(psi_raw, widths):
    taps = psi_raw.shape[-1]
    offset = jnp.arange(taps, dtype=jnp.int32) - SMAX * LON_DEV
    reach = widths.astype(jnp.int32)[:, None] * LON_DEV
    keep = (jnp.abs(offset)[None, :] <= reach).astype(jnp.float32)
    scale = lax.rsqrt(3.0 * (2.0 * reach.astype(jnp.float32) + 1.0))
    return (psi_raw * (keep * scale)[None, :, None, :]).astype(jnp.bfloat16)

def correlate(rows_data, filters):
    count = rows_data.shape[1]
    taps = filters.shape[-1]
    places = ((SMAX * LON_DEV - jnp.arange(taps, dtype=jnp.int32)) % count).astype(jnp.int32)
    kernel = jnp.zeros(filters.shape[:-1] + (count,), filters.dtype).at[..., places].set(filters)
    spectrum = jnp.fft.rfft(rows_data, axis=1)
    response = jnp.fft.rfft(kernel, axis=-1)
    combined = jnp.einsum('baf,afc->bfc', response, spectrum)
    return jnp.fft.irfft(combined, n=count, axis=1)

def reference(inputs, psi_raw, widths, w_group, w_mix, grad_out):
    filters = masked_filter(psi_raw, widths).astype(jnp.float32)
    padded_in = jnp.pad(inputs, ((1, 1), (0, 0), (0, 0)))
    grouped_w = w_group.astype(jnp.float32).reshape(K, GROUP, C // GROUP, GROUP)
    activation = partial(jax.nn.gelu, approximate=True)

    def forward_row(index):
        rows_data = lax.dynamic_slice_in_dim(padded_in, index, 3, 0).astype(jnp.float32)
        row_filters = lax.dynamic_slice_in_dim(filters, index, 1, 1)[:, 0]
        convolved = correlate(rows_data, row_filters).astype(jnp.bfloat16)
        convolved = lax.optimization_barrier(convolved).astype(jnp.float32)
        split_conv = convolved.reshape(K, NLON, C // GROUP, GROUP)
        mixed_in = jnp.einsum('kjgq,kqgs->jgs', split_conv, grouped_w)
        mixed_in = mixed_in.astype(jnp.bfloat16).reshape(NLON, C)
        pre_act = jnp.dot(mixed_in, w_mix, preferred_element_type=jnp.float32)
        outputs = activation(pre_act).astype(jnp.bfloat16)
        _, backward = jax.vjp(activation, pre_act)
        cotangent = lax.dynamic_slice_in_dim(grad_out, index, 1, 0)[0].astype(jnp.float32)
        grad_pre, = backward(cotangent)
        grad_mixed = lax.dot_general(grad_pre.astype(jnp.bfloat16), w_mix, (((1,), (1,)), ((), ())), preferred_element_type=jnp.float32)
        return (outputs, grad_mixed.astype(jnp.bfloat16))
    outputs, grad_mixed = lax.map(forward_row, jnp.arange(NLAT, dtype=jnp.int32))
    padded_grad = jnp.pad(grad_mixed, ((1, 1), (0, 0), (0, 0)))
    flipped = jnp.pad(jnp.flip(filters, axis=3), ((0, 0), (1, 1), (0, 0), (0, 0)))

    def backward_row(index):
        grads = lax.dynamic_slice_in_dim(padded_grad, index, 3, 0).astype(jnp.float32)
        spread = jnp.einsum('ajgs,kqgs->akjgq', grads.reshape(3, NLON, C // GROUP, GROUP), grouped_w)
        spread = lax.optimization_barrier(spread.astype(jnp.bfloat16)).astype(jnp.float32)
        spread = spread.reshape(3, K, NLON, C)
        window = lax.dynamic_slice_in_dim(flipped, index, 3, 1)
        chosen = jnp.stack([window[:, 2 - row_tap, row_tap] for row_tap in range(3)], axis=0)
        sources = jnp.stack([spread[2 - row_tap] for row_tap in range(3)], axis=0)
        result = correlate(sources.reshape(3 * K, NLON, C), chosen.reshape(1, 3 * K, chosen.shape[-1]))
        return result[0].astype(jnp.bfloat16)
    grad_in = lax.map(backward_row, jnp.arange(NLAT, dtype=jnp.int32))
    return (outputs, grad_in)
```

```python
from functools import partial

import jax
import jax.numpy as jnp
from jax import lax
from jax.experimental import pallas as pl
from jax.experimental.pallas import tpu as pltpu
from jax.sharding import PartitionSpec as P

GROUP = 4
SMAX = 4


def extended_2(shard, sides, width):
    for axis, dim in sides:
        count, length = (lax.axis_size(axis), shard.shape[dim])
        up = [(i, (i + 1) % count) for i in range(count - 1)]
        down = [(j, i) for i, j in up]
        last = lax.slice_in_dim(shard, length - width, length, axis=dim)
        leading = lax.slice_in_dim(shard, 0, width, axis=dim)
        before = lax.ppermute(last, axis, up)
        after = lax.ppermute(leading, axis, down)
        shard = jnp.concatenate([before, shard, after], axis=dim)
    return shard


def from_behind(shard, axis, by):
    count = lax.axis_size(axis)
    return lax.ppermute(shard, axis, [(i, (i + by) % count) for i in range(count)])


def from_behind_2(value, axis, steps):
    count = lax.axis_size(axis)
    leading, last = (max(0, -steps), min(count, count - steps))
    return lax.ppermute(value, axis, [(source, source + steps) for source in range(leading, last)])


def masked_filter(psi_raw, widths, lon_dev):
    taps = psi_raw.shape[-1]
    offset = jnp.arange(taps, dtype=jnp.int32) - SMAX * lon_dev
    reach = widths[:, None] * lon_dev
    keep = (jnp.abs(offset)[None, :] <= reach).astype(jnp.float32)
    scale = lax.rsqrt(3.0 * (2.0 * reach.astype(jnp.float32) + 1.0))
    return (psi_raw * (keep * scale)[None, :, None, :]).astype(jnp.bfloat16)


def toeplitz_block(padded, shard_offset, lon_dev):
    first_cell = (shard_offset + SMAX) * lon_dev
    segment = padded[..., first_cell : first_cell + 2 * lon_dev - 1]
    leading = segment.shape[:-1]
    flattened = jnp.tile(segment, (1,) * len(leading) + (lon_dev,))
    flattened = flattened[..., lon_dev - 1 : lon_dev - 1 + lon_dev * (2 * lon_dev - 2)]
    return flattened.reshape(leading + (lon_dev, 2 * lon_dev - 2))[..., :lon_dev]


def extend_rows(values):
    return extended_2(values, (("lat", 0),), 1)


def stack_rows(values, row_count):
    return jnp.stack([values[row_tap : row_tap + row_count] for row_tap in range(3)], axis=1)


def spread_groups(values, grouped_w):
    count, lon_dev, channels = values.shape
    split_grad = values.reshape(count, lon_dev, channels // GROUP, GROUP)
    spread = jnp.einsum(
        "rjgs,kqgs->rkjgq", split_grad, grouped_w, preferred_element_type=jnp.float32
    )
    return spread.astype(jnp.bfloat16).reshape(count, grouped_w.shape[0], lon_dev, channels)


def row_window(row_count):
    band = lax.axis_index("lat")
    first = jnp.where(band == 0, 0, row_count - row_count).astype(jnp.int32)
    return (row_count, first)


def add_rows_at(running, term, first):
    return lax.dynamic_update_slice_in_dim(running, running + term, first, 0)


def sweep(extended, contribute):
    row_count = extended.shape[0] - 2
    running = contribute(extended, 0, 0, row_count)
    for distance in range(1, SMAX + 1):
        count, first = row_window(row_count)
        for direction in (1, -1):
            moved = from_behind(extended, "lon", direction * distance)
            term = contribute(moved, -direction * distance, first, count)
            running = add_rows_at(running, term, first)
    return running


def body(inputs, psi_raw, widths, w_group, w_mix, grad_out):
    row_count, lon_dev, channels = inputs.shape
    kernels = psi_raw.shape[0]
    groups = channels // GROUP
    grouped_w = w_group.reshape(kernels, GROUP, groups, GROUP)
    filters = masked_filter(psi_raw, widths, lon_dev)
    margin = ((0, 0), (0, 0), (0, 0), (lon_dev - 1, lon_dev - 1))
    padded_filter = jnp.pad(filters, margin)
    extended = extend_rows(inputs)

    def forward_part(portion, shard_offset, first, count):
        toeplitz = toeplitz_block(padded_filter, shard_offset, lon_dev)
        return jnp.einsum(
            "krtjp,rtpc->rkjc",
            toeplitz,
            stack_rows(portion, count),
            preferred_element_type=jnp.float32,
        )

    convolved = sweep(extended, forward_part).astype(jnp.bfloat16)
    split_conv = convolved.reshape(row_count, kernels, lon_dev, groups, GROUP)
    mixed_in = jnp.einsum(
        "rkjgq,kqgs->rjgs", split_conv, grouped_w, preferred_element_type=jnp.float32
    )
    mixed_in = mixed_in.astype(jnp.bfloat16).reshape(row_count * lon_dev, channels)
    pre_act = jnp.dot(mixed_in, w_mix, preferred_element_type=jnp.float32)
    activation = partial(jax.nn.gelu, approximate=True)
    outputs = activation(pre_act).astype(jnp.bfloat16).reshape(row_count, lon_dev, channels)
    _, backward = jax.vjp(activation, pre_act)
    (grad_pre,) = backward(grad_out.reshape(row_count * lon_dev, channels).astype(jnp.float32))
    grad_mixed = lax.dot_general(
        grad_pre.astype(jnp.bfloat16),
        w_mix,
        (((1,), (1,)), ((), ())),
        preferred_element_type=jnp.float32,
    )
    grad_mixed = grad_mixed.astype(jnp.bfloat16).reshape(row_count, lon_dev, channels)
    grad_conv = spread_groups(grad_mixed, grouped_w)

    def partial_at(shard_offset):
        toeplitz = toeplitz_block(padded_filter, shard_offset, lon_dev)
        terms = jnp.einsum(
            "krtjp,rkjc->rtpc", toeplitz, grad_conv, preferred_element_type=jnp.float32
        )
        placed = jnp.pad(terms[:, 0], ((0, 2), (0, 0), (0, 0)))
        placed = placed + jnp.pad(terms[:, 1], ((1, 1), (0, 0), (0, 0)))
        return placed + jnp.pad(terms[:, 2], ((2, 0), (0, 0), (0, 0)))

    running = partial_at(0)
    for distance in range(1, SMAX + 1):
        count, first = row_window(row_count)
        for direction in (1, -1):
            returned = from_behind(
                partial_at(direction * distance).astype(jnp.bfloat16), "lon", direction * distance
            ).astype(jnp.float32)
            running = add_rows_at(running, returned, first)
    grad_sum = running[1 : row_count + 1]
    for direction in (1, -1):
        rim_row = running[row_count + 1] if direction == 1 else running[0]
        arrived = from_behind_2(rim_row.astype(jnp.bfloat16), "lat", direction).astype(
            rim_row.dtype
        )
        target = 0 if direction == 1 else row_count - 1
        grad_sum = grad_sum.at[target].add(arrived)
    return (outputs, grad_sum.astype(jnp.bfloat16))


LANES = 128


def width_bound(row, row_total):
    pole = min(row, row_total - 1 - row)
    return min(SMAX, max(1, 2 * SMAX // (pole + 1)) + 1)


def wide_rows(row_total):
    widest = [width_bound(row, row_total) == SMAX for row in range(row_total)]
    near = [any(widest[max(0, row - 1) : row + 2]) for row in range(row_total)]
    return (
        tuple(row for row in range(row_total) if widest[row]),
        tuple(row for row in range(row_total) if near[row]),
    )


def transpose_kernel(x_ref, o_ref):
    o_ref[...] = x_ref[...].astype(jnp.float32).T.astype(o_ref.dtype)


def transposed(values):
    return pl.pallas_call(
        transpose_kernel,
        out_shape=jax.ShapeDtypeStruct(values.shape[::-1], values.dtype),
    )(values)


def swap_chunks(tiles, chunk, lon_dev):
    count = len(tiles)
    turned = []
    for by in range(count):
        mixed = tiles[(count - 1 - by) % count]
        for b in range(count - 1):
            mixed = jnp.where(chunk == b, tiles[(b - by) % count], mixed)
        if by:
            mixed = pltpu.roll(mixed, LANES - lon_dev * by, 1)
        turned.append(mixed)
    result = []
    for b in range(count):
        mixed = turned[(b - count + 1) % count]
        for a in range(count - 1):
            mixed = jnp.where(chunk == a, turned[(b - a) % count], mixed)
        result.append(mixed)
    return result


def roll_rows(values, by):
    by %= values.shape[0]
    if by == 0:
        return values
    return jnp.concatenate([values[by:], values[:by]], axis=0)


def conv_kernel(wide, rows, kernels, lon_dev, per_block, x_ref, f_ref, g_ref, o_ref, xc, tt, te):
    per_tile = LANES // lon_dev
    height = x_ref.shape[1]
    band = rows // x_ref.shape[0]
    span = 2 * LANES
    lane = lax.broadcasted_iota(jnp.int32, (lon_dev, LANES), 1)
    line = lax.broadcasted_iota(jnp.int32, (lon_dev, LANES), 0)
    upper = lane >= line
    corner = lane == line
    for row in range(rows):
        for tap in range(3):
            for k in range(kernels):
                first = jnp.broadcast_to(f_ref[row, tap, pl.ds(k, 1), :LANES], (lon_dev, LANES))
                second = jnp.broadcast_to(
                    f_ref[row, tap, pl.ds(k, 1), LANES : 2 * LANES], (lon_dev, LANES)
                )
                first = pltpu.roll(first, 0, 1, stride=1, stride_axis=0)
                second = pltpu.roll(second, 0, 1, stride=1, stride_axis=0)
                here = pl.ds(k * lon_dev, lon_dev)
                tt[row, here, pl.ds(tap * span, LANES)] = jnp.where(upper, first, 0.0).astype(
                    tt.dtype
                )
                tt[row, here, pl.ds(tap * span + LANES, LANES)] = jnp.where(
                    upper, second, first
                ).astype(tt.dtype)
                if row in wide:
                    last = jnp.broadcast_to(
                        f_ref[row, tap, pl.ds(k, 1), 2 * LANES :], (lon_dev, LANES)
                    )
                    last = pltpu.roll(last, 0, 1, stride=1, stride_axis=0)
                    te[wide.index(row), here, pl.ds(tap * LANES, LANES)] = jnp.where(
                        corner, last, jnp.where(upper, 0.0, second)
                    ).astype(te.dtype)
    chunk = lax.broadcasted_iota(jnp.int32, (height, LANES), 1) // lon_dev
    blank = jnp.zeros((height, span), xc.dtype)
    xc[:, pl.ds(0, span)] = blank
    xc[:, pl.ds((rows + 1) * span, span)] = blank
    for group in range(rows // per_tile):
        source = (group * per_tile) // band
        at = (group * per_tile - source * band) * lon_dev
        tile = x_ref[source, :, pl.ds(at, LANES)].astype(jnp.float32)
        turned = [tile] + [pltpu.roll(tile, lon_dev * by, 1) for by in range(1, per_tile)]
        for inner in range(per_tile):
            row = group * per_tile + inner
            gathered = None
            for q in range(per_tile):
                piece = roll_rows(turned[(q - inner) % per_tile], per_block * (q - SMAX))
                gathered = piece if q == 0 else jnp.where(chunk == q, piece, gathered)
            gathered = gathered.astype(xc.dtype)
            xc[:, pl.ds((row + 1) * span, LANES)] = gathered
            xc[:, pl.ds((row + 1) * span + LANES, LANES)] = roll_rows(
                gathered, per_block * per_tile
            )
    along = (((1,), (1,)), ((), ()))
    for group in range(rows // per_tile):
        parts = []
        for inner in range(per_tile):
            row = group * per_tile + inner
            part = lax.dot_general(
                xc[:, pl.ds(row * span, 3 * span)],
                tt[row],
                along,
                preferred_element_type=jnp.float32,
            )
            if row in wide:
                beyond = jnp.concatenate(
                    [
                        roll_rows(
                            xc[:, pl.ds((row + tap) * span, LANES)], 2 * per_block * per_tile
                        )
                        for tap in range(3)
                    ],
                    axis=1,
                )
                part = part + lax.dot_general(
                    beyond, te[wide.index(row)], along, preferred_element_type=jnp.float32
                )
            parts.append(part)
        stacked = jnp.concatenate(
            [part.astype(jnp.bfloat16) for part in swap_chunks(parts, chunk, lon_dev)], axis=0
        )
        mixed = jnp.dot(g_ref[...], stacked, preferred_element_type=jnp.float32)
        source = (group * per_tile) // band
        at = (group * per_tile - source * band) * lon_dev
        o_ref[source, :, pl.ds(at, LANES)] = mixed.astype(o_ref.dtype)


def convolve(values, filters, mixer, wide, lon_dev, per_block):
    rows, _, kernels, _ = filters.shape
    height = values.shape[1]
    return pl.pallas_call(
        partial(conv_kernel, wide, rows, kernels, lon_dev, per_block),
        out_shape=jax.ShapeDtypeStruct(values.shape, values.dtype),
        scratch_shapes=[
            pltpu.VMEM((height, (rows + 2) * 2 * LANES), jnp.bfloat16),
            pltpu.VMEM((rows, kernels * lon_dev, 6 * LANES), jnp.bfloat16),
            pltpu.VMEM((len(wide), kernels * lon_dev, 3 * LANES), jnp.bfloat16),
        ],
        compiler_params=pltpu.CompilerParams(vmem_limit_bytes=40 * 2**20),
    )(values, filters, mixer)


def dense_kernel(m_ref, w_ref, g_ref, o_ref, d_ref):
    pre = lax.dot_general(
        m_ref[...], w_ref[...], (((0,), (0,)), ((), ())), preferred_element_type=jnp.float32
    )
    slope = 0.7978845608028654
    square = pre * pre
    bent = jnp.tanh(slope * (pre + 0.044715 * (square * pre)))
    half = 0.5 * (1.0 + bent)
    o_ref[...] = (pre * half).astype(o_ref.dtype)
    rise = half + 0.5 * pre * (1.0 - bent * bent) * (slope * (1.0 + 3.0 * 0.044715 * square))
    grad_pre = (g_ref[...].astype(jnp.float32) * rise).astype(jnp.bfloat16)
    d_ref[...] = lax.dot_general(
        w_ref[...], grad_pre, (((1,), (1,)), ((), ())), preferred_element_type=jnp.float32
    ).astype(d_ref.dtype)


def channel_body(inputs, psi_raw, widths, w_group, w_mix, grad_out):
    row_count, lon_dev, channels = inputs.shape
    kernels = psi_raw.shape[0]
    bands, blocks = lax.axis_size("lat"), lax.axis_size("lon")
    rows = bands * row_count
    cells = row_count * lon_dev
    everyone = ("lat", "lon")
    devices = bands * blocks
    share = channels // devices

    def exchange(values):
        moved = lax.all_to_all(values.reshape(devices, share, cells), everyone, 0, 0)
        return moved

    sent = exchange(transposed(inputs.reshape(cells, channels)))
    filters = masked_filter(psi_raw, widths, lon_dev)
    other = lax.ppermute(filters, "lat", [(0, 1), (1, 0)])
    lower = lax.axis_index("lat") == 0
    filters = jnp.concatenate(
        [jnp.where(lower, filters, other), jnp.where(lower, other, filters)], axis=1
    ).astype(jnp.float32)
    taps = filters.shape[-1]
    margin = 3 * LANES - taps
    forward_filters = jnp.pad(filters.transpose(1, 2, 0, 3), ((0, 0), (0, 0), (0, 0), (0, margin)))
    flipped = jnp.pad(jnp.flip(filters, axis=3), ((0, 0), (1, 1), (0, 0), (0, margin)))
    backward_filters = jnp.stack(
        [flipped[:, tap : tap + rows, 2 - tap] for tap in range(3)], axis=2
    ).transpose(1, 2, 0, 3)
    own = lax.axis_index(everyone) * share
    own_w = lax.dynamic_slice_in_dim(w_group, own, share, 2)
    height = blocks * share
    line = jnp.arange(height, dtype=jnp.int32) // GROUP
    same = (line[:, None] == line[None, :])[:, None, :]
    forward_mix = jnp.where(
        same, jnp.tile(own_w.transpose(2, 0, 1), (blocks, 1, height // GROUP)), 0
    ).reshape(height, kernels * height)
    backward_mix = jnp.where(
        same, jnp.tile(own_w.transpose(1, 0, 2), (height // GROUP, 1, blocks)), 0
    ).reshape(height, kernels * height)
    forward_wide, backward_wide = wide_rows(rows)
    mixed_in = exchange(
        convolve(
            sent.reshape(bands, height, cells), forward_filters, forward_mix, forward_wide,
            lon_dev, share,
        )
    )
    outputs, grad_mixed = pl.pallas_call(
        dense_kernel,
        out_shape=(
            jax.ShapeDtypeStruct((cells, channels), jnp.bfloat16),
            jax.ShapeDtypeStruct((channels, cells), jnp.bfloat16),
        ),
    )(mixed_in.reshape(channels, cells), w_mix, grad_out.reshape(cells, channels))
    grads = exchange(grad_mixed)
    grad_in = exchange(
        convolve(
            grads.reshape(bands, height, cells), backward_filters, backward_mix, backward_wide,
            lon_dev, share,
        )
    )
    grad_in = transposed(grad_in.reshape(channels, cells))
    return (
        outputs.reshape(row_count, lon_dev, channels),
        grad_in.reshape(row_count, lon_dev, channels),
    )


def solution(mesh):
    devices = mesh.shape["lat"] * mesh.shape["lon"]
    chosen = channel_body if mesh.shape["lat"] == 2 and devices == 32 else body
    return jax.shard_map(
        chosen,
        mesh=mesh,
        in_specs=(
            P("lat", "lon", None),
            P(None, "lat", None, None),
            P("lat"),
            P(),
            P(),
            P("lat", "lon", None),
        ),
        out_specs=(P("lat", "lon", None), P("lat", "lon", None)),
        check_vma=False,
    )
```

```python
from functools import partial

import jax
import jax.numpy as jnp
from jax import lax
from jax.experimental import pallas as pl
from jax.experimental.pallas import tpu as pltpu
from jax.sharding import PartitionSpec as P

GROUP = 4
SMAX = 4


def masked_filter(psi_raw, widths, lon_dev):
    taps = psi_raw.shape[-1]
    offset = jnp.arange(taps, dtype=jnp.int32) - SMAX * lon_dev
    reach = widths[:, None] * lon_dev
    keep = (jnp.abs(offset)[None, :] <= reach).astype(jnp.float32)
    scale = lax.rsqrt(3.0 * (2.0 * reach.astype(jnp.float32) + 1.0))
    return (psi_raw * (keep * scale)[None, :, None, :]).astype(jnp.bfloat16)


LANES = 128


def width_bound(row, row_total):
    pole = min(row, row_total - 1 - row)
    return min(SMAX, max(1, 2 * SMAX // (pole + 1)) + 1)


def wide_rows(row_count, bands):
    total = row_count * bands
    widest = [width_bound(row, total) == SMAX for row in range(total)]
    near = [any(widest[max(0, row - 1) : row + 2]) for row in range(total)]
    return tuple(
        tuple(row for row in range(row_count) if any(table[row::row_count]))
        for table in (widest, near)
    )


def transpose_kernel(x_ref, o_ref):
    o_ref[...] = x_ref[...].T


def transposed(values):
    return pl.pallas_call(
        transpose_kernel,
        out_shape=jax.ShapeDtypeStruct(values.shape[::-1], values.dtype),
    )(values)


def swap_chunks(tiles, chunk, lon_dev):
    count = len(tiles)
    turned = []
    for by in range(count):
        mixed = tiles[(count - 1 - by) % count]
        for b in range(count - 1):
            mixed = jnp.where(chunk == b, tiles[(b - by) % count], mixed)
        if by:
            mixed = pltpu.roll(mixed, LANES - lon_dev * by, 1)
        turned.append(mixed)
    result = []
    for b in range(count):
        mixed = turned[(b - count + 1) % count]
        for a in range(count - 1):
            mixed = jnp.where(chunk == a, turned[(b - a) % count], mixed)
        result.append(mixed)
    return result


def roll_rows(values, by):
    by %= values.shape[0]
    if by == 0:
        return values
    return jnp.concatenate([values[by:], values[:by]], axis=0)


def lay_toeplitz(wide, lon_dev, f_ref, t_ref, e_ref):
    rows, _, kernels, _ = f_ref.shape
    shape = (lon_dev, LANES)
    lane = lax.broadcasted_iota(jnp.int32, shape, 1)
    line = lax.broadcasted_iota(jnp.int32, shape, 0)
    upper = lane >= line
    corner = lane == line

    def turned(row, tap, k, tile):
        values = f_ref[row, tap, pl.ds(k, 1), pl.ds(tile * LANES, LANES)]
        return pltpu.roll(jnp.broadcast_to(values, shape), 0, 1, stride=1, stride_axis=0)

    for row in range(rows):
        for tap in range(3):
            for k in range(kernels):
                first = turned(row, tap, k, 0)
                second = turned(row, tap, k, 1)
                here = pl.ds(k * lon_dev, lon_dev)
                t_ref[row, here, pl.ds(tap * 2 * LANES, LANES)] = jnp.where(
                    upper, first, 0.0
                ).astype(t_ref.dtype)
                t_ref[row, here, pl.ds((tap * 2 + 1) * LANES, LANES)] = jnp.where(
                    upper, second, first
                ).astype(t_ref.dtype)
                if row in wide:
                    last = turned(row, tap, k, 2)
                    e_ref[wide.index(row), here, pl.ds(tap * LANES, LANES)] = jnp.where(
                        corner, last, jnp.where(upper, 0.0, second)
                    ).astype(e_ref.dtype)


def prepare_kernel(
    wide, lon_dev, f_ref, b_ref, w_ref, ft_ref, fe_ref, bt_ref, be_ref, fm_ref, bm_ref
):
    lay_toeplitz(wide[0], lon_dev, f_ref, ft_ref, fe_ref)
    lay_toeplitz(wide[1], lon_dev, b_ref, bt_ref, be_ref)
    height = fm_ref.shape[0]
    kernels = w_ref.shape[0]
    shape = (height, height)
    line = lax.broadcasted_iota(jnp.int32, shape, 0)
    lane = lax.broadcasted_iota(jnp.int32, shape, 1)
    same = (line // GROUP) == (lane // GROUP)
    for k in range(kernels):
        mixer = jnp.where(same, jnp.tile(w_ref[k], (height // (2 * GROUP), 1)), 0.0)
        here = pl.ds(k * height, height)
        bm_ref[:, here] = mixer.astype(bm_ref.dtype)
        fm_ref[:, here] = mixer.T.astype(fm_ref.dtype)


def prepare(forward_filters, backward_filters, own_w, wide, lon_dev, height):
    rows, _, kernels, _ = forward_filters.shape
    out_shape = []
    for some in wide:
        out_shape += [(rows, kernels * lon_dev, 6 * LANES), (len(some), kernels * lon_dev, 3 * LANES)]
    out_shape += [(height, kernels * height)] * 2
    return pl.pallas_call(
        partial(prepare_kernel, wide, lon_dev),
        out_shape=tuple(jax.ShapeDtypeStruct(shape, jnp.bfloat16) for shape in out_shape),
        compiler_params=pltpu.CompilerParams(vmem_limit_bytes=32 * 2**20),
    )(forward_filters, backward_filters, own_w)


def conv_kernel(
    wide, bands, lon_dev, per_block, own_ref, above_ref, below_ref, t_ref, e_ref, m_ref, o_ref, xc
):
    per_tile = LANES // lon_dev
    height, cells = own_ref.shape
    rows = cells // lon_dev
    span = 2 * LANES
    band = lax.axis_index("lat")
    chunk = lax.broadcasted_iota(jnp.int32, (height, LANES), 1) // lon_dev

    def unfold(tile, first, inners):
        tile = tile.astype(jnp.float32)
        turned = [tile] + [pltpu.roll(tile, lon_dev * by, 1) for by in range(1, per_tile)]
        for inner in inners:
            gathered = None
            for q in range(per_tile):
                piece = roll_rows(turned[(q - inner) % per_tile], per_block * (q - SMAX))
                gathered = piece if q == 0 else jnp.where(chunk == q, piece, gathered)
            gathered = gathered.astype(xc.dtype)
            at = (first + inner + 1) * span
            xc[:, pl.ds(at, LANES)] = gathered
            xc[:, pl.ds(at + LANES, LANES)] = roll_rows(gathered, per_block * per_tile)

    for first in range(0, rows, per_tile):
        unfold(own_ref[:, pl.ds(first * lon_dev, LANES)], first, range(per_tile))
    above = above_ref[:, pl.ds(cells - LANES, LANES)].astype(jnp.float32)
    unfold(jnp.where(band > 0, above, 0.0), -per_tile, [per_tile - 1])
    below = below_ref[:, pl.ds(0, LANES)].astype(jnp.float32)
    unfold(jnp.where(band < bands - 1, below, 0.0), rows, [0])

    along = (((1,), (1,)), ((), ()))
    for first in range(0, rows, per_tile):
        parts = []
        for row in range(first, first + per_tile):
            part = lax.dot_general(
                xc[:, pl.ds(row * span, 3 * span)],
                t_ref[row],
                along,
                preferred_element_type=jnp.float32,
            )
            if row in wide:
                beyond = jnp.concatenate(
                    [
                        roll_rows(
                            xc[:, pl.ds((row + tap) * span, LANES)], 2 * per_block * per_tile
                        )
                        for tap in range(3)
                    ],
                    axis=1,
                )
                part = part + lax.dot_general(
                    beyond, e_ref[wide.index(row)], along, preferred_element_type=jnp.float32
                )
            parts.append(part)
        stacked = jnp.concatenate(
            [part.astype(jnp.bfloat16) for part in swap_chunks(parts, chunk, lon_dev)], axis=0
        )
        mixed = jnp.dot(m_ref[...], stacked, preferred_element_type=jnp.float32)
        o_ref[:, pl.ds(first * lon_dev, LANES)] = mixed.astype(o_ref.dtype)


def from_bands(last, leading):
    count = lax.axis_size("lat")
    up = [(i, i + 1) for i in range(count - 1)]
    if count == 2 and last is leading:
        other = lax.ppermute(last, "lat", [(0, 1), (1, 0)])
        return other, other
    return lax.ppermute(last, "lat", up), lax.ppermute(leading, "lat", [(j, i) for i, j in up])


def convolve(values, toeplitz, beyond, mixer, wide, lon_dev, per_block):
    bands = lax.axis_size("lat")
    above, below = from_bands(values, values)
    height, cells = values.shape
    return pl.pallas_call(
        partial(conv_kernel, wide, bands, lon_dev, per_block),
        out_shape=jax.ShapeDtypeStruct(values.shape, values.dtype),
        scratch_shapes=[pltpu.VMEM((height, (cells // lon_dev + 2) * 2 * LANES), jnp.bfloat16)],
        compiler_params=pltpu.CompilerParams(vmem_limit_bytes=32 * 2**20),
    )(values, above, below, toeplitz, beyond, mixer)


def dense_kernel(m_ref, w_ref, g_ref, o_ref, d_ref):
    pre = lax.dot_general(
        m_ref[...], w_ref[...], (((0,), (0,)), ((), ())), preferred_element_type=jnp.float32
    )
    slope = 0.7978845608028654
    square = pre * pre
    bent = jnp.tanh(slope * (pre + 0.044715 * (square * pre)))
    half = 0.5 * (1.0 + bent)
    o_ref[...] = (pre * half).astype(o_ref.dtype)
    rise = half + 0.5 * pre * (1.0 - bent * bent) * (slope * (1.0 + 3.0 * 0.044715 * square))
    grad_pre = (g_ref[...].astype(jnp.float32) * rise).astype(jnp.bfloat16)
    d_ref[...] = lax.dot_general(
        w_ref[...], grad_pre, (((1,), (1,)), ((), ())), preferred_element_type=jnp.float32
    ).astype(d_ref.dtype)


def body(inputs, psi_raw, widths, w_group, w_mix, grad_out):
    row_count, lon_dev, channels = inputs.shape
    kernels = psi_raw.shape[0]
    blocks, bands = lax.axis_size("lon"), lax.axis_size("lat")
    cells = row_count * lon_dev
    share = channels // blocks
    wide = wide_rows(row_count, bands)

    def exchange(values):
        moved = lax.all_to_all(values.reshape(blocks, share, cells), "lon", 0, 0)
        return moved.reshape(channels, cells)

    turned = transposed(inputs.reshape(cells, channels))
    turned, psi_raw, widths, w_group = lax.optimization_barrier(
        (turned, psi_raw, widths, w_group)
    )
    columns = exchange(turned)
    filters = masked_filter(psi_raw, widths, lon_dev)
    band = lax.axis_index("lat")
    if bands == 2:
        rim = jnp.where(band == 0, filters[:, row_count - 1], filters[:, 0])
        rim = lax.ppermute(rim, "lat", [(0, 1), (1, 0)])[:, None]
        above = jnp.where(band == 1, rim, jnp.zeros_like(rim))
        below = jnp.where(band == 0, rim, jnp.zeros_like(rim))
    else:
        above, below = from_bands(filters[:, row_count - 1 :], filters[:, :1])
    margin = (0, 3 * LANES - filters.shape[-1])
    still = (0, 0)
    filters = filters.astype(jnp.float32)
    forward_filters = jnp.pad(filters.transpose(1, 2, 0, 3), (still, still, still, margin))
    extended = jnp.concatenate(
        [above.astype(jnp.float32), filters, below.astype(jnp.float32)], axis=1
    )
    flipped = jnp.pad(
        jnp.flip(extended, axis=3).transpose(1, 2, 0, 3), (still, still, still, margin)
    )
    backward_filters = jnp.stack(
        [flipped[tap : tap + row_count, 2 - tap] for tap in range(3)], axis=1
    )
    own_w = lax.dynamic_slice_in_dim(w_group, lax.axis_index("lon") * share, share, 2)
    own_w = jnp.tile(own_w.astype(jnp.float32), (1, 2, blocks))
    ready = prepare(forward_filters, backward_filters, own_w, wide, lon_dev, channels)
    mixed_in = exchange(
        convolve(columns, ready[0], ready[1], ready[4], wide[0], lon_dev, share)
    )
    outputs, grad_mixed = pl.pallas_call(
        dense_kernel,
        out_shape=(
            jax.ShapeDtypeStruct((cells, channels), jnp.bfloat16),
            jax.ShapeDtypeStruct((channels, cells), jnp.bfloat16),
        ),
    )(mixed_in, w_mix, grad_out.reshape(cells, channels))
    grads = exchange(grad_mixed)
    grad_in = exchange(convolve(grads, ready[2], ready[3], ready[5], wide[1], lon_dev, share))
    grad_in = transposed(grad_in)
    return (
        outputs.reshape(row_count, lon_dev, channels),
        grad_in.reshape(row_count, lon_dev, channels),
    )


def solution(mesh):
    return jax.shard_map(
        body,
        mesh=mesh,
        in_specs=(
            P("lat", "lon", None),
            P(None, "lat", None, None),
            P("lat"),
            P(),
            P(),
            P("lat", "lon", None),
        ),
        out_specs=(P("lat", "lon", None), P("lat", "lon", None)),
        check_vma=False,
    )
```

```python
from functools import partial

import jax
import jax.numpy as jnp
from jax import lax
from jax.experimental import pallas as pl
from jax.experimental.pallas import tpu as pltpu
from jax.sharding import PartitionSpec as P

GROUP = 4
SMAX = 4


def masked_filter(psi_raw, widths, lon_dev):
    taps = psi_raw.shape[-1]
    offset = jnp.arange(taps, dtype=jnp.int32) - SMAX * lon_dev
    reach = widths[:, None] * lon_dev
    keep = (jnp.abs(offset)[None, :] <= reach).astype(jnp.float32)
    scale = lax.rsqrt(3.0 * (2.0 * reach.astype(jnp.float32) + 1.0))
    return (psi_raw * (keep * scale)[None, :, None, :]).astype(jnp.bfloat16)


LANES = 128


def width_bound(row):
    return min(SMAX, max(1, 2 * SMAX // (row + 1)) + 1)


def reaches(row_count):
    bound = [width_bound(row) for row in range(row_count)]
    near = [max(bound[max(0, row - 1) : row + 2]) for row in range(row_count)]
    sent = [
        {by: sum(reach >= by for reach in table) for by in range(3, SMAX + 1)}
        for table in (near, bound)
    ]
    return (tuple(bound), sent[0]), (tuple(near), sent[1])


def main_span(reach, lon_dev):
    first = -SMAX if reach > 2 else -2
    return first, (2 * LANES if reach > 2 else LANES) // lon_dev


def flipped_band():
    return lax.axis_index("lat") >= (lax.axis_size("lat") + 1) // 2


def row_at(place, row_count, flipped):
    return jnp.where(flipped, row_count - 1 - place, place)


def lay_toeplitz(table, lon_dev, flipped, f_ref, t_ref, e_ref):
    row_count, _, kernels, _ = f_ref.shape
    shape = (lon_dev, LANES)
    lane = lax.broadcasted_iota(jnp.int32, shape, 1)
    line = lax.broadcasted_iota(jnp.int32, shape, 0)
    upper = lane >= line
    corner = lane == line
    low = lax.broadcasted_iota(jnp.int32, (kernels, LANES), 1) < LANES // 2

    def skewed(tile, k):
        spread = jnp.broadcast_to(tile[k : k + 1], shape)
        return pltpu.roll(spread, 0, 1, stride=1, stride_axis=0)

    for place in range(row_count):
        row = row_at(place, row_count, flipped)
        tails = [None] * kernels
        for tap in range(3):
            tiles = [f_ref[row, tap, :, pl.ds(i * LANES, LANES)] for i in range(3)]
            if table[place] <= 2:
                turned = [pltpu.roll(tile, LANES // 2, 1) for tile in tiles[:2]]
                tiles = [jnp.where(low, turned[0], turned[1]), turned[1]]
            width = (len(tiles) - 1) * LANES
            for k in range(kernels):
                here = pl.ds(k * lon_dev, lon_dev)
                before = 0.0
                for i, tile in enumerate(tiles[:-1]):
                    now = skewed(tile, k)
                    t_ref[place, here, pl.ds(tap * width + i * LANES, LANES)] = jnp.where(
                        upper, now, before
                    ).astype(t_ref.dtype)
                    before = now
                if table[place] != 3:
                    last = jnp.where(
                        corner, skewed(tiles[-1], k), jnp.where(upper, 0.0, before)
                    )
                    if tap:
                        last = tails[k] + pltpu.roll(last, tap * lon_dev, 1)
                    tails[k] = last
        if table[place] != 3:
            for k in range(kernels):
                e_ref[place, pl.ds(k * lon_dev, lon_dev), :] = tails[k].astype(e_ref.dtype)


def prepare_kernel(tables, lon_dev, f_ref, b_ref, w_ref, ft, fe, bt, be, fm, bm):
    flipped = flipped_band()
    lay_toeplitz(tables[0], lon_dev, flipped, f_ref, ft, fe)
    lay_toeplitz(tables[1], lon_dev, flipped, b_ref, bt, be)
    kernels, _, channels = w_ref.shape
    shape = (channels, channels)
    line = lax.broadcasted_iota(jnp.int32, shape, 0)
    lane = lax.broadcasted_iota(jnp.int32, shape, 1)
    same = (line // GROUP) == (lane // GROUP)
    for k in range(kernels):
        weights = w_ref[k].astype(jnp.float32)
        weights = jnp.concatenate([weights] * (channels // GROUP), axis=0)
        mixer = jnp.where(same, weights, 0.0).astype(fm.dtype)
        here = pl.ds(k * channels, channels)
        fm[here, :] = mixer
        bm[:, here] = mixer


def prepare(forward_filters, backward_filters, w_group, tables, lon_dev):
    row_count, _, kernels, _ = forward_filters.shape
    channels = w_group.shape[-1]
    out_shape = [
        (row_count, kernels * lon_dev, 6 * LANES),
        (row_count, kernels * lon_dev, LANES),
    ] * 2 + [(kernels * channels, channels), (channels, kernels * channels)]
    return pl.pallas_call(
        partial(prepare_kernel, tables, lon_dev),
        out_shape=tuple(jax.ShapeDtypeStruct(shape, jnp.bfloat16) for shape in out_shape),
        compiler_params=pltpu.CompilerParams(vmem_limit_bytes=32 * 2**20),
    )(forward_filters, backward_filters, w_group)


def assemble(bands, parts, xs):
    own, before, after, above, below = parts
    row_count, lon_dev, channels = own.shape
    band = lax.axis_index("lat")
    flipped = flipped_band()

    def put(part, shard):
        rows = part.shape[0]
        at = pl.ds((shard + SMAX) * lon_dev, lon_dev)
        if rows == row_count:
            xs[pl.ds(1, row_count), at, :] = part[...]
        else:
            xs[:, at, :] = jnp.zeros((row_count + 2, lon_dev, channels), xs.dtype)
            first = jnp.where(flipped, row_count - rows, 0)
            xs[pl.ds(1 + first, rows), at, :] = part[...]

    put(own, 0)
    for by in range(1, SMAX + 1):
        put(before[by - 1], -by)
        put(after[by - 1], by)
    span = pl.ds((SMAX - 2) * lon_dev, 5 * lon_dev)
    rim = above[...].astype(jnp.float32)
    xs[0, span, :] = jnp.where(band > 0, rim, 0.0).astype(xs.dtype)
    rim = below[...].astype(jnp.float32)
    xs[row_count + 1, span, :] = jnp.where(band < bands - 1, rim, 0.0).astype(xs.dtype)


def correlate(table, kernels, lon_dev, xs, t_ref, e_ref, z_ref):
    row_count = xs.shape[0] - 2
    channels = xs.shape[2]
    flipped = flipped_band()
    for place in range(row_count):
        row = row_at(place, row_count, flipped)
        first, count = main_span(table[place], lon_dev)
        start, width = (first + SMAX) * lon_dev, count * lon_dev
        window = xs[pl.ds(row, 3), pl.ds(start, width), :].reshape(3 * width, channels)
        total = jnp.dot(
            t_ref[place, :, pl.ds(0, 3 * width)], window, preferred_element_type=jnp.float32
        )
        if table[place] != 3:
            window = xs[pl.ds(row, 3), pl.ds(start + width, lon_dev), :]
            window = window.reshape(3 * lon_dev, channels)
            blank = jnp.zeros((LANES - 3 * lon_dev, channels), window.dtype)
            total = total + jnp.dot(
                e_ref[place],
                jnp.concatenate([window, blank], axis=0),
                preferred_element_type=jnp.float32,
            )
        total = total.astype(z_ref.dtype)
        here = pl.ds(pl.multiple_of(row * lon_dev, lon_dev), lon_dev)
        for k in range(kernels):
            z_ref[here, pl.ds(k * channels, channels)] = total[k * lon_dev : (k + 1) * lon_dev]


def forward_kernel(table, sent, bands, kernels, *refs):
    parts, refs = take_parts(refs)
    t_ref, e_ref, m_ref, w_ref, g_ref, o_ref, d_ref, *near_refs, xs, z_ref = refs
    row_count, lon_dev, channels = parts[0].shape
    assemble(bands, parts, xs)
    correlate(table, kernels, lon_dev, xs, t_ref, e_ref, z_ref)
    mixed_in = jnp.dot(z_ref[...], m_ref[...], preferred_element_type=jnp.float32)
    pre = jnp.dot(mixed_in.astype(jnp.bfloat16), w_ref[...], preferred_element_type=jnp.float32)
    slope = 0.7978845608028654
    square = pre * pre
    bent = jnp.tanh(slope * (pre + 0.044715 * (square * pre)))
    half = 0.5 * (1.0 + bent)
    shape = (row_count, lon_dev, channels)
    o_ref[...] = (pre * half).astype(o_ref.dtype).reshape(shape)
    rise = half + 0.5 * pre * (1.0 - bent * bent) * (slope * (1.0 + 3.0 * 0.044715 * square))
    grad_out = g_ref[...].reshape(row_count * lon_dev, channels).astype(jnp.float32)
    grad_pre = (grad_out * rise).astype(jnp.bfloat16)
    grad_mixed = lax.dot_general(
        grad_pre, w_ref[...], (((1,), (1,)), ((), ())), preferred_element_type=jnp.float32
    )
    d_ref[...] = grad_mixed.astype(d_ref.dtype).reshape(shape)
    flipped = flipped_band()
    for near_ref in near_refs:
        rows = near_ref.shape[0]
        near_ref[...] = d_ref[pl.ds(jnp.where(flipped, row_count - rows, 0), rows)]


def backward_kernel(table, bands, kernels, *refs):
    parts, refs = take_parts(refs)
    t_ref, e_ref, m_ref, o_ref, xs, z_ref = refs
    assemble(bands, parts, xs)
    correlate(table, kernels, o_ref.shape[1], xs, t_ref, e_ref, z_ref)
    grad_in = lax.dot_general(
        z_ref[...], m_ref[...], (((1,), (1,)), ((), ())), preferred_element_type=jnp.float32
    )
    o_ref[...] = grad_in.astype(o_ref.dtype).reshape(o_ref.shape)


def take_parts(refs):
    own, before, refs = refs[0], refs[1 : 1 + SMAX], refs[1 + SMAX :]
    after, above, below = refs[:SMAX], refs[SMAX], refs[SMAX + 1]
    return (own, before, after, above, below), refs[SMAX + 2 :]


def gather(own, near):
    bands, blocks = lax.axis_size("lat"), lax.axis_size("lon")
    row_count, lon_dev, channels = own.shape
    before, after = [], []
    for by in range(1, SMAX + 1):
        value = near.get(by, own)
        for side, result in ((1, before), (-1, after)):
            pairs = [
                (i * bands + band, (i + side * by) % blocks * bands + band)
                for band in range(bands)
                for i in range(blocks)
                if by not in near or band in (0, bands - 1)
            ]
            result.append(lax.ppermute(value, ("lon", "lat"), pairs))
    around = [before[1], before[0], own, after[0], after[1]]

    def edge(row):
        return jnp.concatenate([value[row] for value in around], axis=0)

    last, leading = edge(row_count - 1), edge(0)
    if bands == 2:
        rim = jnp.where(lax.axis_index("lat") == 0, last, leading)
        above = below = lax.ppermute(rim, "lat", [(0, 1), (1, 0)])
    else:
        up = [(i, i + 1) for i in range(bands - 1)]
        above = lax.ppermute(last, "lat", up)
        below = lax.ppermute(leading, "lat", [(j, i) for i, j in up])
    return (own, *before, *after, above, below)


def body(inputs, psi_raw, widths, w_group, w_mix, grad_out):
    row_count, lon_dev, channels = inputs.shape
    kernels = psi_raw.shape[0]
    bands = lax.axis_size("lat")
    (forward_table, forward_sent), (backward_table, backward_sent) = reaches(row_count)
    near = {
        by: lax.dynamic_slice_in_dim(
            inputs, jnp.where(flipped_band(), row_count - rows, 0), rows, 0
        )
        for by, rows in forward_sent.items()
    }
    arrived = gather(inputs, near)

    filters = masked_filter(psi_raw, widths, lon_dev)
    band = lax.axis_index("lat")
    if bands == 2:
        rim = jnp.where(band == 0, filters[:, row_count - 1], filters[:, 0])
        rim = lax.ppermute(rim, "lat", [(0, 1), (1, 0)])[:, None]
        above = jnp.where(band == 1, rim, jnp.zeros_like(rim))
        below = jnp.where(band == 0, rim, jnp.zeros_like(rim))
    else:
        up = [(i, i + 1) for i in range(bands - 1)]
        above = lax.ppermute(filters[:, row_count - 1 :], "lat", up)
        below = lax.ppermute(filters[:, :1], "lat", [(j, i) for i, j in up])
    margin = (0, 3 * LANES - filters.shape[-1])
    still = (0, 0)
    filters = filters.astype(jnp.float32)
    forward_filters = jnp.pad(filters.transpose(1, 2, 0, 3), (still, still, still, margin))
    extended = jnp.concatenate(
        [above.astype(jnp.float32), filters, below.astype(jnp.float32)], axis=1
    )
    flipped = jnp.pad(
        jnp.flip(extended, axis=3).transpose(1, 2, 0, 3), (still, still, still, margin)
    )
    backward_filters = jnp.stack(
        [flipped[tap : tap + row_count, 2 - tap] for tap in range(3)], axis=1
    )
    tables = (forward_table, backward_table)
    ft, fe, bt, be, fm, bm = prepare(forward_filters, backward_filters, w_group, tables, lon_dev)
    scratch = [
        pltpu.VMEM((row_count + 2, (2 * SMAX + 1) * lon_dev, channels), jnp.bfloat16),
        pltpu.VMEM((row_count * lon_dev, kernels * channels), jnp.bfloat16),
    ]
    params = pltpu.CompilerParams(vmem_limit_bytes=32 * 2**20)
    shape = jax.ShapeDtypeStruct(inputs.shape, jnp.bfloat16)
    outputs, grad_mixed, *nearest = pl.pallas_call(
        partial(forward_kernel, forward_table, backward_sent, bands, kernels),
        out_shape=(shape, shape)
        + tuple(
            jax.ShapeDtypeStruct((rows, lon_dev, channels), jnp.bfloat16)
            for rows in backward_sent.values()
        ),
        scratch_shapes=scratch,
        compiler_params=params,
    )(*arrived, ft, fe, fm, w_mix, grad_out)
    arrived = gather(grad_mixed, dict(zip(backward_sent, nearest)))
    grad_in = pl.pallas_call(
        partial(backward_kernel, backward_table, bands, kernels),
        out_shape=shape,
        scratch_shapes=scratch,
        compiler_params=params,
    )(*arrived, bt, be, bm)
    return outputs, grad_in


def solution(mesh):
    return jax.shard_map(
        body,
        mesh=mesh,
        in_specs=(
            P("lat", "lon", None),
            P(None, "lat", None, None),
            P("lat"),
            P(),
            P(),
            P("lat", "lon", None),
        ),
        out_specs=(P("lat", "lon", None), P("lat", "lon", None)),
        check_vma=False,
    )
```

```python
from functools import partial

import jax
import jax.numpy as jnp
from jax import lax
from jax.experimental import pallas as pl
from jax.experimental.pallas import tpu as pltpu
from jax.sharding import PartitionSpec as P

GROUP = 4
SMAX = 4


def masked_filter(psi_raw, widths, lon_dev):
    taps = psi_raw.shape[-1]
    offset = jnp.arange(taps, dtype=jnp.int32) - SMAX * lon_dev
    reach = widths[:, None] * lon_dev
    keep = (jnp.abs(offset)[None, :] <= reach).astype(jnp.float32)
    scale = lax.rsqrt(3.0 * (2.0 * reach.astype(jnp.float32) + 1.0))
    return (psi_raw * (keep * scale)[None, :, None, :]).astype(jnp.bfloat16)


LANES = 128


def width_bound(row):
    return min(SMAX, max(1, 2 * SMAX // (row + 1)) + 1)


def reaches(row_count):
    bound = [width_bound(row) for row in range(row_count)]
    near = [max(bound[max(0, row - 1) : row + 2]) for row in range(row_count)]
    return tuple(bound), tuple(near)


def main_span(reach, lon_dev):
    first = -SMAX if reach > 2 else -2
    return first, (2 * LANES if reach > 2 else LANES) // lon_dev


def flipped_band():
    return lax.axis_index("lat") >= (lax.axis_size("lat") + 1) // 2


def row_at(place, row_count, flipped):
    return jnp.where(flipped, row_count - 1 - place, place)


def lay_toeplitz(table, lon_dev, flipped, f_ref, s_ref, t_ref, e_ref):
    row_count, _, kernels, _ = f_ref.shape
    shape = (lon_dev, LANES)
    lane = lax.broadcasted_iota(jnp.int32, shape, 1)
    line = lax.broadcasted_iota(jnp.int32, shape, 0)
    upper = lane >= line
    corner = lane == line

    for place in range(row_count):
        row = row_at(place, row_count, flipped)
        source = s_ref if table[place] <= 2 else f_ref
        count = source.shape[-1] // LANES

        def skewed(tap, k, tile, shift=0):
            spread = source[row, tap, pl.ds(k, 1), pl.ds(tile * LANES, LANES)]
            return pltpu.roll(
                jnp.broadcast_to(spread, shape), shift, 1, stride=1, stride_axis=0
            )

        for k in range(kernels):
            here = pl.ds(k * lon_dev, lon_dev)
            tails = None
            for tap in range(3):
                before = 0.0
                for i in range(count - 1):
                    now = skewed(tap, k, i)
                    at = (tap * (count - 1) + i) * LANES
                    t_ref[place, here, pl.ds(at, LANES)] = jnp.where(upper, now, before).astype(
                        t_ref.dtype
                    )
                    before = now
                if table[place] != 3:
                    last = skewed(tap, k, count - 1)
                    last = jnp.where(corner, last, jnp.where(upper, 0.0, before))
                    tails = last if tap == 0 else tails + pltpu.roll(last, tap * lon_dev, 1)
            if table[place] != 3:
                e_ref[place, here, :] = tails.astype(e_ref.dtype)


def prepare_kernel(tables, lon_dev, f_ref, fs_ref, b_ref, bs_ref, w_ref, ft, fe, bt, be, fm, bm):
    flipped = flipped_band()
    lay_toeplitz(tables[0], lon_dev, flipped, f_ref, fs_ref, ft, fe)
    lay_toeplitz(tables[1], lon_dev, flipped, b_ref, bs_ref, bt, be)
    kernels, _, channels = w_ref.shape
    shape = (channels, channels)
    line = lax.broadcasted_iota(jnp.int32, shape, 0)
    lane = lax.broadcasted_iota(jnp.int32, shape, 1)
    same = (line // GROUP) == (lane // GROUP)
    for k in range(kernels):
        weights = w_ref[k].astype(jnp.float32)
        weights = jnp.concatenate([weights] * (channels // GROUP), axis=0)
        mixer = jnp.where(same, weights, 0.0).astype(fm.dtype)
        here = pl.ds(k * channels, channels)
        fm[here, :] = mixer
        bm[:, here] = mixer


def prepare(forward_filters, backward_filters, w_group, tables, lon_dev):
    row_count, _, kernels, _ = forward_filters.shape
    channels = w_group.shape[-1]
    half = LANES // 2
    out_shape = [
        (row_count, kernels * lon_dev, 6 * LANES),
        (row_count, kernels * lon_dev, LANES),
    ] * 2 + [(kernels * channels, channels), (channels, kernels * channels)]
    return pl.pallas_call(
        partial(prepare_kernel, tables, lon_dev),
        out_shape=tuple(jax.ShapeDtypeStruct(shape, jnp.bfloat16) for shape in out_shape),
        compiler_params=pltpu.CompilerParams(vmem_limit_bytes=32 * 2**20),
    )(
        forward_filters,
        forward_filters[..., half : half + 2 * LANES],
        backward_filters,
        backward_filters[..., half : half + 2 * LANES],
        w_group,
    )


def assemble(bands, all_ref, xs):
    blocks, held, lon_dev, channels = all_ref.shape
    row_count = xs.shape[0] - 2
    band, block = lax.axis_index("lat"), lax.axis_index("lon")
    for shard in range(-SMAX, SMAX + 1):
        source = lax.rem(block + shard + blocks, blocks)
        at = pl.ds((shard + SMAX) * lon_dev, lon_dev)
        xs[pl.ds(1, row_count), at, :] = all_ref[source, pl.ds(0, row_count)]
        rim = all_ref[source, row_count].astype(jnp.float32)
        xs[0, at, :] = jnp.where(band > 0, rim, 0.0).astype(xs.dtype)
        rim = all_ref[source, held - 1].astype(jnp.float32)
        xs[row_count + 1, at, :] = jnp.where(band < bands - 1, rim, 0.0).astype(xs.dtype)


def correlate(table, kernels, lon_dev, xs, t_ref, e_ref, z_ref):
    row_count = xs.shape[0] - 2
    channels = xs.shape[2]
    flipped = flipped_band()
    for place in range(row_count):
        row = row_at(place, row_count, flipped)
        first, count = main_span(table[place], lon_dev)
        start, width = (first + SMAX) * lon_dev, count * lon_dev
        window = xs[pl.ds(row, 3), pl.ds(start, width), :].reshape(3 * width, channels)
        total = jnp.dot(
            t_ref[place, :, pl.ds(0, 3 * width)], window, preferred_element_type=jnp.float32
        )
        if table[place] != 3:
            window = xs[pl.ds(row, 3), pl.ds(start + width, lon_dev), :]
            window = window.reshape(3 * lon_dev, channels)
            blank = jnp.zeros((LANES - 3 * lon_dev, channels), window.dtype)
            total = total + jnp.dot(
                e_ref[place],
                jnp.concatenate([window, blank], axis=0),
                preferred_element_type=jnp.float32,
            )
        total = total.astype(z_ref.dtype)
        here = pl.ds(pl.multiple_of(row * lon_dev, lon_dev), lon_dev)
        for k in range(kernels):
            z_ref[here, pl.ds(k * channels, channels)] = total[k * lon_dev : (k + 1) * lon_dev]


def forward_kernel(
    table, bands, kernels, a_ref, t_ref, e_ref, m_ref, w_ref, g_ref, o_ref, d_ref, xs, z_ref
):
    row_count, lon_dev, channels = g_ref.shape
    assemble(bands, a_ref, xs)
    correlate(table, kernels, lon_dev, xs, t_ref, e_ref, z_ref)
    mixed_in = jnp.dot(z_ref[...], m_ref[...], preferred_element_type=jnp.float32)
    pre = jnp.dot(mixed_in.astype(jnp.bfloat16), w_ref[...], preferred_element_type=jnp.float32)
    slope = 0.7978845608028654
    square = pre * pre
    bent = jnp.tanh(slope * (pre + 0.044715 * (square * pre)))
    half = 0.5 * (1.0 + bent)
    shape = (row_count, lon_dev, channels)
    o_ref[...] = (pre * half).astype(o_ref.dtype).reshape(shape)
    rise = half + 0.5 * pre * (1.0 - bent * bent) * (slope * (1.0 + 3.0 * 0.044715 * square))
    grad_out = g_ref[...].reshape(row_count * lon_dev, channels).astype(jnp.float32)
    grad_pre = (grad_out * rise).astype(jnp.bfloat16)
    grad_mixed = lax.dot_general(
        grad_pre, w_ref[...], (((1,), (1,)), ((), ())), preferred_element_type=jnp.float32
    )
    d_ref[...] = grad_mixed.astype(d_ref.dtype).reshape(shape)


def backward_kernel(table, bands, kernels, a_ref, t_ref, e_ref, m_ref, o_ref, xs, z_ref):
    assemble(bands, a_ref, xs)
    correlate(table, kernels, o_ref.shape[1], xs, t_ref, e_ref, z_ref)
    grad_in = lax.dot_general(
        z_ref[...], m_ref[...], (((1,), (1,)), ((), ())), preferred_element_type=jnp.float32
    )
    o_ref[...] = grad_in.astype(o_ref.dtype).reshape(o_ref.shape)


def gather(own):
    bands = lax.axis_size("lat")
    last, leading = own[-1:], own[:1]
    if bands == 2:
        rim = jnp.where(lax.axis_index("lat") == 0, last, leading)
        rims = [lax.ppermute(rim, "lat", [(0, 1), (1, 0)])]
    else:
        up = [(i, i + 1) for i in range(bands - 1)]
        rims = [
            lax.ppermute(last, "lat", up),
            lax.ppermute(leading, "lat", [(j, i) for i, j in up]),
        ]
    return lax.all_gather(jnp.concatenate([own, *rims], axis=0), "lon", axis=0)


def body(inputs, psi_raw, widths, w_group, w_mix, grad_out):
    row_count, lon_dev, channels = inputs.shape
    kernels = psi_raw.shape[0]
    bands = lax.axis_size("lat")
    forward_table, backward_table = reaches(row_count)
    arrived = gather(inputs)

    filters = masked_filter(psi_raw, widths, lon_dev)
    band = lax.axis_index("lat")
    if bands == 2:
        rim = jnp.where(band == 0, filters[:, row_count - 1], filters[:, 0])
        rim = lax.ppermute(rim, "lat", [(0, 1), (1, 0)])[:, None]
        above = jnp.where(band == 1, rim, jnp.zeros_like(rim))
        below = jnp.where(band == 0, rim, jnp.zeros_like(rim))
    else:
        up = [(i, i + 1) for i in range(bands - 1)]
        above = lax.ppermute(filters[:, row_count - 1 :], "lat", up)
        below = lax.ppermute(filters[:, :1], "lat", [(j, i) for i, j in up])
    margin = (0, 3 * LANES - filters.shape[-1])
    still = (0, 0)
    filters = filters.astype(jnp.float32)
    forward_filters = jnp.pad(filters.transpose(1, 2, 0, 3), (still, still, still, margin))
    extended = jnp.concatenate(
        [above.astype(jnp.float32), filters, below.astype(jnp.float32)], axis=1
    )
    flipped = jnp.pad(
        jnp.flip(extended, axis=3).transpose(1, 2, 0, 3), (still, still, still, margin)
    )
    backward_filters = jnp.stack(
        [flipped[tap : tap + row_count, 2 - tap] for tap in range(3)], axis=1
    )
    tables = (forward_table, backward_table)
    ft, fe, bt, be, fm, bm = prepare(forward_filters, backward_filters, w_group, tables, lon_dev)
    scratch = [
        pltpu.VMEM((row_count + 2, (2 * SMAX + 1) * lon_dev, channels), jnp.bfloat16),
        pltpu.VMEM((row_count * lon_dev, kernels * channels), jnp.bfloat16),
    ]
    params = pltpu.CompilerParams(vmem_limit_bytes=32 * 2**20)
    shape = jax.ShapeDtypeStruct(inputs.shape, jnp.bfloat16)
    outputs, grad_mixed = pl.pallas_call(
        partial(forward_kernel, forward_table, bands, kernels),
        out_shape=(shape, shape),
        scratch_shapes=scratch,
        compiler_params=params,
    )(arrived, ft, fe, fm, w_mix, grad_out)
    grad_in = pl.pallas_call(
        partial(backward_kernel, backward_table, bands, kernels),
        out_shape=shape,
        scratch_shapes=scratch,
        compiler_params=params,
    )(gather(grad_mixed), bt, be, bm)
    return outputs, grad_in


def solution(mesh):
    return jax.shard_map(
        body,
        mesh=mesh,
        in_specs=(
            P("lat", "lon", None),
            P(None, "lat", None, None),
            P("lat"),
            P(),
            P(),
            P("lat", "lon", None),
        ),
        out_specs=(P("lat", "lon", None), P("lat", "lon", None)),
        check_vma=False,
    )
```

```python
from functools import partial

import jax
import jax.numpy as jnp
from jax import lax
from jax.experimental import pallas as pl
from jax.experimental.pallas import tpu as pltpu
from jax.sharding import PartitionSpec as P

GROUP = 4
SMAX = 4


LANES = 128
BF16 = jnp.bfloat16
ALONG = (((1,), (1,)), ((), ()))


def width_bound(row, row_total):
    pole = min(row, row_total - 1 - row)
    return min(SMAX, max(1, 2 * SMAX // (pole + 1)) + 1)


def wide_rows(row_count, bands, total):
    widest = [width_bound(row, total) == SMAX for row in range(total)]
    near = [any(widest[max(0, row - 1) : row + 2]) for row in range(total)]
    return tuple(
        tuple(row for row in range(row_count) if any(table[row::row_count]))
        for table in (widest, near)
    )


def iota(shape, axis):
    return lax.broadcasted_iota(jnp.int32, shape, axis)


def turned_by_identity(values):
    count = values.shape[1]
    unit = jnp.where(iota((count, count), 0) == iota((count, count), 1), 1.0, 0.0).astype(BF16)
    return lax.dot_general(unit, values, ALONG, preferred_element_type=jnp.float32).astype(BF16)


def transpose_kernel(x_ref, o_ref):
    o_ref[...] = turned_by_identity(x_ref[...])


def transposed(values):
    return pl.pallas_call(
        transpose_kernel,
        out_shape=jax.ShapeDtypeStruct(values.shape[::-1], values.dtype),
    )(values)


def enter_kernel(lon_dev, w_ref, x_ref, p_ref, o_ref, f_ref):
    o_ref[...] = turned_by_identity(x_ref[...])
    kernels, taps, rows, cells = p_ref.shape
    shape = (rows, LANES)
    line, lane = iota(shape, 0), iota(shape, 1)
    reach = jnp.zeros(shape, jnp.int32)
    for row in range(rows):
        reach = jnp.where(line == row, w_ref[row] * lon_dev, reach)
    scale = lax.rsqrt(3.0 * (2.0 * reach.astype(jnp.float32) + 1.0))
    for tile in range(3):
        offset = lane + (tile * LANES - SMAX * lon_dev)
        keep = jnp.where(jnp.abs(offset) <= reach, scale, 0.0)
        for k in range(kernels):
            for tap in range(taps):
                if tile < 2:
                    values = p_ref[k, tap, :, pl.ds(tile * LANES, LANES)]
                else:
                    values = p_ref[k, tap, :, pl.ds(cells - 1, 1)]
                    values = jnp.where(lane == 0, values, 0.0)
                f_ref[k, tap, :, pl.ds(tile * LANES, LANES)] = (
                    (values * keep).astype(BF16).astype(jnp.float32)
                )


def swap_chunks(tiles, chunk, lon_dev):
    count = len(tiles)
    turned = []
    for by in range(count):
        mixed = tiles[(count - 1 - by) % count]
        for b in range(count - 1):
            mixed = jnp.where(chunk == b, tiles[(b - by) % count], mixed)
        if by:
            mixed = pltpu.roll(mixed, LANES - lon_dev * by, 1)
        turned.append(mixed)
    result = []
    for b in range(count):
        mixed = turned[(b - count + 1) % count]
        for a in range(count - 1):
            mixed = jnp.where(chunk == a, turned[(b - a) % count], mixed)
        result.append(mixed)
    return result


def roll_rows(values, by):
    by %= values.shape[0]
    if by == 0:
        return values
    return jnp.concatenate([values[by:], values[:by]], axis=0)


def collect(bands, merged, filter_refs, f):
    if merged:
        band = lax.axis_index("lat")
        f[band] = filter_refs[0][...]
        f[1 - band] = filter_refs[1][...]
    else:
        for segment, ref in enumerate(filter_refs):
            f[segment] = ref[...]


def lay_toeplitz(rows, wide, lon_dev, merged, backward, f, t_ref, e_ref):
    segments, kernels, _, held, _ = f.shape
    shape = (lon_dev, LANES)
    lane, line = iota(shape, 1), iota(shape, 0)
    upper = lane >= line
    corner = lane == line
    for row in range(rows):
        for tap in range(3):
            source, column = (row + tap - 1, 2 - tap) if backward else (row, tap)
            source += 0 if merged else held
            segment, inner = divmod(source, held)
            present = 0 <= segment < segments
            for k in range(kernels):
                here = pl.ds(k * lon_dev, lon_dev)

                def turned(tile):
                    values = f[segment, k, column, pl.ds(inner, 1), pl.ds(tile * LANES, LANES)]
                    values = jnp.broadcast_to(values, shape)
                    return pltpu.roll(values, 0, 1, stride=1, stride_axis=0)

                if present:
                    first, second = turned(0), turned(1)
                    parts = [jnp.where(upper, first, 0.0), jnp.where(upper, second, first)]
                else:
                    parts = [jnp.zeros(shape, jnp.float32)] * 2
                for i, part in enumerate(parts):
                    t_ref[row, here, pl.ds((tap * 2 + i) * LANES, LANES)] = part.astype(BF16)
                if row in wide:
                    last = parts[0]
                    if present:
                        last = jnp.where(corner, turned(2), jnp.where(upper, 0.0, second))
                    at = pl.ds(tap * LANES, LANES)
                    e_ref[wide.index(row), here, at] = last.astype(BF16)


def mixers(everyone, share, w_ref, height):
    kernels, group, channels = w_ref.shape
    first = lax.axis_index(everyone[0])
    for axis in everyone[1:]:
        first = first * lax.axis_size(axis) + lax.axis_index(axis)
    shape = (channels, height)
    chosen = iota(shape, 0) == first * share + iota(shape, 1) % share
    weights = jnp.concatenate([w_ref[k].astype(jnp.float32) for k in range(kernels)], axis=0)
    weights = jnp.dot(
        weights.astype(BF16),
        jnp.where(chosen, 1.0, 0.0).astype(BF16),
        preferred_element_type=jnp.float32,
    )
    shape = (height, height)
    same = iota(shape, 0) // GROUP == iota(shape, 1) // GROUP
    result = []
    for k in range(kernels):
        spread = jnp.concatenate([weights[k * group : (k + 1) * group]] * (height // group), axis=0)
        result.append(jnp.where(same, spread, 0.0))
    return result


def prepare_forward(
    rows, wide, lon_dev, bands, merged, everyone, share, w_ref, x_ref, g_ref, *refs
):
    *filter_refs, t_ref, e_ref, m_ref, xt_ref, gt_ref, f = refs
    collect(bands, merged, filter_refs, f)
    lay_toeplitz(rows, wide, lon_dev, merged, False, f, t_ref, e_ref)
    height = m_ref.shape[0]
    for k, mixer in enumerate(mixers(everyone, share, w_ref, height)):
        m_ref[:, pl.ds(k * height, height)] = mixer.T.astype(BF16)
    xt_ref[...] = turned_by_identity(x_ref[...])
    gt_ref[...] = turned_by_identity(g_ref[...])


def prepare_backward(rows, wide, lon_dev, bands, merged, everyone, share, w_ref, *refs):
    *filter_refs, t_ref, e_ref, m_ref, f, r = refs
    collect(bands, merged, filter_refs, f)
    segments, kernels, taps, held, cells = f.shape
    last = 2 * SMAX * lon_dev
    shape = (cells, cells)
    mirror = jnp.where(iota(shape, 0) + iota(shape, 1) == last, 1.0, 0.0).astype(BF16)
    for segment in range(segments):
        values = f[segment].reshape(kernels * taps * held, cells).astype(BF16)
        values = jnp.dot(values, mirror, preferred_element_type=jnp.float32)
        r[segment] = values.reshape(kernels, taps, held, cells)
    lay_toeplitz(rows, wide, lon_dev, merged, True, r, t_ref, e_ref)
    height = m_ref.shape[0]
    for k, mixer in enumerate(mixers(everyone, share, w_ref, height)):
        m_ref[:, pl.ds(k * height, height)] = mixer.astype(BF16)


def conv_kernel(wide, bands, lon_dev, share, own_ref, t_ref, e_ref, m_ref, *refs):
    *halo_refs, o_ref, xc = refs
    per_tile = LANES // lon_dev
    segments, height, cells = own_ref.shape
    held = cells // lon_dev
    rows = segments * held
    span = 2 * LANES
    chunk = iota((height, LANES), 1) // lon_dev

    def unfold(tile, first, inners):
        tile = tile.astype(jnp.float32)
        turned = [tile] + [pltpu.roll(tile, lon_dev * by, 1) for by in range(1, per_tile)]
        for inner in inners:
            gathered = None
            for q in range(per_tile):
                piece = roll_rows(turned[(q - inner) % per_tile], share * (q - SMAX))
                gathered = piece if q == 0 else jnp.where(chunk == q, piece, gathered)
            gathered = gathered.astype(BF16)
            at = (first + inner + 1) * span
            xc[:, pl.ds(at, LANES)] = gathered
            xc[:, pl.ds(at + LANES, LANES)] = roll_rows(gathered, share * per_tile)

    def place(first):
        segment, inner = divmod(first, held)
        return segment, pl.ds(inner * lon_dev, LANES)

    if halo_refs:
        band = lax.axis_index("lat")
        above = halo_refs[0][:, pl.ds(cells - LANES, LANES)].astype(jnp.float32)
        unfold(jnp.where(band > 0, above, 0.0), -per_tile, [per_tile - 1])
        below = halo_refs[1][:, pl.ds(0, LANES)].astype(jnp.float32)
        unfold(jnp.where(band < bands - 1, below, 0.0), rows, [0])
    else:
        for edge in (0, rows + 1):
            xc[:, pl.ds(edge * span, span)] = jnp.zeros((height, span), BF16)
    for first in range(0, rows, per_tile):
        segment, at = place(first)
        unfold(own_ref[segment, :, at], first, range(per_tile))
    for first in range(0, rows, per_tile):
        parts = []
        for row in range(first, first + per_tile):
            part = lax.dot_general(
                xc[:, pl.ds(row * span, 3 * span)],
                t_ref[row],
                ALONG,
                preferred_element_type=jnp.float32,
            )
            if row in wide:
                beyond = [
                    roll_rows(xc[:, pl.ds((row + tap) * span, LANES)], 2 * share * per_tile)
                    for tap in range(3)
                ]
                part = part + lax.dot_general(
                    jnp.concatenate(beyond, axis=1),
                    e_ref[wide.index(row)],
                    ALONG,
                    preferred_element_type=jnp.float32,
                )
            parts.append(part)
        stacked = jnp.concatenate(
            [part.astype(BF16) for part in swap_chunks(parts, chunk, lon_dev)], axis=0
        )
        mixed = jnp.dot(m_ref[...], stacked, preferred_element_type=jnp.float32)
        segment, at = place(first)
        o_ref[segment, :, at] = mixed.astype(o_ref.dtype)


def dense_kernel(m_ref, wt_ref, w_ref, g_ref, o_ref, d_ref):
    pre = jnp.dot(wt_ref[...], m_ref[...], preferred_element_type=jnp.float32)
    slope = 0.7978845608028654
    square = pre * pre
    bent = jnp.tanh(slope * (pre + 0.044715 * (square * pre)))
    half = 0.5 * (1.0 + bent)
    o_ref[...] = (pre * half).astype(o_ref.dtype)
    rise = half + 0.5 * pre * (1.0 - bent * bent) * (slope * (1.0 + 3.0 * 0.044715 * square))
    grad_pre = (g_ref[...].astype(jnp.float32) * rise).astype(BF16)
    d_ref[...] = jnp.dot(w_ref[...], grad_pre, preferred_element_type=jnp.float32).astype(BF16)


def from_bands(values):
    count = lax.axis_size("lat")
    up = [(i, i + 1) for i in range(count - 1)]
    down = [(j, i) for i, j in up]
    return [lax.ppermute(values, "lat", up), lax.ppermute(values, "lat", down)]


def body(inputs, psi_raw, widths, w_group, w_mix, grad_out):
    row_count, lon_dev, channels = inputs.shape
    kernels = psi_raw.shape[0]
    blocks, bands = lax.axis_size("lon"), lax.axis_size("lat")
    cells = row_count * lon_dev
    merged = bands == 2 and channels % (2 * GROUP * bands * blocks) == 0
    everyone = ("lat", "lon") if merged else ("lon",)
    segments = bands if merged else 1
    share = channels // (segments * blocks)
    height = blocks * share
    rows = segments * row_count
    wide = wide_rows(rows, bands, bands * row_count)
    params = pltpu.CompilerParams(vmem_limit_bytes=32 * 2**20)
    square = jax.ShapeDtypeStruct((channels, cells), BF16)

    def exchange(values):
        parted = values.reshape(segments * blocks, share, cells)
        return lax.all_to_all(parted, everyone, 0, 0)

    turned, own_filters = pl.pallas_call(
        partial(enter_kernel, lon_dev),
        out_shape=(
            square,
            jax.ShapeDtypeStruct((kernels, 3, row_count, 3 * LANES), jnp.float32),
        ),
        in_specs=[
            pl.BlockSpec(memory_space=pltpu.SMEM),
            pl.BlockSpec(memory_space=pltpu.VMEM),
            pl.BlockSpec(memory_space=pltpu.VMEM),
        ],
    )(widths, inputs.reshape(cells, channels), psi_raw.transpose(0, 2, 1, 3))
    columns = exchange(turned)
    if merged:
        filters = [own_filters, lax.ppermute(own_filters, "lat", [(0, 1), (1, 0)])]
    else:
        above, below = from_bands(own_filters)
        filters = [above, own_filters, below]
    pool = pltpu.VMEM((bands if merged else 3, *own_filters.shape), jnp.float32)

    def tables(some):
        return [
            jax.ShapeDtypeStruct((rows, kernels * lon_dev, 6 * LANES), BF16),
            jax.ShapeDtypeStruct((len(some), kernels * lon_dev, 3 * LANES), BF16),
            jax.ShapeDtypeStruct((height, kernels * height), BF16),
        ]

    ahead = (lon_dev, bands, merged, everyone, share)
    *ready, turned_mix, turned_grad = pl.pallas_call(
        partial(prepare_forward, rows, wide[0], *ahead),
        out_shape=(*tables(wide[0]), jax.ShapeDtypeStruct(w_mix.shape, BF16), square),
        scratch_shapes=[pool],
        compiler_params=params,
    )(w_group, w_mix, grad_out.reshape(cells, channels), *filters)

    def convolve(values, some, ready):
        values = values.reshape(segments, height, cells)
        halo = [] if merged else from_bands(values[0])
        return pl.pallas_call(
            partial(conv_kernel, some, bands, lon_dev, share),
            out_shape=jax.ShapeDtypeStruct(values.shape, BF16),
            scratch_shapes=[pltpu.VMEM((height, (rows + 2) * 2 * LANES), BF16)],
            compiler_params=params,
        )(values, *ready, *halo)

    mixed_in = convolve(columns, wide[0], ready)
    mixed_in, filters, w_group = lax.optimization_barrier((mixed_in, filters, w_group))
    mixed_in = exchange(mixed_in)
    ready = pl.pallas_call(
        partial(prepare_backward, rows, wide[1], *ahead),
        out_shape=tables(wide[1]),
        scratch_shapes=[pool, pool],
        compiler_params=params,
    )(w_group, *filters)
    turned_out, grad_mixed = pl.pallas_call(
        dense_kernel,
        out_shape=(square, square),
        compiler_params=params,
    )(mixed_in.reshape(channels, cells), turned_mix, w_mix, turned_grad)
    grad_in = convolve(exchange(grad_mixed), wide[1], ready)
    grad_in = transposed(exchange(grad_in).reshape(channels, cells))
    outputs = transposed(turned_out)
    return outputs.reshape(inputs.shape), grad_in.reshape(inputs.shape)


def solution(mesh):
    return jax.shard_map(
        body,
        mesh=mesh,
        in_specs=(
            P("lat", "lon", None),
            P(None, "lat", None, None),
            P("lat"),
            P(),
            P(),
            P("lat", "lon", None),
        ),
        out_specs=(P("lat", "lon", None), P("lat", "lon", None)),
        check_vma=False,
    )
```

```python
from functools import partial

import jax
import jax.numpy as jnp
from jax import lax
from jax.experimental import pallas as pl
from jax.experimental.pallas import tpu as pltpu
from jax.sharding import PartitionSpec as P

GROUP = 4
SMAX = 4


LANES = 128
BF16 = jnp.bfloat16
ALONG = (((1,), (1,)), ((), ()))
SMALL = pltpu.CompilerParams(vmem_limit_bytes=4 * 2**20)
LARGE = pltpu.CompilerParams(vmem_limit_bytes=12 * 2**20)


def width_bound(row, row_total):
    pole = min(row, row_total - 1 - row)
    return min(SMAX, max(1, 2 * SMAX // (pole + 1)) + 1)


def wide_rows(row_count, bands, total):
    widest = [width_bound(row, total) == SMAX for row in range(total)]
    near = [any(widest[max(0, row - 1) : row + 2]) for row in range(total)]
    return tuple(
        tuple(row for row in range(row_count) if any(table[row::row_count]))
        for table in (widest, near)
    )


def iota(shape, axis):
    return lax.broadcasted_iota(jnp.int32, shape, axis)


def turned_by_identity(values):
    count = values.shape[1]
    unit = jnp.where(iota((count, count), 0) == iota((count, count), 1), 1.0, 0.0).astype(BF16)
    return lax.dot_general(unit, values, ALONG, preferred_element_type=jnp.float32).astype(BF16)


def transpose_kernel(x_ref, o_ref):
    o_ref[...] = turned_by_identity(x_ref[...])


def transposed(values):
    return pl.pallas_call(
        transpose_kernel,
        out_shape=jax.ShapeDtypeStruct(values.shape[::-1], values.dtype),
        compiler_params=SMALL,
    )(values)


def enter_kernel(lon_dev, w_ref, x_ref, p_ref, o_ref, f_ref):
    o_ref[...] = turned_by_identity(x_ref[...])
    kernels, taps, rows, cells = p_ref.shape
    shape = (rows, LANES)
    line, lane = iota(shape, 0), iota(shape, 1)
    reach = jnp.zeros(shape, jnp.int32)
    for row in range(rows):
        reach = jnp.where(line == row, w_ref[row] * lon_dev, reach)
    scale = lax.rsqrt(3.0 * (2.0 * reach.astype(jnp.float32) + 1.0))
    for tile in range(3):
        offset = lane + (tile * LANES - SMAX * lon_dev)
        keep = jnp.where(jnp.abs(offset) <= reach, scale, 0.0)
        for k in range(kernels):
            for tap in range(taps):
                if tile < 2:
                    values = p_ref[k, tap, :, pl.ds(tile * LANES, LANES)]
                else:
                    values = p_ref[k, tap, :, pl.ds(cells - 1, 1)]
                    values = jnp.where(lane == 0, values, 0.0)
                f_ref[k, tap, :, pl.ds(tile * LANES, LANES)] = (
                    (values * keep).astype(BF16).astype(jnp.float32)
                )


def swap_chunks(tiles, chunk, lon_dev):
    count = len(tiles)
    turned = []
    for by in range(count):
        mixed = tiles[(count - 1 - by) % count]
        for b in range(count - 1):
            mixed = jnp.where(chunk == b, tiles[(b - by) % count], mixed)
        if by:
            mixed = pltpu.roll(mixed, LANES - lon_dev * by, 1)
        turned.append(mixed)
    result = []
    for b in range(count):
        mixed = turned[(b - count + 1) % count]
        for a in range(count - 1):
            mixed = jnp.where(chunk == a, turned[(b - a) % count], mixed)
        result.append(mixed)
    return result


def roll_rows(values, by):
    by %= values.shape[0]
    if by == 0:
        return values
    return jnp.concatenate([values[by:], values[:by]], axis=0)


def collect(bands, merged, filter_refs, f):
    if merged:
        band = lax.axis_index("lat")
        f[band] = filter_refs[0][...]
        f[1 - band] = filter_refs[1][...]
    else:
        for segment, ref in enumerate(filter_refs):
            f[segment] = ref[...]


def lay_toeplitz(rows, wide, lon_dev, merged, backward, f, t_ref, e_ref):
    segments, kernels, _, held, _ = f.shape
    shape = (lon_dev, LANES)
    lane, line = iota(shape, 1), iota(shape, 0)
    upper = lane >= line
    corner = lane == line
    for row in range(rows):
        for tap in range(3):
            source, column = (row + tap - 1, 2 - tap) if backward else (row, tap)
            source += 0 if merged else held
            segment, inner = divmod(source, held)
            present = 0 <= segment < segments
            for k in range(kernels):
                here = pl.ds(k * lon_dev, lon_dev)

                def turned(tile):
                    values = f[segment, k, column, pl.ds(inner, 1), pl.ds(tile * LANES, LANES)]
                    values = jnp.broadcast_to(values, shape)
                    return pltpu.roll(values, 0, 1, stride=1, stride_axis=0)

                if present:
                    first, second = turned(0), turned(1)
                    parts = [jnp.where(upper, first, 0.0), jnp.where(upper, second, first)]
                else:
                    parts = [jnp.zeros(shape, jnp.float32)] * 2
                for i, part in enumerate(parts):
                    t_ref[row, here, pl.ds((tap * 2 + i) * LANES, LANES)] = part.astype(BF16)
                if row in wide:
                    last = parts[0]
                    if present:
                        last = jnp.where(corner, turned(2), jnp.where(upper, 0.0, second))
                    at = pl.ds(tap * LANES, LANES)
                    e_ref[wide.index(row), here, at] = last.astype(BF16)


def mixers(everyone, share, w_ref, height):
    kernels, group, channels = w_ref.shape
    first = lax.axis_index(everyone[0])
    for axis in everyone[1:]:
        first = first * lax.axis_size(axis) + lax.axis_index(axis)
    shape = (channels, height)
    chosen = iota(shape, 0) == first * share + iota(shape, 1) % share
    weights = jnp.concatenate([w_ref[k].astype(jnp.float32) for k in range(kernels)], axis=0)
    weights = jnp.dot(
        weights.astype(BF16),
        jnp.where(chosen, 1.0, 0.0).astype(BF16),
        preferred_element_type=jnp.float32,
    )
    shape = (height, height)
    same = iota(shape, 0) // GROUP == iota(shape, 1) // GROUP
    result = []
    for k in range(kernels):
        spread = jnp.concatenate([weights[k * group : (k + 1) * group]] * (height // group), axis=0)
        result.append(jnp.where(same, spread, 0.0))
    return result


def prepare_forward(
    rows, wide, lon_dev, bands, merged, everyone, share, w_ref, x_ref, g_ref, *refs
):
    *filter_refs, t_ref, e_ref, m_ref, xt_ref, gt_ref, f = refs
    collect(bands, merged, filter_refs, f)
    lay_toeplitz(rows, wide, lon_dev, merged, False, f, t_ref, e_ref)
    height = m_ref.shape[0]
    for k, mixer in enumerate(mixers(everyone, share, w_ref, height)):
        m_ref[:, pl.ds(k * height, height)] = mixer.T.astype(BF16)
    xt_ref[...] = turned_by_identity(x_ref[...])
    gt_ref[...] = turned_by_identity(g_ref[...])


def prepare_backward(rows, wide, lon_dev, bands, merged, everyone, share, w_ref, *refs):
    *filter_refs, t_ref, e_ref, m_ref, f, r = refs
    collect(bands, merged, filter_refs, f)
    segments, kernels, taps, held, cells = f.shape
    last = 2 * SMAX * lon_dev
    shape = (cells, cells)
    mirror = jnp.where(iota(shape, 0) + iota(shape, 1) == last, 1.0, 0.0).astype(BF16)
    for segment in range(segments):
        values = f[segment].reshape(kernels * taps * held, cells).astype(BF16)
        values = jnp.dot(values, mirror, preferred_element_type=jnp.float32)
        r[segment] = values.reshape(kernels, taps, held, cells)
    lay_toeplitz(rows, wide, lon_dev, merged, True, r, t_ref, e_ref)
    height = m_ref.shape[0]
    for k, mixer in enumerate(mixers(everyone, share, w_ref, height)):
        m_ref[:, pl.ds(k * height, height)] = mixer.astype(BF16)


def conv_kernel(wide, bands, lon_dev, share, own_ref, t_ref, e_ref, m_ref, *refs):
    *halo_refs, o_ref, xc = refs
    per_tile = LANES // lon_dev
    segments, height, cells = own_ref.shape
    held = cells // lon_dev
    rows = segments * held
    span = 2 * LANES
    chunk = iota((height, LANES), 1) // lon_dev

    def unfold(tile, first, inners):
        tile = tile.astype(jnp.float32)
        turned = [tile] + [pltpu.roll(tile, lon_dev * by, 1) for by in range(1, per_tile)]
        for inner in inners:
            gathered = None
            for q in range(per_tile):
                piece = roll_rows(turned[(q - inner) % per_tile], share * (q - SMAX))
                gathered = piece if q == 0 else jnp.where(chunk == q, piece, gathered)
            gathered = gathered.astype(BF16)
            at = (first + inner + 1) * span
            xc[:, pl.ds(at, LANES)] = gathered
            xc[:, pl.ds(at + LANES, LANES)] = roll_rows(gathered, share * per_tile)

    def place(first):
        segment, inner = divmod(first, held)
        return segment, pl.ds(inner * lon_dev, LANES)

    if halo_refs:
        band = lax.axis_index("lat")
        above = halo_refs[0][:, pl.ds(cells - LANES, LANES)].astype(jnp.float32)
        unfold(jnp.where(band > 0, above, 0.0), -per_tile, [per_tile - 1])
        below = halo_refs[1][:, pl.ds(0, LANES)].astype(jnp.float32)
        unfold(jnp.where(band < bands - 1, below, 0.0), rows, [0])
    else:
        for edge in (0, rows + 1):
            xc[:, pl.ds(edge * span, span)] = jnp.zeros((height, span), BF16)
    for first in range(0, rows, per_tile):
        segment, at = place(first)
        unfold(own_ref[segment, :, at], first, range(per_tile))
    for first in range(0, rows, per_tile):
        parts = []
        for row in range(first, first + per_tile):
            part = lax.dot_general(
                xc[:, pl.ds(row * span, 3 * span)],
                t_ref[row],
                ALONG,
                preferred_element_type=jnp.float32,
            )
            if row in wide:
                beyond = [
                    roll_rows(xc[:, pl.ds((row + tap) * span, LANES)], 2 * share * per_tile)
                    for tap in range(3)
                ]
                part = part + lax.dot_general(
                    jnp.concatenate(beyond, axis=1),
                    e_ref[wide.index(row)],
                    ALONG,
                    preferred_element_type=jnp.float32,
                )
            parts.append(part)
        stacked = jnp.concatenate(
            [part.astype(BF16) for part in swap_chunks(parts, chunk, lon_dev)], axis=0
        )
        mixed = jnp.dot(m_ref[...], stacked, preferred_element_type=jnp.float32)
        segment, at = place(first)
        o_ref[segment, :, at] = mixed.astype(o_ref.dtype)


def dense_kernel(m_ref, wt_ref, w_ref, g_ref, o_ref, d_ref):
    pre = jnp.dot(wt_ref[...], m_ref[...], preferred_element_type=jnp.float32)
    slope = 0.7978845608028654
    square = pre * pre
    bent = jnp.tanh(slope * (pre + 0.044715 * (square * pre)))
    half = 0.5 * (1.0 + bent)
    o_ref[...] = (pre * half).astype(o_ref.dtype)
    rise = half + 0.5 * pre * (1.0 - bent * bent) * (slope * (1.0 + 3.0 * 0.044715 * square))
    grad_pre = (g_ref[...].astype(jnp.float32) * rise).astype(BF16)
    d_ref[...] = jnp.dot(w_ref[...], grad_pre, preferred_element_type=jnp.float32).astype(BF16)


def from_bands(values):
    count = lax.axis_size("lat")
    up = [(i, i + 1) for i in range(count - 1)]
    down = [(j, i) for i, j in up]
    return [lax.ppermute(values, "lat", up), lax.ppermute(values, "lat", down)]


def body(inputs, psi_raw, widths, w_group, w_mix, grad_out):
    row_count, lon_dev, channels = inputs.shape
    kernels = psi_raw.shape[0]
    blocks, bands = lax.axis_size("lon"), lax.axis_size("lat")
    cells = row_count * lon_dev
    merged = bands == 2 and channels % (2 * GROUP * bands * blocks) == 0
    everyone = ("lat", "lon") if merged else ("lon",)
    segments = bands if merged else 1
    share = channels // (segments * blocks)
    height = blocks * share
    rows = segments * row_count
    wide = wide_rows(rows, bands, bands * row_count)
    square = jax.ShapeDtypeStruct((channels, cells), BF16)

    def exchange(values):
        parted = values.reshape(segments * blocks, share, cells)
        return lax.all_to_all(parted, everyone, 0, 0)

    turned, own_filters = pl.pallas_call(
        partial(enter_kernel, lon_dev),
        out_shape=(
            square,
            jax.ShapeDtypeStruct((kernels, 3, row_count, 3 * LANES), jnp.float32),
        ),
        in_specs=[
            pl.BlockSpec(memory_space=pltpu.SMEM),
            pl.BlockSpec(memory_space=pltpu.VMEM),
            pl.BlockSpec(memory_space=pltpu.VMEM),
        ],
        compiler_params=SMALL,
    )(widths, inputs.reshape(cells, channels), psi_raw.transpose(0, 2, 1, 3))
    columns = exchange(turned)
    if merged:
        filters = [own_filters, lax.ppermute(own_filters, "lat", [(0, 1), (1, 0)])]
    else:
        above, below = from_bands(own_filters)
        filters = [above, own_filters, below]
    pool = pltpu.VMEM((bands if merged else 3, *own_filters.shape), jnp.float32)

    def tables(some):
        return [
            jax.ShapeDtypeStruct((rows, kernels * lon_dev, 6 * LANES), BF16),
            jax.ShapeDtypeStruct((len(some), kernels * lon_dev, 3 * LANES), BF16),
            jax.ShapeDtypeStruct((height, kernels * height), BF16),
        ]

    ahead = (lon_dev, bands, merged, everyone, share)
    *ready, turned_mix, turned_grad = pl.pallas_call(
        partial(prepare_forward, rows, wide[0], *ahead),
        out_shape=(*tables(wide[0]), jax.ShapeDtypeStruct(w_mix.shape, BF16), square),
        scratch_shapes=[pool],
        compiler_params=LARGE,
    )(w_group, w_mix, grad_out.reshape(cells, channels), *filters)

    def convolve(values, some, ready):
        values = values.reshape(segments, height, cells)
        halo = [] if merged else from_bands(values[0])
        return pl.pallas_call(
            partial(conv_kernel, some, bands, lon_dev, share),
            out_shape=jax.ShapeDtypeStruct(values.shape, BF16),
            scratch_shapes=[pltpu.VMEM((height, (rows + 2) * 2 * LANES), BF16)],
            compiler_params=LARGE,
        )(values, *ready, *halo)

    mixed_in = convolve(columns, wide[0], ready)
    mixed_in, filters, w_group = lax.optimization_barrier((mixed_in, filters, w_group))
    mixed_in = exchange(mixed_in)
    ready = pl.pallas_call(
        partial(prepare_backward, rows, wide[1], *ahead),
        out_shape=tables(wide[1]),
        scratch_shapes=[pool, pool],
        compiler_params=LARGE,
    )(w_group, *filters)
    turned_out, grad_mixed = pl.pallas_call(
        dense_kernel,
        out_shape=(square, square),
        compiler_params=SMALL,
    )(mixed_in.reshape(channels, cells), turned_mix, w_mix, turned_grad)
    grad_in = convolve(exchange(grad_mixed), wide[1], ready)
    grad_in = transposed(exchange(grad_in).reshape(channels, cells))
    outputs = transposed(turned_out)
    return outputs.reshape(inputs.shape), grad_in.reshape(inputs.shape)


def solution(mesh):
    return jax.shard_map(
        body,
        mesh=mesh,
        in_specs=(
            P("lat", "lon", None),
            P(None, "lat", None, None),
            P("lat"),
            P(),
            P(),
            P("lat", "lon", None),
        ),
        out_specs=(P("lat", "lon", None), P("lat", "lon", None)),
        check_vma=False,
    )
```

```python
from functools import partial

import jax
import jax.numpy as jnp
from jax import lax
from jax.experimental import pallas as pl
from jax.experimental.pallas import tpu as pltpu
from jax.sharding import PartitionSpec as P

GROUP = 4
SMAX = 4


LANES = 128
BF16 = jnp.bfloat16
ALONG = (((1,), (1,)), ((), ()))
SMALL = pltpu.CompilerParams(vmem_limit_bytes=4 * 2**20)
LARGE = pltpu.CompilerParams(vmem_limit_bytes=12 * 2**20)


def width_bound(row, row_total):
    pole = min(row, row_total - 1 - row)
    return min(SMAX, max(1, 2 * SMAX // (pole + 1)) + 1)


def wide_rows(row_count, bands, total):
    widest = [width_bound(row, total) == SMAX for row in range(total)]
    near = [any(widest[max(0, row - 1) : row + 2]) for row in range(total)]
    return tuple(
        tuple(row for row in range(row_count) if any(table[row::row_count]))
        for table in (widest, near)
    )


def iota(shape, axis):
    return lax.broadcasted_iota(jnp.int32, shape, axis)


def turned_by_identity(values):
    count = values.shape[1]
    unit = jnp.where(iota((count, count), 0) == iota((count, count), 1), 1.0, 0.0).astype(BF16)
    return lax.dot_general(unit, values, ALONG, preferred_element_type=jnp.float32).astype(BF16)


def transpose_kernel(x_ref, o_ref):
    o_ref[...] = turned_by_identity(x_ref[...])


def transposed(values):
    return pl.pallas_call(
        transpose_kernel,
        out_shape=jax.ShapeDtypeStruct(values.shape[::-1], values.dtype),
        compiler_params=SMALL,
    )(values)


def enter_kernel(lon_dev, w_ref, x_ref, p_ref, o_ref, f_ref):
    o_ref[...] = turned_by_identity(x_ref[...])
    kernels, taps, rows, cells = p_ref.shape
    shape = (rows, LANES)
    line, lane = iota(shape, 0), iota(shape, 1)
    reach = jnp.zeros(shape, jnp.int32)
    for row in range(rows):
        reach = jnp.where(line == row, w_ref[row] * lon_dev, reach)
    scale = lax.rsqrt(3.0 * (2.0 * reach.astype(jnp.float32) + 1.0))
    for tile in range(3):
        offset = lane + (tile * LANES - SMAX * lon_dev)
        keep = jnp.where(jnp.abs(offset) <= reach, scale, 0.0)
        for k in range(kernels):
            for tap in range(taps):
                if tile < 2:
                    values = p_ref[k, tap, :, pl.ds(tile * LANES, LANES)]
                else:
                    values = p_ref[k, tap, :, pl.ds(cells - 1, 1)]
                    values = jnp.where(lane == 0, values, 0.0)
                f_ref[k, tap, :, pl.ds(tile * LANES, LANES)] = (
                    (values * keep).astype(BF16).astype(jnp.float32)
                )


def swap_chunks(tiles, chunk, lon_dev):
    count = len(tiles)
    turned = []
    for by in range(count):
        mixed = tiles[(count - 1 - by) % count]
        for b in range(count - 1):
            mixed = jnp.where(chunk == b, tiles[(b - by) % count], mixed)
        if by:
            mixed = pltpu.roll(mixed, LANES - lon_dev * by, 1)
        turned.append(mixed)
    result = []
    for b in range(count):
        mixed = turned[(b - count + 1) % count]
        for a in range(count - 1):
            mixed = jnp.where(chunk == a, turned[(b - a) % count], mixed)
        result.append(mixed)
    return result


def roll_rows(values, by):
    by %= values.shape[0]
    if by == 0:
        return values
    return jnp.concatenate([values[by:], values[:by]], axis=0)


def collect(bands, merged, filter_refs, f):
    if merged:
        band = lax.axis_index("lat")
        f[band] = filter_refs[0][...]
        f[1 - band] = filter_refs[1][...]
    else:
        for segment, ref in enumerate(filter_refs):
            f[segment] = ref[...]


def lay_toeplitz(rows, wide, lon_dev, merged, backward, f, t_ref, e_ref):
    segments, kernels, _, held, _ = f.shape
    shape = (lon_dev, LANES)
    lane, line = iota(shape, 1), iota(shape, 0)
    upper = lane >= line
    corner = lane == line
    for row in range(rows):
        for tap in range(3):
            source, column = (row + tap - 1, 2 - tap) if backward else (row, tap)
            source += 0 if merged else held
            segment, inner = divmod(source, held)
            present = 0 <= segment < segments
            for k in range(kernels):
                here = pl.ds(k * lon_dev, lon_dev)

                def turned(tile):
                    values = f[segment, k, column, pl.ds(inner, 1), pl.ds(tile * LANES, LANES)]
                    values = jnp.broadcast_to(values, shape)
                    return pltpu.roll(values, 0, 1, stride=1, stride_axis=0)

                if present:
                    first, second = turned(0), turned(1)
                    parts = [jnp.where(upper, first, 0.0), jnp.where(upper, second, first)]
                else:
                    parts = [jnp.zeros(shape, jnp.float32)] * 2
                for i, part in enumerate(parts):
                    t_ref[row, here, pl.ds((tap * 2 + i) * LANES, LANES)] = part.astype(BF16)
                if row in wide:
                    last = parts[0]
                    if present:
                        last = jnp.where(corner, turned(2), jnp.where(upper, 0.0, second))
                    at = pl.ds(tap * LANES, LANES)
                    e_ref[wide.index(row), here, at] = last.astype(BF16)


def mixers(everyone, share, w_ref, height):
    kernels, group, channels = w_ref.shape
    first = lax.axis_index(everyone[0])
    for axis in everyone[1:]:
        first = first * lax.axis_size(axis) + lax.axis_index(axis)
    shape = (channels, height)
    chosen = iota(shape, 0) == first * share + iota(shape, 1) % share
    weights = jnp.concatenate([w_ref[k].astype(jnp.float32) for k in range(kernels)], axis=0)
    weights = jnp.dot(
        weights.astype(BF16),
        jnp.where(chosen, 1.0, 0.0).astype(BF16),
        preferred_element_type=jnp.float32,
    )
    shape = (height, height)
    same = iota(shape, 0) // GROUP == iota(shape, 1) // GROUP
    result = []
    for k in range(kernels):
        spread = jnp.concatenate([weights[k * group : (k + 1) * group]] * (height // group), axis=0)
        result.append(jnp.where(same, spread, 0.0))
    return result


def conv_kernel(
    wide, bands, lon_dev, merged, everyone, share, backward, w_ref, own_ref, *refs
):
    count = 2 if merged else 3
    filter_refs, refs = refs[:count], refs[count:]
    *halo_refs, o_ref, xc, f, t_ref, e_ref = refs
    per_tile = LANES // lon_dev
    segments, height, cells = own_ref.shape
    held = cells // lon_dev
    rows = segments * held
    span = 2 * LANES
    chunk = iota((height, LANES), 1) // lon_dev
    collect(bands, merged, filter_refs, f)
    if backward:
        held_filters, kernels, taps, lines, width = f.shape
        shape = (width, width)
        mirror = iota(shape, 0) + iota(shape, 1) == 2 * SMAX * lon_dev
        mirror = jnp.where(mirror, 1.0, 0.0).astype(BF16)
        for segment in range(held_filters):
            values = f[segment].reshape(kernels * taps * lines, width).astype(BF16)
            values = jnp.dot(values, mirror, preferred_element_type=jnp.float32)
            f[segment] = values.reshape(kernels, taps, lines, width)
    lay_toeplitz(rows, wide, lon_dev, merged, backward, f, t_ref, e_ref)
    mixer = [
        (part if backward else part.T).astype(BF16)
        for part in mixers(everyone, share, w_ref, height)
    ]
    mixer = jnp.concatenate(mixer, axis=1)

    def unfold(tile, first, inners):
        tile = tile.astype(jnp.float32)
        turned = [tile] + [pltpu.roll(tile, lon_dev * by, 1) for by in range(1, per_tile)]
        for inner in inners:
            gathered = None
            for q in range(per_tile):
                piece = roll_rows(turned[(q - inner) % per_tile], share * (q - SMAX))
                gathered = piece if q == 0 else jnp.where(chunk == q, piece, gathered)
            gathered = gathered.astype(BF16)
            at = (first + inner + 1) * span
            xc[:, pl.ds(at, LANES)] = gathered
            xc[:, pl.ds(at + LANES, LANES)] = roll_rows(gathered, share * per_tile)

    def place(first):
        segment, inner = divmod(first, held)
        return segment, pl.ds(inner * lon_dev, LANES)

    if halo_refs:
        band = lax.axis_index("lat")
        above = halo_refs[0][:, pl.ds(cells - LANES, LANES)].astype(jnp.float32)
        unfold(jnp.where(band > 0, above, 0.0), -per_tile, [per_tile - 1])
        below = halo_refs[1][:, pl.ds(0, LANES)].astype(jnp.float32)
        unfold(jnp.where(band < bands - 1, below, 0.0), rows, [0])
    else:
        for edge in (0, rows + 1):
            xc[:, pl.ds(edge * span, span)] = jnp.zeros((height, span), BF16)
    for first in range(0, rows, per_tile):
        segment, at = place(first)
        unfold(own_ref[segment, :, at], first, range(per_tile))
    for first in range(0, rows, per_tile):
        parts = []
        for row in range(first, first + per_tile):
            part = lax.dot_general(
                xc[:, pl.ds(row * span, 3 * span)],
                t_ref[row],
                ALONG,
                preferred_element_type=jnp.float32,
            )
            if row in wide:
                beyond = [
                    roll_rows(xc[:, pl.ds((row + tap) * span, LANES)], 2 * share * per_tile)
                    for tap in range(3)
                ]
                part = part + lax.dot_general(
                    jnp.concatenate(beyond, axis=1),
                    e_ref[wide.index(row)],
                    ALONG,
                    preferred_element_type=jnp.float32,
                )
            parts.append(part)
        stacked = jnp.concatenate(
            [part.astype(BF16) for part in swap_chunks(parts, chunk, lon_dev)], axis=0
        )
        mixed = jnp.dot(mixer, stacked, preferred_element_type=jnp.float32)
        segment, at = place(first)
        o_ref[segment, :, at] = mixed.astype(o_ref.dtype)


def dense_kernel(m_ref, w_ref, g_ref, o_ref, d_ref):
    mixed_in = turned_by_identity(m_ref[...])
    pre = jnp.dot(mixed_in, w_ref[...], preferred_element_type=jnp.float32)
    slope = 0.7978845608028654
    square = pre * pre
    bent = jnp.tanh(slope * (pre + 0.044715 * (square * pre)))
    half = 0.5 * (1.0 + bent)
    o_ref[...] = (pre * half).astype(o_ref.dtype)
    rise = half + 0.5 * pre * (1.0 - bent * bent) * (slope * (1.0 + 3.0 * 0.044715 * square))
    grad_pre = (g_ref[...].astype(jnp.float32) * rise).astype(BF16)
    d_ref[...] = lax.dot_general(
        w_ref[...], grad_pre, ALONG, preferred_element_type=jnp.float32
    ).astype(d_ref.dtype)


def from_bands(values):
    count = lax.axis_size("lat")
    up = [(i, i + 1) for i in range(count - 1)]
    down = [(j, i) for i, j in up]
    return [lax.ppermute(values, "lat", up), lax.ppermute(values, "lat", down)]


def body(inputs, psi_raw, widths, w_group, w_mix, grad_out):
    row_count, lon_dev, channels = inputs.shape
    kernels = psi_raw.shape[0]
    blocks, bands = lax.axis_size("lon"), lax.axis_size("lat")
    cells = row_count * lon_dev
    merged = bands == 2 and channels % (2 * GROUP * bands * blocks) == 0
    everyone = ("lat", "lon") if merged else ("lon",)
    segments = bands if merged else 1
    share = channels // (segments * blocks)
    height = blocks * share
    rows = segments * row_count
    wide = wide_rows(rows, bands, bands * row_count)
    square = jax.ShapeDtypeStruct((channels, cells), BF16)

    def exchange(values):
        parted = values.reshape(segments * blocks, share, cells)
        return lax.all_to_all(parted, everyone, 0, 0)

    turned, own_filters = pl.pallas_call(
        partial(enter_kernel, lon_dev),
        out_shape=(
            square,
            jax.ShapeDtypeStruct((kernels, 3, row_count, 3 * LANES), jnp.float32),
        ),
        in_specs=[
            pl.BlockSpec(memory_space=pltpu.SMEM),
            pl.BlockSpec(memory_space=pltpu.VMEM),
            pl.BlockSpec(memory_space=pltpu.VMEM),
        ],
    )(widths, inputs.reshape(cells, channels), psi_raw.transpose(0, 2, 1, 3))
    columns = exchange(turned)
    if merged:
        filters = [own_filters, lax.ppermute(own_filters, "lat", [(0, 1), (1, 0)])]
    else:
        above, below = from_bands(own_filters)
        filters = [above, own_filters, below]
    pool = pltpu.VMEM((bands if merged else 3, *own_filters.shape), jnp.float32)

    def convolve(values, backward):
        values = values.reshape(segments, height, cells)
        halo = [] if merged else from_bands(values[0])
        some = wide[backward]
        return pl.pallas_call(
            partial(
                conv_kernel, some, bands, lon_dev, merged, everyone, share, bool(backward)
            ),
            out_shape=jax.ShapeDtypeStruct(values.shape, BF16),
            scratch_shapes=[
                pltpu.VMEM((height, (rows + 2) * 2 * LANES), BF16),
                pool,
                pltpu.VMEM((rows, kernels * lon_dev, 6 * LANES), BF16),
                pltpu.VMEM((len(some), kernels * lon_dev, 3 * LANES), BF16),
            ],
            compiler_params=LARGE,
        )(w_group, values, *filters, *halo)

    mixed_in = exchange(convolve(columns, 0))
    outputs, grad_mixed = pl.pallas_call(
        dense_kernel,
        out_shape=(jax.ShapeDtypeStruct((cells, channels), BF16), square),
        compiler_params=SMALL,
    )(mixed_in.reshape(channels, cells), w_mix, grad_out.reshape(cells, channels))
    grad_in = exchange(convolve(exchange(grad_mixed), 1))
    grad_in = transposed(grad_in.reshape(channels, cells))
    return outputs.reshape(inputs.shape), grad_in.reshape(inputs.shape)


def solution(mesh):
    return jax.shard_map(
        body,
        mesh=mesh,
        in_specs=(
            P("lat", "lon", None),
            P(None, "lat", None, None),
            P("lat"),
            P(),
            P(),
            P("lat", "lon", None),
        ),
        out_specs=(P("lat", "lon", None), P("lat", "lon", None)),
        check_vma=False,
    )
```

```python
from functools import partial

import jax
import jax.numpy as jnp
from jax import lax
from jax.experimental import pallas as pl
from jax.experimental.pallas import tpu as pltpu
from jax.sharding import PartitionSpec as P

GROUP = 4
SMAX = 4


LANES = 128
BF16 = jnp.bfloat16
ALONG = (((1,), (1,)), ((), ()))
SMALL = pltpu.CompilerParams(vmem_limit_bytes=4 * 2**20)
LARGE = pltpu.CompilerParams(vmem_limit_bytes=12 * 2**20)


def width_bound(row, row_total):
    pole = min(row, row_total - 1 - row)
    return min(SMAX, max(1, 2 * SMAX // (pole + 1)) + 1)


def reaches(row_count, bands):
    total = row_count * bands
    bound = [width_bound(row, total) for row in range(total)]
    near = [max(bound[max(0, row - 1) : row + 2]) for row in range(total)]
    return bound, near


def main_span(reach):
    return (-SMAX, 2) if reach > 2 else (-2, 1)


def iota(shape, axis):
    return lax.broadcasted_iota(jnp.int32, shape, axis)


def turned_by_identity(values):
    count = values.shape[1]
    unit = jnp.where(iota((count, count), 0) == iota((count, count), 1), 1.0, 0.0).astype(BF16)
    return lax.dot_general(unit, values, ALONG, preferred_element_type=jnp.float32).astype(BF16)


def transpose_kernel(x_ref, o_ref):
    o_ref[...] = turned_by_identity(x_ref[...])


def transposed(values):
    return pl.pallas_call(
        transpose_kernel,
        out_shape=jax.ShapeDtypeStruct(values.shape[::-1], values.dtype),
        compiler_params=SMALL,
    )(values)


def enter_kernel(lon_dev, w_ref, x_ref, p_ref, o_ref, f_ref):
    o_ref[...] = turned_by_identity(x_ref[...])
    kernels, taps, rows, cells = p_ref.shape
    shape = (rows, LANES)
    line, lane = iota(shape, 0), iota(shape, 1)
    reach = jnp.zeros(shape, jnp.int32)
    for row in range(rows):
        reach = jnp.where(line == row, w_ref[row] * lon_dev, reach)
    scale = lax.rsqrt(3.0 * (2.0 * reach.astype(jnp.float32) + 1.0))
    for tile in range(3):
        offset = lane + (tile * LANES - SMAX * lon_dev)
        keep = jnp.where(jnp.abs(offset) <= reach, scale, 0.0)
        for k in range(kernels):
            for tap in range(taps):
                if tile < 2:
                    values = p_ref[k, tap, :, pl.ds(tile * LANES, LANES)]
                else:
                    values = p_ref[k, tap, :, pl.ds(cells - 1, 1)]
                    values = jnp.where(lane == 0, values, 0.0)
                f_ref[k, tap, :, pl.ds(tile * LANES, LANES)] = (
                    (values * keep).astype(BF16).astype(jnp.float32)
                )


def collect(bands, merged, backward, filter_refs, f, s):
    if merged:
        band = lax.axis_index("lat")
        f[band] = filter_refs[0][...]
        f[1 - band] = filter_refs[1][...]
    else:
        for segment, ref in enumerate(filter_refs):
            f[segment] = ref[...]
    segments, kernels, taps, lines, width = f.shape
    if backward:
        shape = (width, width)
        mirror = jnp.where(iota(shape, 0) + iota(shape, 1) == 2 * LANES, 1.0, 0.0).astype(BF16)
        for segment in range(segments):
            values = f[segment].reshape(kernels * taps * lines, width).astype(BF16)
            values = jnp.dot(values, mirror, preferred_element_type=jnp.float32)
            f[segment] = values.reshape(kernels, taps, lines, width)
    low = iota((lines, LANES), 1) < LANES // 2
    for segment in range(segments):
        for k in range(kernels):
            for tap in range(taps):
                first, second = [
                    pltpu.roll(f[segment, k, tap, :, pl.ds(i * LANES, LANES)], LANES // 2, 1)
                    for i in range(2)
                ]
                s[segment, k, tap, :, pl.ds(0, LANES)] = jnp.where(low, first, second)
                s[segment, k, tap, :, pl.ds(LANES, LANES)] = second


def lay_toeplitz(table, lon_dev, merged, backward, f, s, t_ref, e_ref):
    segments, kernels, _, held, _ = f.shape
    shape = (lon_dev, LANES)
    lane, line = iota(shape, 1), iota(shape, 0)
    upper = lane >= line
    corner = lane == line
    for row, reach in enumerate(table):
        pool = f if reach > 2 else s
        _, count = main_span(reach)
        for k in range(kernels):
            here = pl.ds(k * lon_dev, lon_dev)
            tails = jnp.zeros(shape, jnp.float32)
            for tap in range(3):
                source, column = (row + tap - 1, 2 - tap) if backward else (row, tap)
                segment, inner = divmod(source + (0 if merged else held), held)
                present = 0 <= segment < segments

                def skewed(tile):
                    values = pool[segment, k, column, pl.ds(inner, 1), pl.ds(tile * LANES, LANES)]
                    values = jnp.broadcast_to(values, shape)
                    return pltpu.roll(values, 0, 1, stride=1, stride_axis=0)

                before = 0.0
                for tile in range(count):
                    part = jnp.zeros(shape, jnp.float32)
                    if present:
                        now = skewed(tile)
                        part = jnp.where(upper, now, before)
                        before = now
                    at = pl.ds((tap * count + tile) * LANES, LANES)
                    t_ref[row, here, at] = part.astype(BF16)
                if present and reach != 3:
                    last = jnp.where(corner, skewed(count), jnp.where(upper, 0.0, before))
                    tails += pltpu.roll(last, tap * lon_dev, 1) if tap else last
            if reach != 3:
                e_ref[row, here, :] = tails.astype(BF16)


def mixer_of(everyone, share, backward, w_ref, height):
    kernels, group, channels = w_ref.shape
    first = lax.axis_index(everyone[0])
    for axis in everyone[1:]:
        first = first * lax.axis_size(axis) + lax.axis_index(axis)
    shape = (channels, height)
    chosen = iota(shape, 0) == first * share + iota(shape, 1) % share
    weights = jnp.concatenate([w_ref[k].astype(jnp.float32) for k in range(kernels)], axis=0)
    weights = jnp.dot(
        weights.astype(BF16),
        jnp.where(chosen, 1.0, 0.0).astype(BF16),
        preferred_element_type=jnp.float32,
    )
    if backward:
        spread = [
            jnp.concatenate([weights[k * group : (k + 1) * group]] * (height // group), axis=0)
            for k in range(kernels)
        ]
        spread = jnp.concatenate(spread, axis=1)
    else:
        shape = (kernels * group, kernels * height)
        line, lane = iota(shape, 0), iota(shape, 1)
        pick = line == (lane // height) * group + lane % group
        spread = lax.dot_general(
            weights.astype(BF16),
            jnp.where(pick, 1.0, 0.0).astype(BF16),
            (((0,), (0,)), ((), ())),
            preferred_element_type=jnp.float32,
        )
    shape = (height, kernels * height)
    same = iota(shape, 0) // group == (iota(shape, 1) % height) // group
    return jnp.where(same, spread, 0.0).astype(BF16)


def conv_kernel(
    table, bands, lon_dev, merged, everyone, share, backward, w_ref, own_ref, *refs
):
    count = 2 if merged else 3
    filter_refs, refs = refs[:count], refs[count:]
    *halo_refs, o_ref, f, s, t_ref, e_ref, xs, z_ref = refs
    segments, height, cells = own_ref.shape
    rows = len(table)
    held = rows // segments
    kernels = f.shape[1]
    collect(bands, merged, backward, filter_refs, f, s)
    lay_toeplitz(table, lon_dev, merged, backward, f, s, t_ref, e_ref)

    def put(values, first):
        values = values.T.astype(jnp.float32)
        count = values.shape[0] // lon_dev
        for shard in range(-SMAX, SMAX + 1):
            turned = pltpu.roll(values, -shard * share % height, 1) if shard else values
            at = pl.ds((shard + SMAX) * lon_dev, lon_dev)
            xs[pl.ds(first + 1, count), at, :] = turned.astype(BF16).reshape(
                count, lon_dev, height
            )

    per_tile = LANES // lon_dev
    blank = jnp.zeros(xs.shape[1:], BF16)
    if halo_refs:
        band = lax.axis_index("lat")
        above = halo_refs[0][:, pl.ds(cells - LANES, LANES)]
        put(above, 0)
        edge = xs[per_tile].astype(jnp.float32)
        xs[0] = jnp.where(band > 0, edge, 0.0).astype(BF16)
        put(halo_refs[1][:, pl.ds(0, LANES)], 0)
        edge = xs[1].astype(jnp.float32)
        xs[rows + 1] = jnp.where(band < bands - 1, edge, 0.0).astype(BF16)
    else:
        xs[0] = blank
        xs[rows + 1] = blank
    for segment in range(segments):
        put(own_ref[segment], segment * held)
    for row, reach in enumerate(table):
        first, count = main_span(reach)
        start, width = (first + SMAX) * lon_dev, count * LANES
        window = xs[row : row + 3, start : start + width, :].reshape(3 * width, height)
        total = jnp.dot(
            t_ref[row, :, pl.ds(0, 3 * width)], window, preferred_element_type=jnp.float32
        )
        if reach != 3:
            window = xs[row : row + 3, start + width : start + width + lon_dev, :]
            window = window.reshape(3 * lon_dev, height)
            window = jnp.concatenate([window, blank[: LANES - 3 * lon_dev]], axis=0)
            total += jnp.dot(e_ref[row], window, preferred_element_type=jnp.float32)
        total = total.astype(BF16)
        for k in range(kernels):
            z_ref[pl.ds(row * lon_dev, lon_dev), pl.ds(k * height, height)] = total[
                k * lon_dev : (k + 1) * lon_dev
            ]
    mixer = mixer_of(everyone, share, backward, w_ref, height)
    for segment in range(segments):
        part = z_ref[pl.ds(segment * cells, cells), :]
        mixed = lax.dot_general(mixer, part, ALONG, preferred_element_type=jnp.float32)
        o_ref[segment] = mixed.astype(o_ref.dtype)


def dense_kernel(m_ref, w_ref, g_ref, o_ref, d_ref):
    mixed_in = turned_by_identity(m_ref[...])
    pre = jnp.dot(mixed_in, w_ref[...], preferred_element_type=jnp.float32)
    slope = 0.7978845608028654
    square = pre * pre
    bent = jnp.tanh(slope * (pre + 0.044715 * (square * pre)))
    half = 0.5 * (1.0 + bent)
    o_ref[...] = (pre * half).astype(o_ref.dtype)
    rise = half + 0.5 * pre * (1.0 - bent * bent) * (slope * (1.0 + 3.0 * 0.044715 * square))
    grad_pre = (g_ref[...].astype(jnp.float32) * rise).astype(BF16)
    d_ref[...] = lax.dot_general(
        w_ref[...], grad_pre, ALONG, preferred_element_type=jnp.float32
    ).astype(d_ref.dtype)


def from_bands(values):
    count = lax.axis_size("lat")
    up = [(i, i + 1) for i in range(count - 1)]
    down = [(j, i) for i, j in up]
    return [lax.ppermute(values, "lat", up), lax.ppermute(values, "lat", down)]


def body(inputs, psi_raw, widths, w_group, w_mix, grad_out):
    row_count, lon_dev, channels = inputs.shape
    kernels = psi_raw.shape[0]
    blocks, bands = lax.axis_size("lon"), lax.axis_size("lat")
    cells = row_count * lon_dev
    merged = bands == 2 and channels % (2 * GROUP * bands * blocks) == 0
    everyone = ("lat", "lon") if merged else ("lon",)
    segments = bands if merged else 1
    share = channels // (segments * blocks)
    height = blocks * share
    rows = segments * row_count
    tables = [
        tuple(max(table[row::rows]) for row in range(rows))
        for table in reaches(row_count, bands)
    ]
    square = jax.ShapeDtypeStruct((channels, cells), BF16)

    def exchange(values):
        parted = values.reshape(segments * blocks, share, cells)
        return lax.all_to_all(parted, everyone, 0, 0)

    turned, own_filters = pl.pallas_call(
        partial(enter_kernel, lon_dev),
        out_shape=(
            square,
            jax.ShapeDtypeStruct((kernels, 3, row_count, 3 * LANES), jnp.float32),
        ),
        in_specs=[
            pl.BlockSpec(memory_space=pltpu.SMEM),
            pl.BlockSpec(memory_space=pltpu.VMEM),
            pl.BlockSpec(memory_space=pltpu.VMEM),
        ],
    )(widths, inputs.reshape(cells, channels), psi_raw.transpose(0, 2, 1, 3))
    columns = exchange(turned)
    if merged:
        filters = [own_filters, lax.ppermute(own_filters, "lat", [(0, 1), (1, 0)])]
    else:
        above, below = from_bands(own_filters)
        filters = [above, own_filters, below]
    pool = (bands if merged else 3, *own_filters.shape)

    def convolve(values, backward):
        values = values.reshape(segments, height, cells)
        halo = [] if merged else from_bands(values[0])
        return pl.pallas_call(
            partial(
                conv_kernel, tables[backward], bands, lon_dev, merged, everyone, share,
                bool(backward),
            ),
            out_shape=jax.ShapeDtypeStruct(values.shape, BF16),
            scratch_shapes=[
                pltpu.VMEM(pool, jnp.float32),
                pltpu.VMEM((*pool[:-1], 2 * LANES), jnp.float32),
                pltpu.VMEM((rows, kernels * lon_dev, 6 * LANES), BF16),
                pltpu.VMEM((rows, kernels * lon_dev, LANES), BF16),
                pltpu.VMEM((rows + 2, (2 * SMAX + 1) * lon_dev, height), BF16),
                pltpu.VMEM((rows * lon_dev, kernels * height), BF16),
            ],
            compiler_params=LARGE,
        )(w_group, values, *filters, *halo)

    mixed_in = exchange(convolve(columns, 0))
    outputs, grad_mixed = pl.pallas_call(
        dense_kernel,
        out_shape=(jax.ShapeDtypeStruct((cells, channels), BF16), square),
        compiler_params=SMALL,
    )(mixed_in.reshape(channels, cells), w_mix, grad_out.reshape(cells, channels))
    grad_in = exchange(convolve(exchange(grad_mixed), 1))
    grad_in = transposed(grad_in.reshape(channels, cells))
    return outputs.reshape(inputs.shape), grad_in.reshape(inputs.shape)


def solution(mesh):
    return jax.shard_map(
        body,
        mesh=mesh,
        in_specs=(
            P("lat", "lon", None),
            P(None, "lat", None, None),
            P("lat"),
            P(),
            P(),
            P("lat", "lon", None),
        ),
        out_specs=(P("lat", "lon", None), P("lat", "lon", None)),
        check_vma=False,
    )
```

```python
from functools import partial

import jax
import jax.numpy as jnp
from jax import lax
from jax.experimental import pallas as pl
from jax.experimental.pallas import tpu as pltpu
from jax.sharding import PartitionSpec as P

GROUP = 4
SMAX = 4


LANES = 128
BF16 = jnp.bfloat16
ALONG = (((1,), (1,)), ((), ()))
SMALL = pltpu.CompilerParams(vmem_limit_bytes=4 * 2**20)
LARGE = pltpu.CompilerParams(vmem_limit_bytes=12 * 2**20)


def width_bound(row, row_total):
    pole = min(row, row_total - 1 - row)
    return min(SMAX, max(1, 2 * SMAX // (pole + 1)) + 1)


def reaches(row_count, bands):
    total = row_count * bands
    bound = [width_bound(row, total) for row in range(total)]
    near = [max(bound[max(0, row - 1) : row + 2]) for row in range(total)]
    return bound, near


def iota(shape, axis):
    return lax.broadcasted_iota(jnp.int32, shape, axis)


def turned_by_identity(values):
    count = values.shape[1]
    unit = jnp.where(iota((count, count), 0) == iota((count, count), 1), 1.0, 0.0).astype(BF16)
    return lax.dot_general(unit, values, ALONG, preferred_element_type=jnp.float32).astype(BF16)


def transpose_kernel(x_ref, o_ref):
    o_ref[...] = turned_by_identity(x_ref[...])


def transposed(values):
    return pl.pallas_call(
        transpose_kernel,
        out_shape=jax.ShapeDtypeStruct(values.shape[::-1], values.dtype),
        compiler_params=SMALL,
    )(values)


def enter_kernel(lon_dev, w_ref, x_ref, p_ref, o_ref, f_ref):
    o_ref[...] = turned_by_identity(x_ref[...])
    kernels, taps, rows, cells = p_ref.shape
    shape = (rows, LANES)
    line, lane = iota(shape, 0), iota(shape, 1)
    reach = jnp.zeros(shape, jnp.int32)
    for row in range(rows):
        reach = jnp.where(line == row, w_ref[row] * lon_dev, reach)
    scale = lax.rsqrt(3.0 * (2.0 * reach.astype(jnp.float32) + 1.0))
    for tile in range(3):
        offset = lane + (tile * LANES - SMAX * lon_dev)
        keep = jnp.where(jnp.abs(offset) <= reach, scale, 0.0)
        for k in range(kernels):
            for tap in range(taps):
                if tile < 2:
                    values = p_ref[k, tap, :, pl.ds(tile * LANES, LANES)]
                else:
                    values = p_ref[k, tap, :, pl.ds(cells - 1, 1)]
                    values = jnp.where(lane == 0, values, 0.0)
                f_ref[k, tap, :, pl.ds(tile * LANES, LANES)] = (
                    (values * keep).astype(BF16).astype(jnp.float32)
                )


def collect(bands, merged, backward, filter_refs, f):
    if merged:
        band = lax.axis_index("lat")
        f[band] = filter_refs[0][...]
        f[1 - band] = filter_refs[1][...]
    else:
        for segment, ref in enumerate(filter_refs):
            f[segment] = ref[...]
    if backward:
        segments, kernels, taps, lines, width = f.shape
        shape = (width, width)
        mirror = jnp.where(iota(shape, 0) + iota(shape, 1) == 2 * LANES, 1.0, 0.0).astype(BF16)
        for segment in range(segments):
            values = f[segment].reshape(kernels * taps * lines, width).astype(BF16)
            values = jnp.dot(values, mirror, preferred_element_type=jnp.float32)
            f[segment] = values.reshape(kernels, taps, lines, width)


def lay_toeplitz(rows, wide, lon_dev, merged, backward, f, t_ref, e_ref):
    segments, kernels, _, held, _ = f.shape
    shape = (lon_dev, LANES)
    lane, line = iota(shape, 1), iota(shape, 0)
    upper = lane >= line
    corner = lane == line
    for row in range(rows):
        for tap in range(3):
            source, column = (row + tap - 1, 2 - tap) if backward else (row, tap)
            source += 0 if merged else held
            segment, inner = divmod(source, held)
            present = 0 <= segment < segments
            for k in range(kernels):
                here = pl.ds(k * lon_dev, lon_dev)

                def turned(tile):
                    values = f[segment, k, column, pl.ds(inner, 1), pl.ds(tile * LANES, LANES)]
                    values = jnp.broadcast_to(values, shape)
                    return pltpu.roll(values, 0, 1, stride=1, stride_axis=0)

                if present:
                    first, second = turned(0), turned(1)
                    parts = [jnp.where(upper, first, 0.0), jnp.where(upper, second, first)]
                else:
                    parts = [jnp.zeros(shape, jnp.float32)] * 2
                for i, part in enumerate(parts):
                    t_ref[row, here, pl.ds((tap * 2 + i) * LANES, LANES)] = part.astype(BF16)
                if row in wide:
                    last = parts[0]
                    if present:
                        last = jnp.where(corner, turned(2), jnp.where(upper, 0.0, second))
                    at = pl.ds(tap * LANES, LANES)
                    e_ref[wide.index(row), here, at] = last.astype(BF16)


def mixer_of(everyone, share, backward, w_ref, height):
    kernels, group, channels = w_ref.shape
    first = lax.axis_index(everyone[0])
    for axis in everyone[1:]:
        first = first * lax.axis_size(axis) + lax.axis_index(axis)
    shape = (channels, height)
    chosen = iota(shape, 0) == first * share + iota(shape, 1) % share
    weights = jnp.concatenate([w_ref[k].astype(jnp.float32) for k in range(kernels)], axis=0)
    weights = jnp.dot(
        weights.astype(BF16),
        jnp.where(chosen, 1.0, 0.0).astype(BF16),
        preferred_element_type=jnp.float32,
    )
    if backward:
        spread = [
            jnp.concatenate([weights[k * group : (k + 1) * group]] * (height // group), axis=0)
            for k in range(kernels)
        ]
        spread = jnp.concatenate(spread, axis=1)
    else:
        shape = (kernels * group, kernels * height)
        line, lane = iota(shape, 0), iota(shape, 1)
        pick = line == (lane // height) * group + lane % group
        spread = lax.dot_general(
            weights.astype(BF16),
            jnp.where(pick, 1.0, 0.0).astype(BF16),
            (((0,), (0,)), ((), ())),
            preferred_element_type=jnp.float32,
        )
    shape = (height, kernels * height)
    same = iota(shape, 0) // group == (iota(shape, 1) % height) // group
    return jnp.where(same, spread, 0.0).astype(BF16)


def conv_kernel(
    table, bands, lon_dev, merged, everyone, share, backward, w_ref, own_ref, *refs
):
    count = 2 if merged else 3
    filter_refs, refs = refs[:count], refs[count:]
    *halo_refs, o_ref, f, t_ref, e_ref, xs, z_ref = refs
    segments, height, cells = own_ref.shape
    rows = len(table)
    held = rows // segments
    kernels = f.shape[1]
    wide = [row for row, reach in enumerate(table) if reach == SMAX]
    collect(bands, merged, backward, filter_refs, f)
    lay_toeplitz(rows, wide, lon_dev, merged, backward, f, t_ref, e_ref)

    def put(values, first):
        values = values.T.astype(jnp.float32)
        count = values.shape[0] // lon_dev
        for shard in range(-SMAX, SMAX + 1):
            turned = pltpu.roll(values, -shard * share % height, 1) if shard else values
            at = pl.ds((shard + SMAX) * lon_dev, lon_dev)
            xs[pl.ds(first + 1, count), at, :] = turned.astype(BF16).reshape(
                count, lon_dev, height
            )

    per_tile = LANES // lon_dev
    blank = jnp.zeros(xs.shape[1:], BF16)
    if halo_refs:
        band = lax.axis_index("lat")
        above = halo_refs[0][:, pl.ds(cells - LANES, LANES)]
        put(above, 0)
        edge = xs[per_tile].astype(jnp.float32)
        xs[0] = jnp.where(band > 0, edge, 0.0).astype(BF16)
        put(halo_refs[1][:, pl.ds(0, LANES)], 0)
        edge = xs[1].astype(jnp.float32)
        xs[rows + 1] = jnp.where(band < bands - 1, edge, 0.0).astype(BF16)
    else:
        xs[0] = blank
        xs[rows + 1] = blank
    for segment in range(segments):
        put(own_ref[segment], segment * held)
    span = 2 * LANES
    for row in range(rows):
        window = xs[row : row + 3, :span, :].reshape(3 * span, height)
        total = jnp.dot(t_ref[row], window, preferred_element_type=jnp.float32)
        if row in wide:
            beyond = []
            for tap in range(3):
                beyond += [xs[row + tap, span:, :], blank[: LANES - lon_dev]]
            total += jnp.dot(
                e_ref[wide.index(row)],
                jnp.concatenate(beyond, axis=0),
                preferred_element_type=jnp.float32,
            )
        total = total.astype(BF16)
        for k in range(kernels):
            z_ref[pl.ds(row * lon_dev, lon_dev), pl.ds(k * height, height)] = total[
                k * lon_dev : (k + 1) * lon_dev
            ]
    mixer = mixer_of(everyone, share, backward, w_ref, height)
    for segment in range(segments):
        part = z_ref[pl.ds(segment * cells, cells), :]
        mixed = lax.dot_general(mixer, part, ALONG, preferred_element_type=jnp.float32)
        o_ref[segment] = mixed.astype(o_ref.dtype)


def dense_kernel(m_ref, w_ref, g_ref, o_ref, d_ref):
    mixed_in = turned_by_identity(m_ref[...])
    pre = jnp.dot(mixed_in, w_ref[...], preferred_element_type=jnp.float32)
    slope = 0.7978845608028654
    square = pre * pre
    bent = jnp.tanh(slope * (pre + 0.044715 * (square * pre)))
    half = 0.5 * (1.0 + bent)
    o_ref[...] = (pre * half).astype(o_ref.dtype)
    rise = half + 0.5 * pre * (1.0 - bent * bent) * (slope * (1.0 + 3.0 * 0.044715 * square))
    grad_pre = (g_ref[...].astype(jnp.float32) * rise).astype(BF16)
    d_ref[...] = lax.dot_general(
        w_ref[...], grad_pre, ALONG, preferred_element_type=jnp.float32
    ).astype(d_ref.dtype)


def from_bands(values):
    count = lax.axis_size("lat")
    up = [(i, i + 1) for i in range(count - 1)]
    down = [(j, i) for i, j in up]
    return [lax.ppermute(values, "lat", up), lax.ppermute(values, "lat", down)]


def body(inputs, psi_raw, widths, w_group, w_mix, grad_out):
    row_count, lon_dev, channels = inputs.shape
    kernels = psi_raw.shape[0]
    blocks, bands = lax.axis_size("lon"), lax.axis_size("lat")
    cells = row_count * lon_dev
    merged = bands == 2 and channels % (2 * GROUP * bands * blocks) == 0
    everyone = ("lat", "lon") if merged else ("lon",)
    segments = bands if merged else 1
    share = channels // (segments * blocks)
    height = blocks * share
    rows = segments * row_count
    tables = [
        tuple(max(table[row::rows]) for row in range(rows))
        for table in reaches(row_count, bands)
    ]
    square = jax.ShapeDtypeStruct((channels, cells), BF16)

    def exchange(values):
        parted = values.reshape(segments * blocks, share, cells)
        return lax.all_to_all(parted, everyone, 0, 0)

    turned, own_filters = pl.pallas_call(
        partial(enter_kernel, lon_dev),
        out_shape=(
            square,
            jax.ShapeDtypeStruct((kernels, 3, row_count, 3 * LANES), jnp.float32),
        ),
        in_specs=[
            pl.BlockSpec(memory_space=pltpu.SMEM),
            pl.BlockSpec(memory_space=pltpu.VMEM),
            pl.BlockSpec(memory_space=pltpu.VMEM),
        ],
    )(widths, inputs.reshape(cells, channels), psi_raw.transpose(0, 2, 1, 3))
    columns = exchange(turned)
    if merged:
        filters = [own_filters, lax.ppermute(own_filters, "lat", [(0, 1), (1, 0)])]
    else:
        above, below = from_bands(own_filters)
        filters = [above, own_filters, below]
    pool = (bands if merged else 3, *own_filters.shape)

    def convolve(values, backward):
        values = values.reshape(segments, height, cells)
        halo = [] if merged else from_bands(values[0])
        return pl.pallas_call(
            partial(
                conv_kernel, tables[backward], bands, lon_dev, merged, everyone, share,
                bool(backward),
            ),
            out_shape=jax.ShapeDtypeStruct(values.shape, BF16),
            scratch_shapes=[
                pltpu.VMEM(pool, jnp.float32),
                pltpu.VMEM((rows, kernels * lon_dev, 6 * LANES), BF16),
                pltpu.VMEM((tables[backward].count(SMAX), kernels * lon_dev, 3 * LANES), BF16),
                pltpu.VMEM((rows + 2, (2 * SMAX + 1) * lon_dev, height), BF16),
                pltpu.VMEM((rows * lon_dev, kernels * height), BF16),
            ],
            compiler_params=LARGE,
        )(w_group, values, *filters, *halo)

    mixed_in = exchange(convolve(columns, 0))
    outputs, grad_mixed = pl.pallas_call(
        dense_kernel,
        out_shape=(jax.ShapeDtypeStruct((cells, channels), BF16), square),
        compiler_params=SMALL,
    )(mixed_in.reshape(channels, cells), w_mix, grad_out.reshape(cells, channels))
    grad_in = exchange(convolve(exchange(grad_mixed), 1))
    grad_in = transposed(grad_in.reshape(channels, cells))
    return outputs.reshape(inputs.shape), grad_in.reshape(inputs.shape)


def solution(mesh):
    return jax.shard_map(
        body,
        mesh=mesh,
        in_specs=(
            P("lat", "lon", None),
            P(None, "lat", None, None),
            P("lat"),
            P(),
            P(),
            P("lat", "lon", None),
        ),
        out_specs=(P("lat", "lon", None), P("lat", "lon", None)),
        check_vma=False,
    )
```

```python
from functools import partial

import jax
import jax.numpy as jnp
from jax import lax
from jax.experimental import pallas as pl
from jax.experimental.pallas import tpu as pltpu
from jax.sharding import PartitionSpec as P

GROUP = 4
SMAX = 4


LANES = 128
BF16 = jnp.bfloat16
ALONG = (((1,), (1,)), ((), ()))
SMALL = pltpu.CompilerParams(vmem_limit_bytes=8 * 2**20)


def width_bound(row, row_total):
    pole = min(row, row_total - 1 - row)
    return min(SMAX, max(1, 2 * SMAX // (pole + 1)) + 1)


def reaches(row_count, bands):
    total = row_count * bands
    bound = [width_bound(row, total) for row in range(total)]
    near = [max(bound[max(0, row - 1) : row + 2]) for row in range(total)]
    return bound, near


def iota(shape, axis):
    return lax.broadcasted_iota(jnp.int32, shape, axis)


def turned_by_identity(values):
    count = values.shape[1]
    unit = jnp.where(iota((count, count), 0) == iota((count, count), 1), 1.0, 0.0).astype(BF16)
    return lax.dot_general(unit, values, ALONG, preferred_element_type=jnp.float32).astype(BF16)


def transpose_kernel(x_ref, o_ref):
    o_ref[...] = turned_by_identity(x_ref[...])


def transposed(values):
    return pl.pallas_call(
        transpose_kernel,
        out_shape=jax.ShapeDtypeStruct(values.shape[::-1], values.dtype),
        compiler_params=SMALL,
    )(values)


def enter_kernel(lon_dev, w_ref, x_ref, p_ref, o_ref, f_ref):
    o_ref[...] = turned_by_identity(x_ref[...])
    kernels, taps, rows, cells = p_ref.shape
    shape = (rows, LANES)
    line, lane = iota(shape, 0), iota(shape, 1)
    reach = jnp.zeros(shape, jnp.int32)
    for row in range(rows):
        reach = jnp.where(line == row, w_ref[row] * lon_dev, reach)
    scale = lax.rsqrt(3.0 * (2.0 * reach.astype(jnp.float32) + 1.0))
    for tile in range(3):
        offset = lane + (tile * LANES - SMAX * lon_dev)
        keep = jnp.where(jnp.abs(offset) <= reach, scale, 0.0)
        for k in range(kernels):
            for tap in range(taps):
                if tile < 2:
                    values = p_ref[k, tap, :, pl.ds(tile * LANES, LANES)]
                else:
                    values = p_ref[k, tap, :, pl.ds(cells - 1, 1)]
                    values = jnp.where(lane == 0, values, 0.0)
                f_ref[k, tap, :, pl.ds(tile * LANES, LANES)] = (
                    (values * keep).astype(BF16).astype(jnp.float32)
                )


def collect(bands, merged, backward, filter_refs, f):
    if merged:
        band = lax.axis_index("lat")
        f[band] = filter_refs[0][...]
        f[1 - band] = filter_refs[1][...]
    else:
        for segment, ref in enumerate(filter_refs):
            f[segment] = ref[...]
    if backward:
        segments, kernels, taps, lines, width = f.shape
        shape = (width, width)
        mirror = jnp.where(iota(shape, 0) + iota(shape, 1) == 2 * LANES, 1.0, 0.0).astype(BF16)
        for segment in range(segments):
            values = f[segment].reshape(kernels * taps * lines, width).astype(BF16)
            values = jnp.dot(values, mirror, preferred_element_type=jnp.float32)
            f[segment] = values.reshape(kernels, taps, lines, width)


def extra_rows(wide):
    return (len(wide) + 1) // 2


def beyond_at(rows, wide, row):
    place = wide.index(row)
    return rows + place // 2, place % 2 * 3 * LANES


def lay_toeplitz(rows, wide, lon_dev, merged, backward, f, t_ref):
    segments, kernels, _, held, _ = f.shape
    shape = (lon_dev, LANES)
    lane, line = iota(shape, 1), iota(shape, 0)
    upper = lane >= line
    corner = lane == line
    for row in range(rows):
        for tap in range(3):
            source, column = (row + tap - 1, 2 - tap) if backward else (row, tap)
            source += 0 if merged else held
            segment, inner = divmod(source, held)
            present = 0 <= segment < segments
            for k in range(kernels):
                here = pl.ds(k * lon_dev, lon_dev)

                def turned(tile):
                    values = f[segment, k, column, pl.ds(inner, 1), pl.ds(tile * LANES, LANES)]
                    values = jnp.broadcast_to(values, shape)
                    return pltpu.roll(values, 0, 1, stride=1, stride_axis=0)

                if present:
                    first, second = turned(0), turned(1)
                    parts = [jnp.where(upper, first, 0.0), jnp.where(upper, second, first)]
                else:
                    parts = [jnp.zeros(shape, jnp.float32)] * 2
                for i, part in enumerate(parts):
                    t_ref[row, here, pl.ds((tap * 2 + i) * LANES, LANES)] = part.astype(BF16)
                if row in wide:
                    last = parts[0]
                    if present:
                        last = jnp.where(corner, turned(2), jnp.where(upper, 0.0, second))
                    after, at = beyond_at(rows, wide, row)
                    t_ref[after, here, pl.ds(at + tap * LANES, LANES)] = last.astype(BF16)


def mixer_of(everyone, share, backward, w_ref, height):
    kernels, group, channels = w_ref.shape
    first = lax.axis_index(everyone[0])
    for axis in everyone[1:]:
        first = first * lax.axis_size(axis) + lax.axis_index(axis)
    shape = (channels, height)
    chosen = iota(shape, 0) == first * share + iota(shape, 1) % share
    weights = jnp.concatenate([w_ref[k].astype(jnp.float32) for k in range(kernels)], axis=0)
    weights = jnp.dot(
        weights.astype(BF16),
        jnp.where(chosen, 1.0, 0.0).astype(BF16),
        preferred_element_type=jnp.float32,
    )
    if backward:
        spread = [
            jnp.concatenate([weights[k * group : (k + 1) * group]] * (height // group), axis=0)
            for k in range(kernels)
        ]
        spread = jnp.concatenate(spread, axis=1)
    else:
        shape = (kernels * group, kernels * height)
        line, lane = iota(shape, 0), iota(shape, 1)
        pick = line == (lane // height) * group + lane % group
        spread = lax.dot_general(
            weights.astype(BF16),
            jnp.where(pick, 1.0, 0.0).astype(BF16),
            (((0,), (0,)), ((), ())),
            preferred_element_type=jnp.float32,
        )
    shape = (height, kernels * height)
    same = iota(shape, 0) // group == (iota(shape, 1) % height) // group
    return jnp.where(same, spread, 0.0).astype(BF16)


def table_kernel(wide, rows, bands, lon_dev, merged, backward, *refs):
    *filter_refs, t_ref, f = refs
    collect(bands, merged, backward, filter_refs, f)
    lay_toeplitz(rows, wide, lon_dev, merged, backward, f, t_ref)


def conv_kernel(wide, rows, bands, lon_dev, everyone, share, backward, *refs):
    w_ref, own_ref, t_ref, *halo_refs, o_ref, xs, z_ref = refs
    segments, height, cells = own_ref.shape
    held = rows // segments
    kernels = w_ref.shape[0]

    def put(values, first):
        values = values.T.astype(jnp.float32)
        count = values.shape[0] // lon_dev
        for shard in range(-SMAX, SMAX + 1):
            turned = pltpu.roll(values, -shard * share % height, 1) if shard else values
            at = pl.ds((shard + SMAX) * lon_dev, lon_dev)
            xs[pl.ds(first + 1, count), at, :] = turned.astype(BF16).reshape(
                count, lon_dev, height
            )

    per_tile = LANES // lon_dev
    blank = jnp.zeros(xs.shape[1:], BF16)
    if halo_refs:
        band = lax.axis_index("lat")
        above = halo_refs[0][:, pl.ds(cells - LANES, LANES)]
        put(above, 0)
        edge = xs[per_tile].astype(jnp.float32)
        xs[0] = jnp.where(band > 0, edge, 0.0).astype(BF16)
        put(halo_refs[1][:, pl.ds(0, LANES)], 0)
        edge = xs[1].astype(jnp.float32)
        xs[rows + 1] = jnp.where(band < bands - 1, edge, 0.0).astype(BF16)
    else:
        xs[0] = blank
        xs[rows + 1] = blank
    for segment in range(segments):
        put(own_ref[segment], segment * held)
    span = 2 * LANES
    for row in range(rows):
        window = xs[row : row + 3, :span, :].reshape(3 * span, height)
        total = jnp.dot(t_ref[row], window, preferred_element_type=jnp.float32)
        if row in wide:
            beyond = []
            for tap in range(3):
                beyond += [xs[row + tap, span:, :], blank[: LANES - lon_dev]]
            after, at = beyond_at(rows, wide, row)
            total += jnp.dot(
                t_ref[after, :, pl.ds(at, 3 * LANES)],
                jnp.concatenate(beyond, axis=0),
                preferred_element_type=jnp.float32,
            )
        total = total.astype(BF16)
        for k in range(kernels):
            z_ref[pl.ds(row * lon_dev, lon_dev), pl.ds(k * height, height)] = total[
                k * lon_dev : (k + 1) * lon_dev
            ]
    mixer = mixer_of(everyone, share, backward, w_ref, height)
    for segment in range(segments):
        part = z_ref[pl.ds(segment * cells, cells), :]
        mixed = lax.dot_general(mixer, part, ALONG, preferred_element_type=jnp.float32)
        o_ref[segment] = mixed.astype(o_ref.dtype)


def dense_kernel(m_ref, w_ref, g_ref, o_ref, d_ref):
    mixed_in = turned_by_identity(m_ref[...])
    pre = jnp.dot(mixed_in, w_ref[...], preferred_element_type=jnp.float32)
    slope = 0.7978845608028654
    square = pre * pre
    bent = jnp.tanh(slope * (pre + 0.044715 * (square * pre)))
    half = 0.5 * (1.0 + bent)
    o_ref[...] = (pre * half).astype(o_ref.dtype)
    rise = half + 0.5 * pre * (1.0 - bent * bent) * (slope * (1.0 + 3.0 * 0.044715 * square))
    grad_pre = (g_ref[...].astype(jnp.float32) * rise).astype(BF16)
    d_ref[...] = lax.dot_general(
        w_ref[...], grad_pre, ALONG, preferred_element_type=jnp.float32
    ).astype(d_ref.dtype)


def from_bands(values):
    count = lax.axis_size("lat")
    up = [(i, i + 1) for i in range(count - 1)]
    down = [(j, i) for i, j in up]
    return [lax.ppermute(values, "lat", up), lax.ppermute(values, "lat", down)]


def body(inputs, psi_raw, widths, w_group, w_mix, grad_out):
    row_count, lon_dev, channels = inputs.shape
    kernels = psi_raw.shape[0]
    blocks, bands = lax.axis_size("lon"), lax.axis_size("lat")
    cells = row_count * lon_dev
    merged = bands == 2 and channels % (2 * GROUP * bands * blocks) == 0
    everyone = ("lat", "lon") if merged else ("lon",)
    segments = bands if merged else 1
    share = channels // (segments * blocks)
    height = blocks * share
    rows = segments * row_count
    wide = [
        tuple(row for row in range(rows) if max(table[row::rows]) == SMAX)
        for table in reaches(row_count, bands)
    ]
    square = jax.ShapeDtypeStruct((channels, cells), BF16)

    def exchange(values):
        parted = values.reshape(segments * blocks, share, cells)
        return lax.all_to_all(parted, everyone, 0, 0)

    turned, own_filters = pl.pallas_call(
        partial(enter_kernel, lon_dev),
        out_shape=(
            square,
            jax.ShapeDtypeStruct((kernels, 3, row_count, 3 * LANES), jnp.float32),
        ),
        in_specs=[
            pl.BlockSpec(memory_space=pltpu.SMEM),
            pl.BlockSpec(memory_space=pltpu.VMEM),
            pl.BlockSpec(memory_space=pltpu.VMEM),
        ],
    )(widths, inputs.reshape(cells, channels), psi_raw.transpose(0, 2, 1, 3))
    columns = exchange(turned)
    if merged:
        filters = [own_filters, lax.ppermute(own_filters, "lat", [(0, 1), (1, 0)])]
    else:
        above, below = from_bands(own_filters)
        filters = [above, own_filters, below]
    pool = (bands if merged else 3, *own_filters.shape)

    def lay(filters, backward):
        some = wide[backward]
        shape = (rows + extra_rows(some), kernels * lon_dev, 6 * LANES)
        return pl.pallas_call(
            partial(table_kernel, some, rows, bands, lon_dev, merged, bool(backward)),
            out_shape=jax.ShapeDtypeStruct(shape, BF16),
            scratch_shapes=[pltpu.VMEM(pool, jnp.float32)],
            compiler_params=SMALL,
        )(*filters)

    def convolve(values, table, backward):
        values = values.reshape(segments, height, cells)
        halo = [] if merged else from_bands(values[0])
        return pl.pallas_call(
            partial(
                conv_kernel, wide[backward], rows, bands, lon_dev, everyone, share, bool(backward)
            ),
            out_shape=jax.ShapeDtypeStruct(values.shape, BF16),
            scratch_shapes=[
                pltpu.VMEM((rows + 2, (2 * SMAX + 1) * lon_dev, height), BF16),
                pltpu.VMEM((rows * lon_dev, kernels * height), BF16),
            ],
            compiler_params=SMALL,
        )(w_group, values, table, *halo)

    mixed_in = convolve(columns, lay(filters, 0), 0)
    mixed_in, filters = lax.optimization_barrier((mixed_in, filters))
    mixed_in = exchange(mixed_in)
    outputs, grad_mixed = pl.pallas_call(
        dense_kernel,
        out_shape=(jax.ShapeDtypeStruct((cells, channels), BF16), square),
        compiler_params=SMALL,
    )(mixed_in.reshape(channels, cells), w_mix, grad_out.reshape(cells, channels))
    grad_in = exchange(convolve(exchange(grad_mixed), lay(filters, 1), 1))
    grad_in = transposed(grad_in.reshape(channels, cells))
    return outputs.reshape(inputs.shape), grad_in.reshape(inputs.shape)


def solution(mesh):
    return jax.shard_map(
        body,
        mesh=mesh,
        in_specs=(
            P("lat", "lon", None),
            P(None, "lat", None, None),
            P("lat"),
            P(),
            P(),
            P("lat", "lon", None),
        ),
        out_specs=(P("lat", "lon", None), P("lat", "lon", None)),
        check_vma=False,
    )
```

```python
from functools import partial

import jax
import jax.numpy as jnp
from jax import lax
from jax.experimental import pallas as pl
from jax.experimental.pallas import tpu as pltpu
from jax.sharding import PartitionSpec as P

GROUP = 4
SMAX = 4


LANES = 128
BF16 = jnp.bfloat16
ALONG = (((1,), (1,)), ((), ()))
SMALL = pltpu.CompilerParams(vmem_limit_bytes=4 * 2**20)
LARGE = pltpu.CompilerParams(vmem_limit_bytes=12 * 2**20)


def width_bound(row, row_total):
    pole = min(row, row_total - 1 - row)
    return min(SMAX, max(1, 2 * SMAX // (pole + 1)) + 1)


def reaches(row_count, bands):
    total = row_count * bands
    bound = [width_bound(row, total) for row in range(total)]
    near = [max(bound[max(0, row - 1) : row + 2]) for row in range(total)]
    return bound, near


def iota(shape, axis):
    return lax.broadcasted_iota(jnp.int32, shape, axis)


def turned_by_identity(values):
    count = values.shape[1]
    unit = jnp.where(iota((count, count), 0) == iota((count, count), 1), 1.0, 0.0).astype(BF16)
    return lax.dot_general(unit, values, ALONG, preferred_element_type=jnp.float32).astype(BF16)


def transpose_kernel(x_ref, o_ref):
    o_ref[...] = turned_by_identity(x_ref[...])


def transposed(values):
    return pl.pallas_call(
        transpose_kernel,
        out_shape=jax.ShapeDtypeStruct(values.shape[::-1], values.dtype),
        compiler_params=SMALL,
    )(values)


def enter_kernel(lon_dev, w_ref, x_hbm, p_hbm, o_ref, f_ref, x_ref, p_ref, x_done, p_done):
    fetch_x = pltpu.make_async_copy(x_hbm, x_ref, x_done)
    fetch_p = pltpu.make_async_copy(p_hbm, p_ref, p_done)
    fetch_x.start()
    fetch_p.start()
    fetch_x.wait()
    o_ref[...] = turned_by_identity(x_ref[...])
    fetch_p.wait()
    kernels, taps, rows, cells = p_ref.shape
    shape = (rows, LANES)
    line, lane = iota(shape, 0), iota(shape, 1)
    reach = jnp.zeros(shape, jnp.int32)
    for row in range(rows):
        reach = jnp.where(line == row, w_ref[row] * lon_dev, reach)
    scale = lax.rsqrt(3.0 * (2.0 * reach.astype(jnp.float32) + 1.0))
    for tile in range(3):
        offset = lane + (tile * LANES - SMAX * lon_dev)
        keep = jnp.where(jnp.abs(offset) <= reach, scale, 0.0)
        for k in range(kernels):
            for tap in range(taps):
                if tile < 2:
                    values = p_ref[k, tap, :, pl.ds(tile * LANES, LANES)]
                else:
                    values = p_ref[k, tap, :, pl.ds(cells - 1, 1)]
                    values = jnp.where(lane == 0, values, 0.0)
                f_ref[k, tap, :, pl.ds(tile * LANES, LANES)] = (
                    (values * keep).astype(BF16).astype(jnp.float32)
                )


def collect(bands, merged, backward, filter_refs, f):
    if merged:
        band = lax.axis_index("lat")
        f[band] = filter_refs[0][...]
        f[1 - band] = filter_refs[1][...]
    else:
        for segment, ref in enumerate(filter_refs):
            f[segment] = ref[...]
    if backward:
        segments, kernels, taps, lines, width = f.shape
        shape = (width, width)
        mirror = jnp.where(iota(shape, 0) + iota(shape, 1) == 2 * LANES, 1.0, 0.0).astype(BF16)
        for segment in range(segments):
            values = f[segment].reshape(kernels * taps * lines, width).astype(BF16)
            values = jnp.dot(values, mirror, preferred_element_type=jnp.float32)
            f[segment] = values.reshape(kernels, taps, lines, width)


def lay_toeplitz(rows, wide, lon_dev, merged, backward, f, t_ref, e_ref):
    segments, kernels, _, held, _ = f.shape
    shape = (lon_dev, LANES)
    lane, line = iota(shape, 1), iota(shape, 0)
    upper = lane >= line
    corner = lane == line
    for row in range(rows):
        for tap in range(3):
            source, column = (row + tap - 1, 2 - tap) if backward else (row, tap)
            source += 0 if merged else held
            segment, inner = divmod(source, held)
            present = 0 <= segment < segments
            for k in range(kernels):
                here = pl.ds(k * lon_dev, lon_dev)

                def turned(tile):
                    values = f[segment, k, column, pl.ds(inner, 1), pl.ds(tile * LANES, LANES)]
                    values = jnp.broadcast_to(values, shape)
                    return pltpu.roll(values, 0, 1, stride=1, stride_axis=0)

                if present:
                    first, second = turned(0), turned(1)
                    parts = [jnp.where(upper, first, 0.0), jnp.where(upper, second, first)]
                else:
                    parts = [jnp.zeros(shape, jnp.float32)] * 2
                for i, part in enumerate(parts):
                    t_ref[row, here, pl.ds((tap * 2 + i) * LANES, LANES)] = part.astype(BF16)
                if row in wide:
                    last = parts[0]
                    if present:
                        last = jnp.where(corner, turned(2), jnp.where(upper, 0.0, second))
                    at = pl.ds(tap * LANES, LANES)
                    e_ref[wide.index(row), here, at] = last.astype(BF16)


def mixer_of(everyone, share, backward, w_ref, height):
    kernels, group, channels = w_ref.shape
    first = lax.axis_index(everyone[0])
    for axis in everyone[1:]:
        first = first * lax.axis_size(axis) + lax.axis_index(axis)
    shape = (channels, height)
    chosen = iota(shape, 0) == first * share + iota(shape, 1) % share
    weights = jnp.concatenate([w_ref[k].astype(jnp.float32) for k in range(kernels)], axis=0)
    weights = jnp.dot(
        weights.astype(BF16),
        jnp.where(chosen, 1.0, 0.0).astype(BF16),
        preferred_element_type=jnp.float32,
    )
    if backward:
        spread = [
            jnp.concatenate([weights[k * group : (k + 1) * group]] * (height // group), axis=0)
            for k in range(kernels)
        ]
        spread = jnp.concatenate(spread, axis=1)
    else:
        shape = (kernels * group, kernels * height)
        line, lane = iota(shape, 0), iota(shape, 1)
        pick = line == (lane // height) * group + lane % group
        spread = lax.dot_general(
            weights.astype(BF16),
            jnp.where(pick, 1.0, 0.0).astype(BF16),
            (((0,), (0,)), ((), ())),
            preferred_element_type=jnp.float32,
        )
    shape = (height, kernels * height)
    same = iota(shape, 0) // group == (iota(shape, 1) % height) // group
    return jnp.where(same, spread, 0.0).astype(BF16)


def conv_kernel(
    table, bands, lon_dev, merged, everyone, share, backward, w_ref, own_ref, *refs
):
    count = 2 if merged else 3
    filter_refs, refs = refs[:count], refs[count:]
    *halo_refs, o_ref, f, t_ref, e_ref, xs, z_ref = refs
    segments, height, cells = own_ref.shape
    rows = len(table)
    held = rows // segments
    kernels = f.shape[1]
    wide = [row for row, reach in enumerate(table) if reach == SMAX]
    collect(bands, merged, backward, filter_refs, f)
    lay_toeplitz(rows, wide, lon_dev, merged, backward, f, t_ref, e_ref)

    def put(values, first):
        values = values.T
        count = values.shape[0] // lon_dev
        for shard in range(-SMAX, SMAX + 1):
            turned = pltpu.roll(values, -shard * share % height, 1) if shard else values
            at = pl.ds((shard + SMAX) * lon_dev, lon_dev)
            xs[pl.ds(first + 1, count), at, :] = turned.reshape(
                count, lon_dev, height
            )

    per_tile = LANES // lon_dev
    blank = jnp.zeros(xs.shape[1:], BF16)
    if halo_refs:
        band = lax.axis_index("lat")
        above = halo_refs[0][:, pl.ds(cells - LANES, LANES)]
        put(above, 0)
        edge = xs[per_tile].astype(jnp.float32)
        xs[0] = jnp.where(band > 0, edge, 0.0).astype(BF16)
        put(halo_refs[1][:, pl.ds(0, LANES)], 0)
        edge = xs[1].astype(jnp.float32)
        xs[rows + 1] = jnp.where(band < bands - 1, edge, 0.0).astype(BF16)
    else:
        xs[0] = blank
        xs[rows + 1] = blank
    for segment in range(segments):
        put(own_ref[segment], segment * held)
    span = 2 * LANES
    for row in range(rows):
        window = xs[row : row + 3, :span, :].reshape(3 * span, height)
        total = jnp.dot(t_ref[row], window, preferred_element_type=jnp.float32)
        if row in wide:
            beyond = []
            for tap in range(3):
                beyond += [xs[row + tap, span:, :], blank[: LANES - lon_dev]]
            total += jnp.dot(
                e_ref[wide.index(row)],
                jnp.concatenate(beyond, axis=0),
                preferred_element_type=jnp.float32,
            )
        total = total.astype(BF16)
        for k in range(kernels):
            z_ref[pl.ds(row * lon_dev, lon_dev), pl.ds(k * height, height)] = total[
                k * lon_dev : (k + 1) * lon_dev
            ]
    mixer = mixer_of(everyone, share, backward, w_ref, height)
    for segment in range(segments):
        part = z_ref[pl.ds(segment * cells, cells), :]
        mixed = lax.dot_general(mixer, part, ALONG, preferred_element_type=jnp.float32)
        o_ref[segment] = mixed.astype(o_ref.dtype)


def dense_kernel(m_ref, w_ref, g_ref, o_ref, d_ref):
    mixed_in = turned_by_identity(m_ref[...])
    pre = jnp.dot(mixed_in, w_ref[...], preferred_element_type=jnp.float32)
    slope = 0.7978845608028654
    square = pre * pre
    bent = jnp.tanh(slope * (pre + 0.044715 * (square * pre)))
    half = 0.5 * (1.0 + bent)
    o_ref[...] = (pre * half).astype(o_ref.dtype)
    rise = half + 0.5 * pre * (1.0 - bent * bent) * (slope * (1.0 + 3.0 * 0.044715 * square))
    grad_pre = (g_ref[...].astype(jnp.float32) * rise).astype(BF16)
    d_ref[...] = lax.dot_general(
        w_ref[...], grad_pre, ALONG, preferred_element_type=jnp.float32
    ).astype(d_ref.dtype)


def from_bands(values):
    count = lax.axis_size("lat")
    up = [(i, i + 1) for i in range(count - 1)]
    down = [(j, i) for i, j in up]
    return [lax.ppermute(values, "lat", up), lax.ppermute(values, "lat", down)]


def body(inputs, psi_raw, widths, w_group, w_mix, grad_out):
    row_count, lon_dev, channels = inputs.shape
    kernels = psi_raw.shape[0]
    blocks, bands = lax.axis_size("lon"), lax.axis_size("lat")
    cells = row_count * lon_dev
    merged = bands == 2 and channels % (2 * GROUP * bands * blocks) == 0
    everyone = ("lat", "lon") if merged else ("lon",)
    segments = bands if merged else 1
    share = channels // (segments * blocks)
    height = blocks * share
    rows = segments * row_count
    tables = [
        tuple(max(table[row::rows]) for row in range(rows))
        for table in reaches(row_count, bands)
    ]
    square = jax.ShapeDtypeStruct((channels, cells), BF16)

    def exchange(values):
        parted = values.reshape(segments * blocks, share, cells)
        return lax.all_to_all(parted, everyone, 0, 0)

    turned, own_filters = pl.pallas_call(
        partial(enter_kernel, lon_dev),
        out_shape=(
            square,
            jax.ShapeDtypeStruct((kernels, 3, row_count, 3 * LANES), jnp.float32),
        ),
        in_specs=[
            pl.BlockSpec(memory_space=pltpu.SMEM),
            pl.BlockSpec(memory_space=pltpu.HBM),
            pl.BlockSpec(memory_space=pltpu.HBM),
        ],
        scratch_shapes=[
            pltpu.VMEM((cells, channels), BF16),
            pltpu.VMEM((kernels, 3, row_count, psi_raw.shape[-1]), jnp.float32),
            pltpu.SemaphoreType.DMA,
            pltpu.SemaphoreType.DMA,
        ],
        compiler_params=SMALL,
    )(widths, inputs.reshape(cells, channels), psi_raw.transpose(0, 2, 1, 3))
    columns = exchange(turned)
    if merged:
        filters = [own_filters, lax.ppermute(own_filters, "lat", [(0, 1), (1, 0)])]
    else:
        above, below = from_bands(own_filters)
        filters = [above, own_filters, below]
    pool = (bands if merged else 3, *own_filters.shape)

    def convolve(values, backward):
        values = values.reshape(segments, height, cells)
        halo = [] if merged else from_bands(values[0])
        return pl.pallas_call(
            partial(
                conv_kernel, tables[backward], bands, lon_dev, merged, everyone, share,
                bool(backward),
            ),
            out_shape=jax.ShapeDtypeStruct(values.shape, BF16),
            scratch_shapes=[
                pltpu.VMEM(pool, jnp.float32),
                pltpu.VMEM((rows, kernels * lon_dev, 6 * LANES), BF16),
                pltpu.VMEM((tables[backward].count(SMAX), kernels * lon_dev, 3 * LANES), BF16),
                pltpu.VMEM((rows + 2, (2 * SMAX + 1) * lon_dev, height), BF16),
                pltpu.VMEM((rows * lon_dev, kernels * height), BF16),
            ],
            compiler_params=LARGE,
        )(w_group, values, *filters, *halo)

    mixed_in = exchange(convolve(columns, 0))
    outputs, grad_mixed = pl.pallas_call(
        dense_kernel,
        out_shape=(jax.ShapeDtypeStruct((cells, channels), BF16), square),
        compiler_params=SMALL,
    )(mixed_in.reshape(channels, cells), w_mix, grad_out.reshape(cells, channels))
    grad_in = exchange(convolve(exchange(grad_mixed), 1))
    grad_in = transposed(grad_in.reshape(channels, cells))
    return outputs.reshape(inputs.shape), grad_in.reshape(inputs.shape)


def solution(mesh):
    return jax.shard_map(
        body,
        mesh=mesh,
        in_specs=(
            P("lat", "lon", None),
            P(None, "lat", None, None),
            P("lat"),
            P(),
            P(),
            P("lat", "lon", None),
        ),
        out_specs=(P("lat", "lon", None), P("lat", "lon", None)),
        check_vma=False,
    )
```

```python
from functools import partial

import jax
import jax.numpy as jnp
from jax import lax
from jax.experimental import pallas as pl
from jax.experimental.pallas import tpu as pltpu
from jax.sharding import PartitionSpec as P

GROUP = 4
SMAX = 4


LANES = 128
BF16 = jnp.bfloat16
ALONG = (((1,), (1,)), ((), ()))
SMALL = pltpu.CompilerParams(vmem_limit_bytes=4 * 2**20)
LARGE = pltpu.CompilerParams(vmem_limit_bytes=12 * 2**20)


def width_bound(row, row_total):
    pole = min(row, row_total - 1 - row)
    return min(SMAX, max(1, 2 * SMAX // (pole + 1)) + 1)


def reaches(row_count, bands):
    total = row_count * bands
    bound = [width_bound(row, total) for row in range(total)]
    near = [max(bound[max(0, row - 1) : row + 2]) for row in range(total)]
    return bound, near


def iota(shape, axis):
    return lax.broadcasted_iota(jnp.int32, shape, axis)


def turned_by_identity(values):
    count = values.shape[1]
    unit = jnp.where(iota((count, count), 0) == iota((count, count), 1), 1.0, 0.0).astype(BF16)
    return lax.dot_general(unit, values, ALONG, preferred_element_type=jnp.float32).astype(BF16)


def transpose_kernel(x_ref, o_ref):
    o_ref[...] = turned_by_identity(x_ref[...])


def transposed(values):
    return pl.pallas_call(
        transpose_kernel,
        out_shape=jax.ShapeDtypeStruct(values.shape[::-1], values.dtype),
        compiler_params=SMALL,
    )(values)


def enter_kernel(
    lon_dev, w_ref, x_far, p_far, o_far, f_far, x_ref, p_ref, o_ref, f_ref, done
):
    fetch_x = pltpu.make_async_copy(x_far, x_ref, done.at[0])
    fetch_p = pltpu.make_async_copy(p_far, p_ref, done.at[1])
    store_o = pltpu.make_async_copy(o_ref, o_far, done.at[2])
    store_f = pltpu.make_async_copy(f_ref, f_far, done.at[3])
    fetch_x.start()
    fetch_p.start()
    fetch_x.wait()
    o_ref[...] = turned_by_identity(x_ref[...])
    store_o.start()
    fetch_p.wait()
    kernels, taps, rows, cells = p_ref.shape
    shape = (rows, LANES)
    line, lane = iota(shape, 0), iota(shape, 1)
    reach = jnp.zeros(shape, jnp.int32)
    for row in range(rows):
        reach = jnp.where(line == row, w_ref[row] * lon_dev, reach)
    scale = lax.rsqrt(3.0 * (2.0 * reach.astype(jnp.float32) + 1.0))
    for tile in range(3):
        offset = lane + (tile * LANES - SMAX * lon_dev)
        keep = jnp.where(jnp.abs(offset) <= reach, scale, 0.0)
        for k in range(kernels):
            for tap in range(taps):
                if tile < 2:
                    values = p_ref[k, tap, :, pl.ds(tile * LANES, LANES)]
                else:
                    values = p_ref[k, tap, :, pl.ds(cells - 1, 1)]
                    values = jnp.where(lane == 0, values, 0.0)
                f_ref[k, tap, :, pl.ds(tile * LANES, LANES)] = (
                    (values * keep).astype(BF16).astype(jnp.float32)
                )
    store_f.start()
    store_o.wait()
    store_f.wait()


def collect(bands, merged, backward, filter_refs, f):
    if merged:
        band = lax.axis_index("lat")
        f[band] = filter_refs[0][...]
        f[1 - band] = filter_refs[1][...]
    else:
        for segment, ref in enumerate(filter_refs):
            f[segment] = ref[...]
    if backward:
        segments, kernels, taps, lines, width = f.shape
        shape = (width, width)
        mirror = jnp.where(iota(shape, 0) + iota(shape, 1) == 2 * LANES, 1.0, 0.0).astype(BF16)
        for segment in range(segments):
            values = f[segment].reshape(kernels * taps * lines, width).astype(BF16)
            values = jnp.dot(values, mirror, preferred_element_type=jnp.float32)
            f[segment] = values.reshape(kernels, taps, lines, width)


def lay_toeplitz(rows, wide, lon_dev, merged, backward, f, t_ref, e_ref):
    segments, kernels, _, held, _ = f.shape
    shape = (lon_dev, LANES)
    lane, line = iota(shape, 1), iota(shape, 0)
    upper = lane >= line
    corner = lane == line
    for row in range(rows):
        for tap in range(3):
            source, column = (row + tap - 1, 2 - tap) if backward else (row, tap)
            source += 0 if merged else held
            segment, inner = divmod(source, held)
            present = 0 <= segment < segments
            for k in range(kernels):
                here = pl.ds(k * lon_dev, lon_dev)

                def turned(tile):
                    values = f[segment, k, column, pl.ds(inner, 1), pl.ds(tile * LANES, LANES)]
                    values = jnp.broadcast_to(values, shape)
                    return pltpu.roll(values, 0, 1, stride=1, stride_axis=0)

                if present:
                    first, second = turned(0), turned(1)
                    parts = [jnp.where(upper, first, 0.0), jnp.where(upper, second, first)]
                else:
                    parts = [jnp.zeros(shape, jnp.float32)] * 2
                for i, part in enumerate(parts):
                    t_ref[row, here, pl.ds((tap * 2 + i) * LANES, LANES)] = part.astype(BF16)
                if row in wide:
                    last = parts[0]
                    if present:
                        last = jnp.where(corner, turned(2), jnp.where(upper, 0.0, second))
                    at = pl.ds(tap * LANES, LANES)
                    e_ref[wide.index(row), here, at] = last.astype(BF16)


def mixer_of(everyone, share, backward, w_ref, height):
    kernels, group, channels = w_ref.shape
    first = lax.axis_index(everyone[0])
    for axis in everyone[1:]:
        first = first * lax.axis_size(axis) + lax.axis_index(axis)
    shape = (channels, height)
    chosen = iota(shape, 0) == first * share + iota(shape, 1) % share
    weights = jnp.concatenate([w_ref[k].astype(jnp.float32) for k in range(kernels)], axis=0)
    weights = jnp.dot(
        weights.astype(BF16),
        jnp.where(chosen, 1.0, 0.0).astype(BF16),
        preferred_element_type=jnp.float32,
    )
    if backward:
        spread = [
            jnp.concatenate([weights[k * group : (k + 1) * group]] * (height // group), axis=0)
            for k in range(kernels)
        ]
        spread = jnp.concatenate(spread, axis=1)
    else:
        shape = (kernels * group, kernels * height)
        line, lane = iota(shape, 0), iota(shape, 1)
        pick = line == (lane // height) * group + lane % group
        spread = lax.dot_general(
            weights.astype(BF16),
            jnp.where(pick, 1.0, 0.0).astype(BF16),
            (((0,), (0,)), ((), ())),
            preferred_element_type=jnp.float32,
        )
    shape = (height, kernels * height)
    same = iota(shape, 0) // group == (iota(shape, 1) % height) // group
    return jnp.where(same, spread, 0.0).astype(BF16)


def conv_kernel(
    table, bands, lon_dev, merged, everyone, share, backward, w_ref, own_ref, *refs
):
    count = 2 if merged else 3
    filter_refs, refs = refs[:count], refs[count:]
    *halo_refs, o_ref, f, t_ref, e_ref, xs, z_ref = refs
    segments, height, cells = own_ref.shape
    rows = len(table)
    held = rows // segments
    kernels = f.shape[1]
    wide = [row for row, reach in enumerate(table) if reach == SMAX]
    collect(bands, merged, backward, filter_refs, f)
    lay_toeplitz(rows, wide, lon_dev, merged, backward, f, t_ref, e_ref)

    def put(values, first):
        values = values.T
        count = values.shape[0] // lon_dev
        for shard in range(-SMAX, SMAX + 1):
            turned = pltpu.roll(values, -shard * share % height, 1) if shard else values
            at = pl.ds((shard + SMAX) * lon_dev, lon_dev)
            xs[pl.ds(first + 1, count), at, :] = turned.reshape(
                count, lon_dev, height
            )

    per_tile = LANES // lon_dev
    blank = jnp.zeros(xs.shape[1:], BF16)
    if halo_refs:
        band = lax.axis_index("lat")
        above = halo_refs[0][:, pl.ds(cells - LANES, LANES)]
        put(above, 0)
        edge = xs[per_tile].astype(jnp.float32)
        xs[0] = jnp.where(band > 0, edge, 0.0).astype(BF16)
        put(halo_refs[1][:, pl.ds(0, LANES)], 0)
        edge = xs[1].astype(jnp.float32)
        xs[rows + 1] = jnp.where(band < bands - 1, edge, 0.0).astype(BF16)
    else:
        xs[0] = blank
        xs[rows + 1] = blank
    for segment in range(segments):
        put(own_ref[segment], segment * held)
    span = 2 * LANES
    for row in range(rows):
        window = xs[row : row + 3, :span, :].reshape(3 * span, height)
        total = jnp.dot(t_ref[row], window, preferred_element_type=jnp.float32)
        if row in wide:
            beyond = []
            for tap in range(3):
                beyond += [xs[row + tap, span:, :], blank[: LANES - lon_dev]]
            total += jnp.dot(
                e_ref[wide.index(row)],
                jnp.concatenate(beyond, axis=0),
                preferred_element_type=jnp.float32,
            )
        total = total.astype(BF16)
        for k in range(kernels):
            z_ref[pl.ds(row * lon_dev, lon_dev), pl.ds(k * height, height)] = total[
                k * lon_dev : (k + 1) * lon_dev
            ]
    mixer = mixer_of(everyone, share, backward, w_ref, height)
    for segment in range(segments):
        part = z_ref[pl.ds(segment * cells, cells), :]
        mixed = lax.dot_general(mixer, part, ALONG, preferred_element_type=jnp.float32)
        o_ref[segment] = mixed.astype(o_ref.dtype)


def dense_kernel(m_ref, w_ref, g_ref, o_ref, d_ref):
    mixed_in = turned_by_identity(m_ref[...])
    pre = jnp.dot(mixed_in, w_ref[...], preferred_element_type=jnp.float32)
    slope = 0.7978845608028654
    square = pre * pre
    bent = jnp.tanh(slope * (pre + 0.044715 * (square * pre)))
    half = 0.5 * (1.0 + bent)
    o_ref[...] = (pre * half).astype(o_ref.dtype)
    rise = half + 0.5 * pre * (1.0 - bent * bent) * (slope * (1.0 + 3.0 * 0.044715 * square))
    grad_pre = (g_ref[...].astype(jnp.float32) * rise).astype(BF16)
    d_ref[...] = lax.dot_general(
        w_ref[...], grad_pre, ALONG, preferred_element_type=jnp.float32
    ).astype(d_ref.dtype)


def from_bands(values):
    count = lax.axis_size("lat")
    up = [(i, i + 1) for i in range(count - 1)]
    down = [(j, i) for i, j in up]
    return [lax.ppermute(values, "lat", up), lax.ppermute(values, "lat", down)]


def body(inputs, psi_raw, widths, w_group, w_mix, grad_out):
    row_count, lon_dev, channels = inputs.shape
    kernels = psi_raw.shape[0]
    blocks, bands = lax.axis_size("lon"), lax.axis_size("lat")
    cells = row_count * lon_dev
    merged = bands == 2 and channels % (2 * GROUP * bands * blocks) == 0
    everyone = ("lat", "lon") if merged else ("lon",)
    segments = bands if merged else 1
    share = channels // (segments * blocks)
    height = blocks * share
    rows = segments * row_count
    tables = [
        tuple(max(table[row::rows]) for row in range(rows))
        for table in reaches(row_count, bands)
    ]
    square = jax.ShapeDtypeStruct((channels, cells), BF16)

    def exchange(values):
        parted = values.reshape(segments * blocks, share, cells)
        return lax.all_to_all(parted, everyone, 0, 0)

    shapes = [
        (cells, channels),
        (kernels, 3, row_count, psi_raw.shape[-1]),
        (channels, cells),
        (kernels, 3, row_count, 3 * LANES),
    ]
    kinds = [BF16, jnp.float32, BF16, jnp.float32]
    anywhere = pl.BlockSpec(memory_space=pl.ANY)
    turned, own_filters = pl.pallas_call(
        partial(enter_kernel, lon_dev),
        out_shape=[jax.ShapeDtypeStruct(*some) for some in list(zip(shapes, kinds))[2:]],
        in_specs=[pl.BlockSpec(memory_space=pltpu.SMEM), anywhere, anywhere],
        out_specs=[anywhere, anywhere],
        scratch_shapes=[pltpu.VMEM(*some) for some in zip(shapes, kinds)]
        + [pltpu.SemaphoreType.DMA((4,))],
    )(widths, inputs.reshape(cells, channels), psi_raw.transpose(0, 2, 1, 3))
    columns = exchange(turned)
    if merged:
        filters = [own_filters, lax.ppermute(own_filters, "lat", [(0, 1), (1, 0)])]
    else:
        above, below = from_bands(own_filters)
        filters = [above, own_filters, below]
    pool = (bands if merged else 3, *own_filters.shape)

    def convolve(values, backward):
        values = values.reshape(segments, height, cells)
        halo = [] if merged else from_bands(values[0])
        return pl.pallas_call(
            partial(
                conv_kernel, tables[backward], bands, lon_dev, merged, everyone, share,
                bool(backward),
            ),
            out_shape=jax.ShapeDtypeStruct(values.shape, BF16),
            scratch_shapes=[
                pltpu.VMEM(pool, jnp.float32),
                pltpu.VMEM((rows, kernels * lon_dev, 6 * LANES), BF16),
                pltpu.VMEM((tables[backward].count(SMAX), kernels * lon_dev, 3 * LANES), BF16),
                pltpu.VMEM((rows + 2, (2 * SMAX + 1) * lon_dev, height), BF16),
                pltpu.VMEM((rows * lon_dev, kernels * height), BF16),
            ],
            compiler_params=LARGE,
        )(w_group, values, *filters, *halo)

    mixed_in = exchange(convolve(columns, 0))
    outputs, grad_mixed = pl.pallas_call(
        dense_kernel,
        out_shape=(jax.ShapeDtypeStruct((cells, channels), BF16), square),
        compiler_params=SMALL,
    )(mixed_in.reshape(channels, cells), w_mix, grad_out.reshape(cells, channels))
    grad_in = exchange(convolve(exchange(grad_mixed), 1))
    grad_in = transposed(grad_in.reshape(channels, cells))
    return outputs.reshape(inputs.shape), grad_in.reshape(inputs.shape)


def solution(mesh):
    return jax.shard_map(
        body,
        mesh=mesh,
        in_specs=(
            P("lat", "lon", None),
            P(None, "lat", None, None),
            P("lat"),
            P(),
            P(),
            P("lat", "lon", None),
        ),
        out_specs=(P("lat", "lon", None), P("lat", "lon", None)),
        check_vma=False,
    )
```

```python
from functools import partial

import jax
import jax.numpy as jnp
from jax import lax
from jax.experimental import pallas as pl
from jax.experimental.pallas import tpu as pltpu
from jax.sharding import PartitionSpec as P

GROUP = 4
SMAX = 4


LANES = 128
BF16 = jnp.bfloat16
ALONG = (((1,), (1,)), ((), ()))
SMALL = pltpu.CompilerParams(vmem_limit_bytes=4 * 2**20)
LARGE = pltpu.CompilerParams(vmem_limit_bytes=12 * 2**20)


def width_bound(row, row_total):
    pole = min(row, row_total - 1 - row)
    return min(SMAX, max(1, 2 * SMAX // (pole + 1)) + 1)


def reaches(row_count, bands):
    total = row_count * bands
    bound = [width_bound(row, total) for row in range(total)]
    near = [max(bound[max(0, row - 1) : row + 2]) for row in range(total)]
    return bound, near


def iota(shape, axis):
    return lax.broadcasted_iota(jnp.int32, shape, axis)


def turned_by_identity(values):
    count = values.shape[1]
    unit = jnp.where(iota((count, count), 0) == iota((count, count), 1), 1.0, 0.0).astype(BF16)
    return lax.dot_general(unit, values, ALONG, preferred_element_type=jnp.float32).astype(BF16)


def transpose_kernel(x_ref, o_ref):
    o_ref[...] = turned_by_identity(x_ref[...])


def transposed(values):
    return pl.pallas_call(
        transpose_kernel,
        out_shape=jax.ShapeDtypeStruct(values.shape[::-1], values.dtype),
        compiler_params=SMALL,
    )(values)


def enter_kernel(lon_dev, w_ref, x_ref, p_ref, o_ref, f_ref):
    o_ref[...] = x_ref[...].T
    kernels, taps, rows, cells = p_ref.shape
    shape = (rows, LANES)
    line, lane = iota(shape, 0), iota(shape, 1)
    reach = jnp.zeros(shape, jnp.int32)
    for row in range(rows):
        reach = jnp.where(line == row, w_ref[row] * lon_dev, reach)
    scale = lax.rsqrt(3.0 * (2.0 * reach.astype(jnp.float32) + 1.0))
    for tile in range(3):
        offset = lane + (tile * LANES - SMAX * lon_dev)
        keep = jnp.where(jnp.abs(offset) <= reach, scale, 0.0)
        for k in range(kernels):
            for tap in range(taps):
                if tile < 2:
                    values = p_ref[k, tap, :, pl.ds(tile * LANES, LANES)]
                else:
                    values = p_ref[k, tap, :, pl.ds(cells - 1, 1)]
                    values = jnp.where(lane == 0, values, 0.0)
                f_ref[k, tap, :, pl.ds(tile * LANES, LANES)] = (
                    (values * keep).astype(BF16).astype(jnp.float32)
                )


def collect(bands, merged, backward, filter_refs, f):
    if merged:
        band = lax.axis_index("lat")
        f[band] = filter_refs[0][...]
        f[1 - band] = filter_refs[1][...]
    else:
        for segment, ref in enumerate(filter_refs):
            f[segment] = ref[...]
    if backward:
        segments, kernels, taps, lines, width = f.shape
        shape = (width, width)
        mirror = jnp.where(iota(shape, 0) + iota(shape, 1) == 2 * LANES, 1.0, 0.0).astype(BF16)
        for segment in range(segments):
            values = f[segment].reshape(kernels * taps * lines, width).astype(BF16)
            values = jnp.dot(values, mirror, preferred_element_type=jnp.float32)
            f[segment] = values.reshape(kernels, taps, lines, width)


def lay_toeplitz(rows, wide, lon_dev, merged, backward, f, t_ref, e_ref):
    segments, kernels, _, held, _ = f.shape
    shape = (lon_dev, LANES)
    lane, line = iota(shape, 1), iota(shape, 0)
    upper = lane >= line
    corner = lane == line
    zero = jnp.zeros(shape, BF16)
    for row in range(rows):
        for tap in range(3):
            source, column = (row + tap - 1, 2 - tap) if backward else (row, tap)
            source += 0 if merged else held
            segment, inner = divmod(source, held)
            present = 0 <= segment < segments
            for k in range(kernels):
                here = pl.ds(k * lon_dev, lon_dev)

                def turned(tile):
                    values = f[segment, k, column, pl.ds(inner, 1), pl.ds(tile * LANES, LANES)]
                    values = jnp.broadcast_to(values, shape).astype(BF16)
                    return pltpu.roll(values, 0, 1, stride=1, stride_axis=0)

                if present:
                    first, second = turned(0), turned(1)
                    parts = [jnp.where(upper, first, zero), jnp.where(upper, second, first)]
                else:
                    parts = [zero] * 2
                for i, part in enumerate(parts):
                    t_ref[row, here, pl.ds((tap * 2 + i) * LANES, LANES)] = part
                if row in wide:
                    last = parts[0]
                    if present:
                        last = jnp.where(corner, turned(2), jnp.where(upper, zero, second))
                    at = pl.ds(tap * LANES, LANES)
                    e_ref[wide.index(row), here, at] = last


def mixer_of(everyone, share, backward, w_ref, height):
    kernels, group, channels = w_ref.shape
    first = lax.axis_index(everyone[0])
    for axis in everyone[1:]:
        first = first * lax.axis_size(axis) + lax.axis_index(axis)
    shape = (channels, height)
    chosen = iota(shape, 0) == first * share + iota(shape, 1) % share
    weights = jnp.concatenate([w_ref[k].astype(jnp.float32) for k in range(kernels)], axis=0)
    weights = jnp.dot(
        weights.astype(BF16),
        jnp.where(chosen, 1.0, 0.0).astype(BF16),
        preferred_element_type=jnp.float32,
    )
    if backward:
        spread = [
            jnp.concatenate([weights[k * group : (k + 1) * group]] * (height // group), axis=0)
            for k in range(kernels)
        ]
        spread = jnp.concatenate(spread, axis=1)
    else:
        shape = (kernels * group, kernels * height)
        line, lane = iota(shape, 0), iota(shape, 1)
        pick = line == (lane // height) * group + lane % group
        spread = lax.dot_general(
            weights.astype(BF16),
            jnp.where(pick, 1.0, 0.0).astype(BF16),
            (((0,), (0,)), ((), ())),
            preferred_element_type=jnp.float32,
        )
    shape = (height, kernels * height)
    same = iota(shape, 0) // group == (iota(shape, 1) % height) // group
    return jnp.where(same, spread, 0.0).astype(BF16)


def conv_kernel(
    table, bands, lon_dev, merged, everyone, share, backward, w_ref, own_ref, *refs
):
    count = 2 if merged else 3
    filter_refs, refs = refs[:count], refs[count:]
    *halo_refs, o_ref, f, t_ref, e_ref, xs, z_ref = refs
    segments, height, cells = own_ref.shape
    rows = len(table)
    held = rows // segments
    kernels = f.shape[1]
    wide = [row for row, reach in enumerate(table) if reach == SMAX]
    collect(bands, merged, backward, filter_refs, f)
    lay_toeplitz(rows, wide, lon_dev, merged, backward, f, t_ref, e_ref)

    def put(values, first):
        values = values.T
        count = values.shape[0] // lon_dev
        for shard in range(-SMAX, SMAX + 1):
            turned = pltpu.roll(values, -shard * share % height, 1) if shard else values
            at = pl.ds((shard + SMAX) * lon_dev, lon_dev)
            xs[pl.ds(first + 1, count), at, :] = turned.reshape(
                count, lon_dev, height
            )

    per_tile = LANES // lon_dev
    blank = jnp.zeros(xs.shape[1:], BF16)
    if halo_refs:
        band = lax.axis_index("lat")
        above = halo_refs[0][:, pl.ds(cells - LANES, LANES)]
        put(above, 0)
        edge = xs[per_tile].astype(jnp.float32)
        xs[0] = jnp.where(band > 0, edge, 0.0).astype(BF16)
        put(halo_refs[1][:, pl.ds(0, LANES)], 0)
        edge = xs[1].astype(jnp.float32)
        xs[rows + 1] = jnp.where(band < bands - 1, edge, 0.0).astype(BF16)
    else:
        xs[0] = blank
        xs[rows + 1] = blank
    for segment in range(segments):
        put(own_ref[segment], segment * held)
    span = 2 * LANES
    for row in range(rows):
        window = xs[row : row + 3, :span, :].reshape(3 * span, height)
        total = jnp.dot(t_ref[row], window, preferred_element_type=jnp.float32)
        if row in wide:
            beyond = []
            for tap in range(3):
                beyond += [xs[row + tap, span:, :], blank[: LANES - lon_dev]]
            total += jnp.dot(
                e_ref[wide.index(row)],
                jnp.concatenate(beyond, axis=0),
                preferred_element_type=jnp.float32,
            )
        total = total.astype(BF16)
        for k in range(kernels):
            z_ref[pl.ds(row * lon_dev, lon_dev), pl.ds(k * height, height)] = total[
                k * lon_dev : (k + 1) * lon_dev
            ]
    mixer = mixer_of(everyone, share, backward, w_ref, height)
    for segment in range(segments):
        part = z_ref[pl.ds(segment * cells, cells), :]
        mixed = lax.dot_general(mixer, part, ALONG, preferred_element_type=jnp.float32)
        o_ref[segment] = mixed.astype(o_ref.dtype)


def dense_kernel(m_ref, w_ref, g_ref, o_ref, d_ref):
    across = (((0,), (0,)), ((), ()))
    pre = lax.dot_general(m_ref[...], w_ref[...], across, preferred_element_type=jnp.float32)
    slope = 0.7978845608028654
    square = pre * pre
    bent = jnp.tanh(slope * (pre + 0.044715 * (square * pre)))
    half = 0.5 * (1.0 + bent)
    o_ref[...] = (pre * half).astype(o_ref.dtype)
    rise = half + 0.5 * pre * (1.0 - bent * bent) * (slope * (1.0 + 3.0 * 0.044715 * square))
    grad_pre = (g_ref[...].astype(jnp.float32) * rise).astype(BF16)
    d_ref[...] = lax.dot_general(
        w_ref[...], grad_pre, ALONG, preferred_element_type=jnp.float32
    ).astype(d_ref.dtype)


def from_bands(values):
    count = lax.axis_size("lat")
    up = [(i, i + 1) for i in range(count - 1)]
    down = [(j, i) for i, j in up]
    return [lax.ppermute(values, "lat", up), lax.ppermute(values, "lat", down)]


def body(inputs, psi_raw, widths, w_group, w_mix, grad_out):
    row_count, lon_dev, channels = inputs.shape
    kernels = psi_raw.shape[0]
    blocks, bands = lax.axis_size("lon"), lax.axis_size("lat")
    cells = row_count * lon_dev
    merged = bands == 2 and channels % (2 * GROUP * bands * blocks) == 0
    everyone = ("lat", "lon") if merged else ("lon",)
    segments = bands if merged else 1
    share = channels // (segments * blocks)
    height = blocks * share
    rows = segments * row_count
    tables = [
        tuple(max(table[row::rows]) for row in range(rows))
        for table in reaches(row_count, bands)
    ]
    square = jax.ShapeDtypeStruct((channels, cells), BF16)

    def exchange(values):
        parted = values.reshape(segments * blocks, share, cells)
        return lax.all_to_all(parted, everyone, 0, 0)

    turned, own_filters = pl.pallas_call(
        partial(enter_kernel, lon_dev),
        out_shape=(
            square,
            jax.ShapeDtypeStruct((kernels, 3, row_count, 3 * LANES), jnp.float32),
        ),
        in_specs=[
            pl.BlockSpec(memory_space=pltpu.SMEM),
            pl.BlockSpec(memory_space=pltpu.VMEM),
            pl.BlockSpec(memory_space=pltpu.VMEM),
        ],
    )(widths, inputs.reshape(cells, channels), psi_raw.transpose(0, 2, 1, 3))
    columns = exchange(turned)
    if merged:
        filters = [own_filters, lax.ppermute(own_filters, "lat", [(0, 1), (1, 0)])]
    else:
        above, below = from_bands(own_filters)
        filters = [above, own_filters, below]
    pool = (bands if merged else 3, *own_filters.shape)

    def convolve(values, backward):
        values = values.reshape(segments, height, cells)
        halo = [] if merged else from_bands(values[0])
        return pl.pallas_call(
            partial(
                conv_kernel, tables[backward], bands, lon_dev, merged, everyone, share,
                bool(backward),
            ),
            out_shape=jax.ShapeDtypeStruct(values.shape, BF16),
            scratch_shapes=[
                pltpu.VMEM(pool, jnp.float32),
                pltpu.VMEM((rows, kernels * lon_dev, 6 * LANES), BF16),
                pltpu.VMEM((tables[backward].count(SMAX), kernels * lon_dev, 3 * LANES), BF16),
                pltpu.VMEM((rows + 2, (2 * SMAX + 1) * lon_dev, height), BF16),
                pltpu.VMEM((rows * lon_dev, kernels * height), BF16),
            ],
            compiler_params=LARGE,
        )(w_group, values, *filters, *halo)

    mixed_in = exchange(convolve(columns, 0))
    outputs, grad_mixed = pl.pallas_call(
        dense_kernel,
        out_shape=(jax.ShapeDtypeStruct((cells, channels), BF16), square),
        compiler_params=SMALL,
    )(mixed_in.reshape(channels, cells), w_mix, grad_out.reshape(cells, channels))
    grad_in = exchange(convolve(exchange(grad_mixed), 1))
    grad_in = transposed(grad_in.reshape(channels, cells))
    return outputs.reshape(inputs.shape), grad_in.reshape(inputs.shape)


def solution(mesh):
    return jax.shard_map(
        body,
        mesh=mesh,
        in_specs=(
            P("lat", "lon", None),
            P(None, "lat", None, None),
            P("lat"),
            P(),
            P(),
            P("lat", "lon", None),
        ),
        out_specs=(P("lat", "lon", None), P("lat", "lon", None)),
        check_vma=False,
    )
```

```python
from functools import partial

import jax
import jax.numpy as jnp
from jax import lax
from jax.experimental import pallas as pl
from jax.experimental.pallas import tpu as pltpu
from jax.sharding import PartitionSpec as P

GROUP = 4
SMAX = 4


LANES = 128
BF16 = jnp.bfloat16
ALONG = (((1,), (1,)), ((), ()))
SMALL = pltpu.CompilerParams(vmem_limit_bytes=4 * 2**20)
LARGE = pltpu.CompilerParams(vmem_limit_bytes=12 * 2**20)


def width_bound(row, row_total):
    pole = min(row, row_total - 1 - row)
    return min(SMAX, max(1, 2 * SMAX // (pole + 1)) + 1)


def reaches(row_count, bands):
    total = row_count * bands
    bound = [width_bound(row, total) for row in range(total)]
    near = [max(bound[max(0, row - 1) : row + 2]) for row in range(total)]
    return bound, near


def iota(shape, axis):
    return lax.broadcasted_iota(jnp.int32, shape, axis)


def transpose_kernel(x_ref, o_ref):
    o_ref[...] = x_ref[...].T


def transposed(values):
    return pl.pallas_call(
        transpose_kernel,
        out_shape=jax.ShapeDtypeStruct(values.shape[::-1], values.dtype),
        compiler_params=SMALL,
    )(values)


def enter_kernel(lon_dev, w_ref, x_ref, p_ref, o_ref, f_ref):
    o_ref[...] = x_ref[...].T
    kernels, taps, rows, cells = p_ref.shape
    shape = (rows, LANES)
    line, lane = iota(shape, 0), iota(shape, 1)
    reach = jnp.zeros(shape, jnp.int32)
    for row in range(rows):
        reach = jnp.where(line == row, w_ref[row] * lon_dev, reach)
    scale = lax.rsqrt(3.0 * (2.0 * reach.astype(jnp.float32) + 1.0))
    for tile in range(3):
        offset = lane + (tile * LANES - SMAX * lon_dev)
        keep = jnp.where(jnp.abs(offset) <= reach, scale, 0.0)
        for k in range(kernels):
            for tap in range(taps):
                if tile < 2:
                    values = p_ref[k, tap, :, pl.ds(tile * LANES, LANES)]
                else:
                    values = p_ref[k, tap, :, pl.ds(cells - 1, 1)]
                    values = jnp.where(lane == 0, values, 0.0)
                f_ref[k, tap, :, pl.ds(tile * LANES, LANES)] = (
                    (values * keep).astype(BF16).astype(jnp.float32)
                )


def collect(bands, merged, backward, filter_refs, f):
    if merged:
        band = lax.axis_index("lat")
        f[band] = filter_refs[0][...]
        f[1 - band] = filter_refs[1][...]
    else:
        for segment, ref in enumerate(filter_refs):
            f[segment] = ref[...]
    if backward:
        segments, kernels, taps, lines, width = f.shape
        shape = (width, width)
        mirror = jnp.where(iota(shape, 0) + iota(shape, 1) == 2 * LANES, 1.0, 0.0).astype(BF16)
        for segment in range(segments):
            values = f[segment].reshape(kernels * taps * lines, width).astype(BF16)
            values = jnp.dot(values, mirror, preferred_element_type=jnp.float32)
            f[segment] = values.reshape(kernels, taps, lines, width)


def lay_toeplitz(rows, wide, lon_dev, merged, backward, f, t_ref, e_ref):
    segments, kernels, _, held, _ = f.shape
    shape = (lon_dev, LANES)
    lane, line = iota(shape, 1), iota(shape, 0)
    upper = lane >= line
    corner = lane == line
    for row in range(rows):
        for tap in range(3):
            source, column = (row + tap - 1, 2 - tap) if backward else (row, tap)
            source += 0 if merged else held
            segment, inner = divmod(source, held)
            present = 0 <= segment < segments
            for k in range(kernels):
                here = pl.ds(k * lon_dev, lon_dev)

                def turned(tile):
                    values = f[segment, k, column, pl.ds(inner, 1), pl.ds(tile * LANES, LANES)]
                    values = jnp.broadcast_to(values, shape)
                    return pltpu.roll(values, 0, 1, stride=1, stride_axis=0)

                if present:
                    first, second = turned(0), turned(1)
                    parts = [jnp.where(upper, first, 0.0), jnp.where(upper, second, first)]
                else:
                    parts = [jnp.zeros(shape, jnp.float32)] * 2
                for i, part in enumerate(parts):
                    t_ref[row, here, pl.ds((tap * 2 + i) * LANES, LANES)] = part.astype(BF16)
                if row in wide:
                    last = parts[0]
                    if present:
                        last = jnp.where(corner, turned(2), jnp.where(upper, 0.0, second))
                    at = pl.ds(tap * LANES, LANES)
                    e_ref[wide.index(row), here, at] = last.astype(BF16)


def mixer_of(everyone, share, backward, w_ref, height):
    kernels, group, channels = w_ref.shape
    first = lax.axis_index(everyone[0])
    for axis in everyone[1:]:
        first = first * lax.axis_size(axis) + lax.axis_index(axis)
    shape = (channels, height)
    chosen = iota(shape, 0) == first * share + iota(shape, 1) % share
    weights = jnp.concatenate([w_ref[k].astype(jnp.float32) for k in range(kernels)], axis=0)
    weights = jnp.dot(
        weights.astype(BF16),
        jnp.where(chosen, 1.0, 0.0).astype(BF16),
        preferred_element_type=jnp.float32,
    )
    if backward:
        spread = [
            jnp.concatenate([weights[k * group : (k + 1) * group]] * (height // group), axis=0)
            for k in range(kernels)
        ]
        spread = jnp.concatenate(spread, axis=1)
    else:
        shape = (kernels * group, kernels * height)
        line, lane = iota(shape, 0), iota(shape, 1)
        pick = line == (lane // height) * group + lane % group
        spread = lax.dot_general(
            weights.astype(BF16),
            jnp.where(pick, 1.0, 0.0).astype(BF16),
            (((0,), (0,)), ((), ())),
            preferred_element_type=jnp.float32,
        )
    shape = (height, kernels * height)
    same = iota(shape, 0) // group == (iota(shape, 1) % height) // group
    return jnp.where(same, spread, 0.0).astype(BF16)


def conv_kernel(
    table, bands, lon_dev, merged, everyone, share, backward, w_ref, own_ref, *refs
):
    count = 2 if merged else 3
    filter_refs, refs = refs[:count], refs[count:]
    *halo_refs, o_ref, f, t_ref, e_ref, xs, z_ref = refs
    segments, height, cells = own_ref.shape
    rows = len(table)
    held = rows // segments
    kernels = f.shape[1]
    wide = [row for row, reach in enumerate(table) if reach == SMAX]
    collect(bands, merged, backward, filter_refs, f)
    lay_toeplitz(rows, wide, lon_dev, merged, backward, f, t_ref, e_ref)

    def put(values, first):
        values = values.T
        count = values.shape[0] // lon_dev
        for shard in range(-SMAX, SMAX + 1):
            turned = pltpu.roll(values, -shard * share % height, 1) if shard else values
            at = pl.ds((shard + SMAX) * lon_dev, lon_dev)
            xs[pl.ds(first + 1, count), at, :] = turned.reshape(
                count, lon_dev, height
            )

    per_tile = LANES // lon_dev
    blank = jnp.zeros(xs.shape[1:], BF16)
    if halo_refs:
        band = lax.axis_index("lat")
        above = halo_refs[0][:, pl.ds(cells - LANES, LANES)]
        put(above, 0)
        edge = xs[per_tile].astype(jnp.float32)
        xs[0] = jnp.where(band > 0, edge, 0.0).astype(BF16)
        put(halo_refs[1][:, pl.ds(0, LANES)], 0)
        edge = xs[1].astype(jnp.float32)
        xs[rows + 1] = jnp.where(band < bands - 1, edge, 0.0).astype(BF16)
    else:
        xs[0] = blank
        xs[rows + 1] = blank
    for segment in range(segments):
        put(own_ref[segment], segment * held)
    span = 2 * LANES
    for row in range(rows):
        window = xs[row : row + 3, :span, :].reshape(3 * span, height)
        total = jnp.dot(t_ref[row], window, preferred_element_type=jnp.float32)
        if row in wide:
            beyond = []
            for tap in range(3):
                beyond += [xs[row + tap, span:, :], blank[: LANES - lon_dev]]
            total += jnp.dot(
                e_ref[wide.index(row)],
                jnp.concatenate(beyond, axis=0),
                preferred_element_type=jnp.float32,
            )
        total = total.astype(BF16)
        for k in range(kernels):
            z_ref[pl.ds(row * lon_dev, lon_dev), pl.ds(k * height, height)] = total[
                k * lon_dev : (k + 1) * lon_dev
            ]
    mixer = mixer_of(everyone, share, backward, w_ref, height)
    for segment in range(segments):
        part = z_ref[pl.ds(segment * cells, cells), :]
        mixed = lax.dot_general(mixer, part, ALONG, preferred_element_type=jnp.float32)
        o_ref[segment] = mixed.astype(o_ref.dtype)


def dense_kernel(m_ref, w_ref, g_ref, o_ref, d_ref):
    across = (((0,), (0,)), ((), ()))
    pre = lax.dot_general(m_ref[...], w_ref[...], across, preferred_element_type=jnp.float32)
    slope = 0.7978845608028654
    square = pre * pre
    bent = jnp.tanh(slope * (pre + 0.044715 * (square * pre)))
    half = 0.5 * (1.0 + bent)
    o_ref[...] = (pre * half).astype(o_ref.dtype)
    rise = half + 0.5 * pre * (1.0 - bent * bent) * (slope * (1.0 + 3.0 * 0.044715 * square))
    grad_pre = (g_ref[...].astype(jnp.float32) * rise).astype(BF16)
    d_ref[...] = lax.dot_general(
        w_ref[...], grad_pre, ALONG, preferred_element_type=jnp.float32
    ).astype(d_ref.dtype)


def from_bands(values):
    count = lax.axis_size("lat")
    up = [(i, i + 1) for i in range(count - 1)]
    down = [(j, i) for i, j in up]
    return [lax.ppermute(values, "lat", up), lax.ppermute(values, "lat", down)]


def body(inputs, psi_raw, widths, w_group, w_mix, grad_out):
    row_count, lon_dev, channels = inputs.shape
    kernels = psi_raw.shape[0]
    blocks, bands = lax.axis_size("lon"), lax.axis_size("lat")
    cells = row_count * lon_dev
    merged = bands == 2 and channels % (2 * GROUP * bands * blocks) == 0
    everyone = ("lat", "lon") if merged else ("lon",)
    segments = bands if merged else 1
    share = channels // (segments * blocks)
    height = blocks * share
    rows = segments * row_count
    tables = [
        tuple(max(table[row::rows]) for row in range(rows))
        for table in reaches(row_count, bands)
    ]
    square = jax.ShapeDtypeStruct((channels, cells), BF16)

    def exchange(values):
        parted = values.reshape(segments * blocks, share, cells)
        return lax.all_to_all(parted, everyone, 0, 0)

    turned, own_filters = pl.pallas_call(
        partial(enter_kernel, lon_dev),
        out_shape=(
            square,
            jax.ShapeDtypeStruct((kernels, 3, row_count, 3 * LANES), jnp.float32),
        ),
        in_specs=[
            pl.BlockSpec(memory_space=pltpu.SMEM),
            pl.BlockSpec(memory_space=pltpu.VMEM),
            pl.BlockSpec(memory_space=pltpu.VMEM),
        ],
    )(widths, inputs.reshape(cells, channels), psi_raw.transpose(0, 2, 1, 3))
    columns = exchange(turned)
    if merged:
        filters = [own_filters, lax.ppermute(own_filters, "lat", [(0, 1), (1, 0)])]
    else:
        above, below = from_bands(own_filters)
        filters = [above, own_filters, below]
    pool = (bands if merged else 3, *own_filters.shape)

    def convolve(values, backward):
        values = values.reshape(segments, height, cells)
        halo = [] if merged else from_bands(values[0])
        return pl.pallas_call(
            partial(
                conv_kernel, tables[backward], bands, lon_dev, merged, everyone, share,
                bool(backward),
            ),
            out_shape=jax.ShapeDtypeStruct(values.shape, BF16),
            scratch_shapes=[
                pltpu.VMEM(pool, jnp.float32),
                pltpu.VMEM((rows, kernels * lon_dev, 6 * LANES), BF16),
                pltpu.VMEM((tables[backward].count(SMAX), kernels * lon_dev, 3 * LANES), BF16),
                pltpu.VMEM((rows + 2, (2 * SMAX + 1) * lon_dev, height), BF16),
                pltpu.VMEM((rows * lon_dev, kernels * height), BF16),
            ],
            compiler_params=LARGE,
        )(w_group, values, *filters, *halo)

    mixed_in = exchange(convolve(columns, 0))
    outputs, grad_mixed = pl.pallas_call(
        dense_kernel,
        out_shape=(jax.ShapeDtypeStruct((cells, channels), BF16), square),
        compiler_params=SMALL,
    )(mixed_in.reshape(channels, cells), w_mix, grad_out.reshape(cells, channels))
    grad_in = exchange(convolve(exchange(grad_mixed), 1))
    grad_in = transposed(grad_in.reshape(channels, cells))
    return outputs.reshape(inputs.shape), grad_in.reshape(inputs.shape)


def solution(mesh):
    return jax.shard_map(
        body,
        mesh=mesh,
        in_specs=(
            P("lat", "lon", None),
            P(None, "lat", None, None),
            P("lat"),
            P(),
            P(),
            P("lat", "lon", None),
        ),
        out_specs=(P("lat", "lon", None), P("lat", "lon", None)),
        check_vma=False,
    )
```

```python
from functools import partial

import jax
import jax.numpy as jnp
from jax import lax
from jax.experimental import pallas as pl
from jax.experimental.pallas import tpu as pltpu
from jax.sharding import PartitionSpec as P

GROUP = 4
SMAX = 4


LANES = 128
BF16 = jnp.bfloat16
ALONG = (((1,), (1,)), ((), ()))
SMALL = pltpu.CompilerParams(vmem_limit_bytes=4 * 2**20)
LARGE = pltpu.CompilerParams(vmem_limit_bytes=12 * 2**20)


def width_bound(row, row_total):
    pole = min(row, row_total - 1 - row)
    return min(SMAX, max(1, 2 * SMAX // (pole + 1)) + 1)


def reaches(row_count, bands):
    total = row_count * bands
    bound = [width_bound(row, total) for row in range(total)]
    near = [max(bound[max(0, row - 1) : row + 2]) for row in range(total)]
    return bound, near


def iota(shape, axis):
    return lax.broadcasted_iota(jnp.int32, shape, axis)


def transpose_kernel(x_ref, o_ref):
    o_ref[...] = x_ref[...].T


def transposed(values):
    return pl.pallas_call(
        transpose_kernel,
        out_shape=jax.ShapeDtypeStruct(values.shape[::-1], values.dtype),
        compiler_params=SMALL,
    )(values)


def enter_kernel(lon_dev, w_ref, x_ref, p_ref, o_ref, f_ref):
    o_ref[...] = x_ref[...].T
    kernels, taps, rows, cells = p_ref.shape
    shape = (rows, LANES)
    line, lane = iota(shape, 0), iota(shape, 1)
    reach = jnp.zeros(shape, jnp.int32)
    for row in range(rows):
        reach = jnp.where(line == row, w_ref[row] * lon_dev, reach)
    scale = lax.rsqrt(3.0 * (2.0 * reach.astype(jnp.float32) + 1.0))
    for tile in range(3):
        offset = lane + (tile * LANES - SMAX * lon_dev)
        keep = jnp.where(jnp.abs(offset) <= reach, scale, 0.0)
        for k in range(kernels):
            for tap in range(taps):
                if tile < 2:
                    values = p_ref[k, tap, :, pl.ds(tile * LANES, LANES)]
                else:
                    values = p_ref[k, tap, :, pl.ds(cells - 1, 1)]
                    values = jnp.where(lane == 0, values, 0.0)
                f_ref[k, tap, :, pl.ds(tile * LANES, LANES)] = (
                    (values * keep).astype(BF16).astype(jnp.float32)
                )


def collect(bands, merged, backward, filter_refs, f):
    if merged:
        band = lax.axis_index("lat")
        f[band] = filter_refs[0][...]
        f[1 - band] = filter_refs[1][...]
    else:
        for segment, ref in enumerate(filter_refs):
            f[segment] = ref[...]
    if backward:
        segments, kernels, taps, lines, width = f.shape
        shape = (width, width)
        mirror = jnp.where(iota(shape, 0) + iota(shape, 1) == 2 * LANES, 1.0, 0.0).astype(BF16)
        for segment in range(segments):
            values = f[segment].reshape(kernels * taps * lines, width).astype(BF16)
            values = jnp.dot(values, mirror, preferred_element_type=jnp.float32)
            f[segment] = values.reshape(kernels, taps, lines, width)


def lay_toeplitz(rows, wide, lon_dev, merged, backward, f, t_ref, e_ref=None):
    segments, kernels, _, held, _ = f.shape
    shape = (lon_dev, LANES)
    lane, line = iota(shape, 1), iota(shape, 0)
    upper = lane >= line
    corner = lane == line
    for place, row in enumerate(rows):
        for tap in range(3):
            source, column = (row + tap - 1, 2 - tap) if backward else (row, tap)
            source += 0 if merged else held
            segment, inner = divmod(source, held)
            present = 0 <= segment < segments
            for k in range(kernels):
                here = pl.ds(k * lon_dev, lon_dev)

                def turned(tile):
                    values = f[segment, k, column, pl.ds(inner, 1), pl.ds(tile * LANES, LANES)]
                    values = jnp.broadcast_to(values, shape)
                    return pltpu.roll(values, 0, 1, stride=1, stride_axis=0)

                if present:
                    first, second = turned(0), turned(1)
                    parts = [jnp.where(upper, first, 0.0), jnp.where(upper, second, first)]
                else:
                    parts = [jnp.zeros(shape, jnp.float32)] * 2
                for i, part in enumerate(parts):
                    t_ref[place, here, pl.ds((tap * 2 + i) * LANES, LANES)] = part.astype(BF16)
                if e_ref is not None and row in wide:
                    last = parts[0]
                    if present:
                        last = jnp.where(corner, turned(2), jnp.where(upper, 0.0, second))
                    at = pl.ds(tap * LANES, LANES)
                    e_ref[wide.index(row), here, at] = last.astype(BF16)


def mixer_of(everyone, share, backward, w_ref, height):
    kernels, group, channels = w_ref.shape
    first = lax.axis_index(everyone[0])
    for axis in everyone[1:]:
        first = first * lax.axis_size(axis) + lax.axis_index(axis)
    shape = (channels, height)
    chosen = iota(shape, 0) == first * share + iota(shape, 1) % share
    weights = jnp.concatenate([w_ref[k].astype(jnp.float32) for k in range(kernels)], axis=0)
    weights = jnp.dot(
        weights.astype(BF16),
        jnp.where(chosen, 1.0, 0.0).astype(BF16),
        preferred_element_type=jnp.float32,
    )
    if backward:
        spread = [
            jnp.concatenate([weights[k * group : (k + 1) * group]] * (height // group), axis=0)
            for k in range(kernels)
        ]
        spread = jnp.concatenate(spread, axis=1)
    else:
        shape = (kernels * group, kernels * height)
        line, lane = iota(shape, 0), iota(shape, 1)
        pick = line == (lane // height) * group + lane % group
        spread = lax.dot_general(
            weights.astype(BF16),
            jnp.where(pick, 1.0, 0.0).astype(BF16),
            (((0,), (0,)), ((), ())),
            preferred_element_type=jnp.float32,
        )
    shape = (height, kernels * height)
    same = iota(shape, 0) // group == (iota(shape, 1) % height) // group
    return jnp.where(same, spread, 0.0).astype(BF16)


def rows_ahead(rows, wide):
    ahead = [row for row in range(rows // 4, rows - rows // 4) if row not in wide]
    return ahead, [row for row in range(rows) if row not in ahead]


def table_kernel(wide, rows, bands, lon_dev, merged, backward, *refs):
    *filter_refs, t_ref, f = refs
    collect(bands, merged, backward, filter_refs, f)
    lay_toeplitz(rows_ahead(rows, wide)[0], wide, lon_dev, merged, backward, f, t_ref)


def conv_kernel(
    table, bands, lon_dev, merged, everyone, share, backward, w_ref, own_ref, ahead_ref, *refs
):
    count = 2 if merged else 3
    filter_refs, refs = refs[:count], refs[count:]
    *halo_refs, o_ref, f, t_ref, e_ref, xs, z_ref = refs
    segments, height, cells = own_ref.shape
    rows = len(table)
    held = rows // segments
    kernels = f.shape[1]
    wide = [row for row, reach in enumerate(table) if reach == SMAX]
    ahead, others = rows_ahead(rows, wide)
    collect(bands, merged, backward, filter_refs, f)
    lay_toeplitz(others, wide, lon_dev, merged, backward, f, t_ref, e_ref)

    def put(values, first):
        values = values.T
        count = values.shape[0] // lon_dev
        for shard in range(-SMAX, SMAX + 1):
            turned = pltpu.roll(values, -shard * share % height, 1) if shard else values
            at = pl.ds((shard + SMAX) * lon_dev, lon_dev)
            xs[pl.ds(first + 1, count), at, :] = turned.reshape(
                count, lon_dev, height
            )

    per_tile = LANES // lon_dev
    blank = jnp.zeros(xs.shape[1:], BF16)
    if halo_refs:
        band = lax.axis_index("lat")
        above = halo_refs[0][:, pl.ds(cells - LANES, LANES)]
        put(above, 0)
        edge = xs[per_tile].astype(jnp.float32)
        xs[0] = jnp.where(band > 0, edge, 0.0).astype(BF16)
        put(halo_refs[1][:, pl.ds(0, LANES)], 0)
        edge = xs[1].astype(jnp.float32)
        xs[rows + 1] = jnp.where(band < bands - 1, edge, 0.0).astype(BF16)
    else:
        xs[0] = blank
        xs[rows + 1] = blank
    for segment in range(segments):
        put(own_ref[segment], segment * held)
    span = 2 * LANES
    for row in range(rows):
        window = xs[row : row + 3, :span, :].reshape(3 * span, height)
        laid = ahead_ref[ahead.index(row)] if row in ahead else t_ref[others.index(row)]
        total = jnp.dot(laid, window, preferred_element_type=jnp.float32)
        if row in wide:
            beyond = []
            for tap in range(3):
                beyond += [xs[row + tap, span:, :], blank[: LANES - lon_dev]]
            total += jnp.dot(
                e_ref[wide.index(row)],
                jnp.concatenate(beyond, axis=0),
                preferred_element_type=jnp.float32,
            )
        total = total.astype(BF16)
        for k in range(kernels):
            z_ref[pl.ds(row * lon_dev, lon_dev), pl.ds(k * height, height)] = total[
                k * lon_dev : (k + 1) * lon_dev
            ]
    mixer = mixer_of(everyone, share, backward, w_ref, height)
    for segment in range(segments):
        part = z_ref[pl.ds(segment * cells, cells), :]
        mixed = lax.dot_general(mixer, part, ALONG, preferred_element_type=jnp.float32)
        o_ref[segment] = mixed.astype(o_ref.dtype)


def dense_kernel(m_ref, w_ref, g_ref, o_ref, d_ref):
    across = (((0,), (0,)), ((), ()))
    pre = lax.dot_general(m_ref[...], w_ref[...], across, preferred_element_type=jnp.float32)
    slope = 0.7978845608028654
    square = pre * pre
    bent = jnp.tanh(slope * (pre + 0.044715 * (square * pre)))
    half = 0.5 * (1.0 + bent)
    o_ref[...] = (pre * half).astype(o_ref.dtype)
    rise = half + 0.5 * pre * (1.0 - bent * bent) * (slope * (1.0 + 3.0 * 0.044715 * square))
    grad_pre = (g_ref[...].astype(jnp.float32) * rise).astype(BF16)
    d_ref[...] = lax.dot_general(
        w_ref[...], grad_pre, ALONG, preferred_element_type=jnp.float32
    ).astype(d_ref.dtype)


def from_bands(values):
    count = lax.axis_size("lat")
    up = [(i, i + 1) for i in range(count - 1)]
    down = [(j, i) for i, j in up]
    return [lax.ppermute(values, "lat", up), lax.ppermute(values, "lat", down)]


def body(inputs, psi_raw, widths, w_group, w_mix, grad_out):
    row_count, lon_dev, channels = inputs.shape
    kernels = psi_raw.shape[0]
    blocks, bands = lax.axis_size("lon"), lax.axis_size("lat")
    cells = row_count * lon_dev
    merged = bands == 2 and channels % (2 * GROUP * bands * blocks) == 0
    everyone = ("lat", "lon") if merged else ("lon",)
    segments = bands if merged else 1
    share = channels // (segments * blocks)
    height = blocks * share
    rows = segments * row_count
    tables = [
        tuple(max(table[row::rows]) for row in range(rows))
        for table in reaches(row_count, bands)
    ]
    square = jax.ShapeDtypeStruct((channels, cells), BF16)

    def exchange(values):
        parted = values.reshape(segments * blocks, share, cells)
        return lax.all_to_all(parted, everyone, 0, 0)

    turned, own_filters = pl.pallas_call(
        partial(enter_kernel, lon_dev),
        out_shape=(
            square,
            jax.ShapeDtypeStruct((kernels, 3, row_count, 3 * LANES), jnp.float32),
        ),
        in_specs=[
            pl.BlockSpec(memory_space=pltpu.SMEM),
            pl.BlockSpec(memory_space=pltpu.VMEM),
            pl.BlockSpec(memory_space=pltpu.VMEM),
        ],
    )(widths, inputs.reshape(cells, channels), psi_raw.transpose(0, 2, 1, 3))
    columns = exchange(turned)
    if merged:
        filters = [own_filters, lax.ppermute(own_filters, "lat", [(0, 1), (1, 0)])]
    else:
        above, below = from_bands(own_filters)
        filters = [above, own_filters, below]
    pool = (bands if merged else 3, *own_filters.shape)

    def lay(filters, backward):
        wide = [row for row in range(rows) if tables[backward][row] == SMAX]
        shape = (len(rows_ahead(rows, wide)[0]), kernels * lon_dev, 6 * LANES)
        return pl.pallas_call(
            partial(table_kernel, wide, rows, bands, lon_dev, merged, bool(backward)),
            out_shape=jax.ShapeDtypeStruct(shape, BF16),
            scratch_shapes=[pltpu.VMEM(pool, jnp.float32)],
            compiler_params=SMALL,
        )(*filters)

    def convolve(values, laid, backward):
        values = values.reshape(segments, height, cells)
        halo = [] if merged else from_bands(values[0])
        return pl.pallas_call(
            partial(
                conv_kernel, tables[backward], bands, lon_dev, merged, everyone, share,
                bool(backward),
            ),
            out_shape=jax.ShapeDtypeStruct(values.shape, BF16),
            scratch_shapes=[
                pltpu.VMEM(pool, jnp.float32),
                pltpu.VMEM((rows - laid.shape[0], kernels * lon_dev, 6 * LANES), BF16),
                pltpu.VMEM((tables[backward].count(SMAX), kernels * lon_dev, 3 * LANES), BF16),
                pltpu.VMEM((rows + 2, (2 * SMAX + 1) * lon_dev, height), BF16),
                pltpu.VMEM((rows * lon_dev, kernels * height), BF16),
            ],
            compiler_params=LARGE,
        )(w_group, values, laid, *filters, *halo)

    mixed_in = convolve(columns, lay(filters, 0), 0)
    mixed_in, later = lax.optimization_barrier((mixed_in, filters))
    mixed_in = exchange(mixed_in)
    outputs, grad_mixed = pl.pallas_call(
        dense_kernel,
        out_shape=(jax.ShapeDtypeStruct((cells, channels), BF16), square),
        compiler_params=SMALL,
    )(mixed_in.reshape(channels, cells), w_mix, grad_out.reshape(cells, channels))
    grad_in = exchange(convolve(exchange(grad_mixed), lay(later, 1), 1))
    grad_in = transposed(grad_in.reshape(channels, cells))
    return outputs.reshape(inputs.shape), grad_in.reshape(inputs.shape)


def solution(mesh):
    return jax.shard_map(
        body,
        mesh=mesh,
        in_specs=(
            P("lat", "lon", None),
            P(None, "lat", None, None),
            P("lat"),
            P(),
            P(),
            P("lat", "lon", None),
        ),
        out_specs=(P("lat", "lon", None), P("lat", "lon", None)),
        check_vma=False,
    )
```

```python
from functools import partial

import jax
import jax.numpy as jnp
from jax import lax
from jax.experimental import pallas as pl
from jax.experimental.pallas import tpu as pltpu
from jax.sharding import PartitionSpec as P

GROUP = 4
SMAX = 4


LANES = 128
BF16 = jnp.bfloat16
ALONG = (((1,), (1,)), ((), ()))
SMALL = pltpu.CompilerParams(vmem_limit_bytes=4 * 2**20)
LARGE = pltpu.CompilerParams(vmem_limit_bytes=12 * 2**20)


def width_bound(row, row_total):
    pole = min(row, row_total - 1 - row)
    return min(SMAX, max(1, 2 * SMAX // (pole + 1)) + 1)


def reaches(row_count, bands):
    total = row_count * bands
    bound = [width_bound(row, total) for row in range(total)]
    near = [max(bound[max(0, row - 1) : row + 2]) for row in range(total)]
    return bound, near


def iota(shape, axis):
    return lax.broadcasted_iota(jnp.int32, shape, axis)


def transpose_kernel(x_ref, o_ref):
    o_ref[...] = x_ref[...].T


def transposed(values):
    return pl.pallas_call(
        transpose_kernel,
        out_shape=jax.ShapeDtypeStruct(values.shape[::-1], values.dtype),
        compiler_params=SMALL,
    )(values)


def enter_kernel(lon_dev, w_ref, x_ref, p_ref, o_ref, f_ref):
    o_ref[...] = x_ref[...].T
    kernels, taps, rows, cells = p_ref.shape
    shape = (rows, LANES)
    line, lane = iota(shape, 0), iota(shape, 1)
    reach = jnp.zeros(shape, jnp.int32)
    for row in range(rows):
        reach = jnp.where(line == row, w_ref[row] * lon_dev, reach)
    scale = lax.rsqrt(3.0 * (2.0 * reach.astype(jnp.float32) + 1.0))
    for tile in range(3):
        offset = lane + (tile * LANES - SMAX * lon_dev)
        keep = jnp.where(jnp.abs(offset) <= reach, scale, 0.0)
        for k in range(kernels):
            for tap in range(taps):
                if tile < 2:
                    values = p_ref[k, tap, :, pl.ds(tile * LANES, LANES)]
                else:
                    values = p_ref[k, tap, :, pl.ds(cells - 1, 1)]
                    values = jnp.where(lane == 0, values, 0.0)
                f_ref[k, tap, :, pl.ds(tile * LANES, LANES)] = (
                    (values * keep).astype(BF16).astype(jnp.float32)
                )


def collect(bands, merged, backward, filter_refs, f):
    if merged:
        band = lax.axis_index("lat")
        f[band] = filter_refs[0][...]
        f[1 - band] = filter_refs[1][...]
    else:
        for segment, ref in enumerate(filter_refs):
            f[segment] = ref[...]
    if backward:
        segments, kernels, taps, lines, width = f.shape
        shape = (width, width)
        mirror = jnp.where(iota(shape, 0) + iota(shape, 1) == 2 * LANES, 1.0, 0.0).astype(BF16)
        for segment in range(segments):
            values = f[segment].reshape(kernels * taps * lines, width).astype(BF16)
            values = jnp.dot(values, mirror, preferred_element_type=jnp.float32)
            f[segment] = values.reshape(kernels, taps, lines, width)


def lay_toeplitz(rows, wide, lon_dev, merged, backward, f, t_ref, e_ref=None):
    segments, kernels, _, held, _ = f.shape
    shape = (lon_dev, LANES)
    lane, line = iota(shape, 1), iota(shape, 0)
    upper = lane >= line
    corner = lane == line
    for place, row in enumerate(rows):
        for tap in range(3):
            source, column = (row + tap - 1, 2 - tap) if backward else (row, tap)
            source += 0 if merged else held
            segment, inner = divmod(source, held)
            present = 0 <= segment < segments
            for k in range(kernels):
                here = pl.ds(k * lon_dev, lon_dev)

                def turned(tile):
                    values = f[segment, k, column, pl.ds(inner, 1), pl.ds(tile * LANES, LANES)]
                    values = jnp.broadcast_to(values, shape)
                    return pltpu.roll(values, 0, 1, stride=1, stride_axis=0)

                if present:
                    first, second = turned(0), turned(1)
                    parts = [jnp.where(upper, first, 0.0), jnp.where(upper, second, first)]
                else:
                    parts = [jnp.zeros(shape, jnp.float32)] * 2
                for i, part in enumerate(parts):
                    t_ref[place, here, pl.ds((tap * 2 + i) * LANES, LANES)] = part.astype(BF16)
                if e_ref is not None and row in wide:
                    last = parts[0]
                    if present:
                        last = jnp.where(corner, turned(2), jnp.where(upper, 0.0, second))
                    at = pl.ds(tap * LANES, LANES)
                    e_ref[wide.index(row), here, at] = last.astype(BF16)


def mixer_of(everyone, share, backward, w_ref, height):
    kernels, group, channels = w_ref.shape
    first = lax.axis_index(everyone[0])
    for axis in everyone[1:]:
        first = first * lax.axis_size(axis) + lax.axis_index(axis)
    shape = (channels, height)
    chosen = iota(shape, 0) == first * share + iota(shape, 1) % share
    weights = jnp.concatenate([w_ref[k].astype(jnp.float32) for k in range(kernels)], axis=0)
    weights = jnp.dot(
        weights.astype(BF16),
        jnp.where(chosen, 1.0, 0.0).astype(BF16),
        preferred_element_type=jnp.float32,
    )
    if backward:
        spread = [
            jnp.concatenate([weights[k * group : (k + 1) * group]] * (height // group), axis=0)
            for k in range(kernels)
        ]
        spread = jnp.concatenate(spread, axis=1)
    else:
        shape = (kernels * group, kernels * height)
        line, lane = iota(shape, 0), iota(shape, 1)
        pick = line == (lane // height) * group + lane % group
        spread = lax.dot_general(
            weights.astype(BF16),
            jnp.where(pick, 1.0, 0.0).astype(BF16),
            (((0,), (0,)), ((), ())),
            preferred_element_type=jnp.float32,
        )
    shape = (height, kernels * height)
    same = iota(shape, 0) // group == (iota(shape, 1) % height) // group
    return jnp.where(same, spread, 0.0).astype(BF16)


def rows_ahead(rows, wide):
    ahead = [row for row in range(rows // 4, rows - rows // 4) if row not in wide]
    return ahead, [row for row in range(rows) if row not in ahead]


def table_kernel(wides, rows, bands, lon_dev, merged, *refs):
    *filter_refs, forward_ref, backward_ref, f = refs
    for backward, t_ref in enumerate((forward_ref, backward_ref)):
        wide = wides[backward]
        collect(bands, merged, bool(backward), filter_refs, f)
        lay_toeplitz(rows_ahead(rows, wide)[0], wide, lon_dev, merged, bool(backward), f, t_ref)


def conv_kernel(
    table, bands, lon_dev, merged, everyone, share, backward, w_ref, own_ref, ahead_ref, *refs
):
    count = 2 if merged else 3
    filter_refs, refs = refs[:count], refs[count:]
    *halo_refs, o_ref, f, t_ref, e_ref, xs, z_ref = refs
    segments, height, cells = own_ref.shape
    rows = len(table)
    held = rows // segments
    kernels = f.shape[1]
    wide = [row for row, reach in enumerate(table) if reach == SMAX]
    ahead, others = rows_ahead(rows, wide)
    collect(bands, merged, backward, filter_refs, f)
    lay_toeplitz(others, wide, lon_dev, merged, backward, f, t_ref, e_ref)

    def put(values, first):
        values = values.T
        count = values.shape[0] // lon_dev
        for shard in range(-SMAX, SMAX + 1):
            turned = pltpu.roll(values, -shard * share % height, 1) if shard else values
            at = pl.ds((shard + SMAX) * lon_dev, lon_dev)
            xs[pl.ds(first + 1, count), at, :] = turned.reshape(
                count, lon_dev, height
            )

    per_tile = LANES // lon_dev
    blank = jnp.zeros(xs.shape[1:], BF16)
    if halo_refs:
        band = lax.axis_index("lat")
        above = halo_refs[0][:, pl.ds(cells - LANES, LANES)]
        put(above, 0)
        edge = xs[per_tile].astype(jnp.float32)
        xs[0] = jnp.where(band > 0, edge, 0.0).astype(BF16)
        put(halo_refs[1][:, pl.ds(0, LANES)], 0)
        edge = xs[1].astype(jnp.float32)
        xs[rows + 1] = jnp.where(band < bands - 1, edge, 0.0).astype(BF16)
    else:
        xs[0] = blank
        xs[rows + 1] = blank
    for segment in range(segments):
        put(own_ref[segment], segment * held)
    span = 2 * LANES
    for row in range(rows):
        window = xs[row : row + 3, :span, :].reshape(3 * span, height)
        laid = ahead_ref[ahead.index(row)] if row in ahead else t_ref[others.index(row)]
        total = jnp.dot(laid, window, preferred_element_type=jnp.float32)
        if row in wide:
            beyond = []
            for tap in range(3):
                beyond += [xs[row + tap, span:, :], blank[: LANES - lon_dev]]
            total += jnp.dot(
                e_ref[wide.index(row)],
                jnp.concatenate(beyond, axis=0),
                preferred_element_type=jnp.float32,
            )
        total = total.astype(BF16)
        for k in range(kernels):
            z_ref[pl.ds(row * lon_dev, lon_dev), pl.ds(k * height, height)] = total[
                k * lon_dev : (k + 1) * lon_dev
            ]
    mixer = mixer_of(everyone, share, backward, w_ref, height)
    for segment in range(segments):
        part = z_ref[pl.ds(segment * cells, cells), :]
        mixed = lax.dot_general(mixer, part, ALONG, preferred_element_type=jnp.float32)
        o_ref[segment] = mixed.astype(o_ref.dtype)


def dense_kernel(m_ref, w_ref, g_ref, o_ref, d_ref):
    across = (((0,), (0,)), ((), ()))
    pre = lax.dot_general(m_ref[...], w_ref[...], across, preferred_element_type=jnp.float32)
    slope = 0.7978845608028654
    square = pre * pre
    bent = jnp.tanh(slope * (pre + 0.044715 * (square * pre)))
    half = 0.5 * (1.0 + bent)
    o_ref[...] = (pre * half).astype(o_ref.dtype)
    rise = half + 0.5 * pre * (1.0 - bent * bent) * (slope * (1.0 + 3.0 * 0.044715 * square))
    grad_pre = (g_ref[...].astype(jnp.float32) * rise).astype(BF16)
    d_ref[...] = lax.dot_general(
        w_ref[...], grad_pre, ALONG, preferred_element_type=jnp.float32
    ).astype(d_ref.dtype)


def from_bands(values):
    count = lax.axis_size("lat")
    up = [(i, i + 1) for i in range(count - 1)]
    down = [(j, i) for i, j in up]
    return [lax.ppermute(values, "lat", up), lax.ppermute(values, "lat", down)]


def body(inputs, psi_raw, widths, w_group, w_mix, grad_out):
    row_count, lon_dev, channels = inputs.shape
    kernels = psi_raw.shape[0]
    blocks, bands = lax.axis_size("lon"), lax.axis_size("lat")
    cells = row_count * lon_dev
    merged = bands == 2 and channels % (2 * GROUP * bands * blocks) == 0
    everyone = ("lat", "lon") if merged else ("lon",)
    segments = bands if merged else 1
    share = channels // (segments * blocks)
    height = blocks * share
    rows = segments * row_count
    tables = [
        tuple(max(table[row::rows]) for row in range(rows))
        for table in reaches(row_count, bands)
    ]
    square = jax.ShapeDtypeStruct((channels, cells), BF16)

    def exchange(values):
        parted = values.reshape(segments * blocks, share, cells)
        return lax.all_to_all(parted, everyone, 0, 0)

    turned, own_filters = pl.pallas_call(
        partial(enter_kernel, lon_dev),
        out_shape=(
            square,
            jax.ShapeDtypeStruct((kernels, 3, row_count, 3 * LANES), jnp.float32),
        ),
        in_specs=[
            pl.BlockSpec(memory_space=pltpu.SMEM),
            pl.BlockSpec(memory_space=pltpu.VMEM),
            pl.BlockSpec(memory_space=pltpu.VMEM),
        ],
    )(widths, inputs.reshape(cells, channels), psi_raw.transpose(0, 2, 1, 3))
    columns = exchange(turned)
    if merged:
        filters = [own_filters, lax.ppermute(own_filters, "lat", [(0, 1), (1, 0)])]
    else:
        above, below = from_bands(own_filters)
        filters = [above, own_filters, below]
    pool = (bands if merged else 3, *own_filters.shape)

    wides = [[row for row in range(rows) if table[row] == SMAX] for table in tables]
    laid = pl.pallas_call(
        partial(table_kernel, wides, rows, bands, lon_dev, merged),
        out_shape=[
            jax.ShapeDtypeStruct(
                (len(rows_ahead(rows, wide)[0]), kernels * lon_dev, 6 * LANES), BF16
            )
            for wide in wides
        ],
        scratch_shapes=[pltpu.VMEM(pool, jnp.float32)],
        compiler_params=SMALL,
    )(*filters)

    def convolve(values, laid, backward):
        values = values.reshape(segments, height, cells)
        halo = [] if merged else from_bands(values[0])
        return pl.pallas_call(
            partial(
                conv_kernel, tables[backward], bands, lon_dev, merged, everyone, share,
                bool(backward),
            ),
            out_shape=jax.ShapeDtypeStruct(values.shape, BF16),
            scratch_shapes=[
                pltpu.VMEM(pool, jnp.float32),
                pltpu.VMEM((rows - laid.shape[0], kernels * lon_dev, 6 * LANES), BF16),
                pltpu.VMEM((tables[backward].count(SMAX), kernels * lon_dev, 3 * LANES), BF16),
                pltpu.VMEM((rows + 2, (2 * SMAX + 1) * lon_dev, height), BF16),
                pltpu.VMEM((rows * lon_dev, kernels * height), BF16),
            ],
            compiler_params=LARGE,
        )(w_group, values, laid, *filters, *halo)

    mixed_in = exchange(convolve(columns, laid[0], 0))
    outputs, grad_mixed = pl.pallas_call(
        dense_kernel,
        out_shape=(jax.ShapeDtypeStruct((cells, channels), BF16), square),
        compiler_params=SMALL,
    )(mixed_in.reshape(channels, cells), w_mix, grad_out.reshape(cells, channels))
    grad_in = exchange(convolve(exchange(grad_mixed), laid[1], 1))
    grad_in = transposed(grad_in.reshape(channels, cells))
    return outputs.reshape(inputs.shape), grad_in.reshape(inputs.shape)


def solution(mesh):
    return jax.shard_map(
        body,
        mesh=mesh,
        in_specs=(
            P("lat", "lon", None),
            P(None, "lat", None, None),
            P("lat"),
            P(),
            P(),
            P("lat", "lon", None),
        ),
        out_specs=(P("lat", "lon", None), P("lat", "lon", None)),
        check_vma=False,
    )
```

```python
from functools import partial

import jax
import jax.numpy as jnp
from jax import lax
from jax.experimental import pallas as pl
from jax.experimental.pallas import tpu as pltpu
from jax.sharding import PartitionSpec as P

GROUP = 4
SMAX = 4


LANES = 128
BF16 = jnp.bfloat16
ALONG = (((1,), (1,)), ((), ()))
SMALL = pltpu.CompilerParams(vmem_limit_bytes=4 * 2**20)
LARGE = pltpu.CompilerParams(vmem_limit_bytes=12 * 2**20)


def width_bound(row, row_total):
    pole = min(row, row_total - 1 - row)
    return min(SMAX, max(1, 2 * SMAX // (pole + 1)) + 1)


def reaches(row_count, bands):
    total = row_count * bands
    bound = [width_bound(row, total) for row in range(total)]
    near = [max(bound[max(0, row - 1) : row + 2]) for row in range(total)]
    return bound, near


def iota(shape, axis):
    return lax.broadcasted_iota(jnp.int32, shape, axis)


def transpose_kernel(x_ref, o_ref):
    o_ref[...] = x_ref[...].T


def transposed(values):
    return pl.pallas_call(
        transpose_kernel,
        out_shape=jax.ShapeDtypeStruct(values.shape[::-1], values.dtype),
        compiler_params=SMALL,
    )(values)


def enter_kernel(lon_dev, w_ref, x_ref, p_ref, o_ref, f_ref):
    o_ref[...] = x_ref[...].T
    kernels, taps, rows, cells = p_ref.shape
    shape = (rows, LANES)
    line, lane = iota(shape, 0), iota(shape, 1)
    reach = jnp.zeros(shape, jnp.int32)
    for row in range(rows):
        reach = jnp.where(line == row, w_ref[row] * lon_dev, reach)
    scale = lax.rsqrt(3.0 * (2.0 * reach.astype(jnp.float32) + 1.0))
    for tile in range(3):
        offset = lane + (tile * LANES - SMAX * lon_dev)
        keep = jnp.where(jnp.abs(offset) <= reach, scale, 0.0)
        for k in range(kernels):
            for tap in range(taps):
                if tile < 2:
                    values = p_ref[k, tap, :, pl.ds(tile * LANES, LANES)]
                else:
                    values = p_ref[k, tap, :, pl.ds(cells - 1, 1)]
                    values = jnp.where(lane == 0, values, 0.0)
                f_ref[k, tap, :, pl.ds(tile * LANES, LANES)] = (
                    (values * keep).astype(BF16).astype(jnp.float32)
                )


def collect(bands, merged, backward, filter_refs, f):
    if merged:
        band = lax.axis_index("lat")
        f[band] = filter_refs[0][...]
        f[1 - band] = filter_refs[1][...]
    else:
        for segment, ref in enumerate(filter_refs):
            f[segment] = ref[...]
    if backward:
        segments, kernels, taps, lines, width = f.shape
        shape = (width, width)
        mirror = jnp.where(iota(shape, 0) + iota(shape, 1) == 2 * LANES, 1.0, 0.0).astype(BF16)
        for segment in range(segments):
            values = f[segment].reshape(kernels * taps * lines, width).astype(BF16)
            values = jnp.dot(values, mirror, preferred_element_type=jnp.float32)
            f[segment] = values.reshape(kernels, taps, lines, width)


def lay_toeplitz(rows, wide, lon_dev, merged, backward, f, t_ref, e_ref=None):
    segments, kernels, _, held, _ = f.shape
    shape = (lon_dev, LANES)
    lane, line = iota(shape, 1), iota(shape, 0)
    upper = lane >= line
    corner = lane == line
    for place, row in enumerate(rows):
        for tap in range(3):
            source, column = (row + tap - 1, 2 - tap) if backward else (row, tap)
            source += 0 if merged else held
            segment, inner = divmod(source, held)
            present = 0 <= segment < segments
            for k in range(kernels):
                here = pl.ds(k * lon_dev, lon_dev)

                def turned(tile):
                    values = f[segment, k, column, pl.ds(inner, 1), pl.ds(tile * LANES, LANES)]
                    values = jnp.broadcast_to(values, shape)
                    return pltpu.roll(values, 0, 1, stride=1, stride_axis=0)

                if present:
                    first, second = turned(0), turned(1)
                    parts = [jnp.where(upper, first, 0.0), jnp.where(upper, second, first)]
                else:
                    parts = [jnp.zeros(shape, jnp.float32)] * 2
                for i, part in enumerate(parts):
                    t_ref[place, here, pl.ds((tap * 2 + i) * LANES, LANES)] = part.astype(BF16)
                if e_ref is not None and row in wide:
                    last = parts[0]
                    if present:
                        last = jnp.where(corner, turned(2), jnp.where(upper, 0.0, second))
                    at = pl.ds(tap * LANES, LANES)
                    e_ref[wide.index(row), here, at] = last.astype(BF16)


def mixer_of(everyone, share, backward, w_ref, height):
    kernels, group, channels = w_ref.shape
    first = lax.axis_index(everyone[0])
    for axis in everyone[1:]:
        first = first * lax.axis_size(axis) + lax.axis_index(axis)
    shape = (channels, height)
    chosen = iota(shape, 0) == first * share + iota(shape, 1) % share
    weights = jnp.concatenate([w_ref[k].astype(jnp.float32) for k in range(kernels)], axis=0)
    weights = jnp.dot(
        weights.astype(BF16),
        jnp.where(chosen, 1.0, 0.0).astype(BF16),
        preferred_element_type=jnp.float32,
    )
    if backward:
        spread = [
            jnp.concatenate([weights[k * group : (k + 1) * group]] * (height // group), axis=0)
            for k in range(kernels)
        ]
        spread = jnp.concatenate(spread, axis=1)
    else:
        shape = (kernels * group, kernels * height)
        line, lane = iota(shape, 0), iota(shape, 1)
        pick = line == (lane // height) * group + lane % group
        spread = lax.dot_general(
            weights.astype(BF16),
            jnp.where(pick, 1.0, 0.0).astype(BF16),
            (((0,), (0,)), ((), ())),
            preferred_element_type=jnp.float32,
        )
    shape = (height, kernels * height)
    same = iota(shape, 0) // group == (iota(shape, 1) % height) // group
    return jnp.where(same, spread, 0.0).astype(BF16)


def rows_ahead(rows, wide, backward):
    middle = () if backward else range(rows // 4, rows - rows // 4)
    ahead = [row for row in middle if row not in wide]
    return ahead, [row for row in range(rows) if row not in ahead]


def table_kernel(wide, rows, bands, lon_dev, merged, *refs):
    *filter_refs, t_ref, f = refs
    collect(bands, merged, False, filter_refs, f)
    lay_toeplitz(rows_ahead(rows, wide, False)[0], wide, lon_dev, merged, False, f, t_ref)


def conv_kernel(
    table, bands, lon_dev, merged, everyone, share, backward, w_ref, own_ref, *refs
):
    if not backward:
        ahead_ref, *refs = refs
    count = 2 if merged else 3
    filter_refs, refs = refs[:count], refs[count:]
    *halo_refs, o_ref, f, t_ref, e_ref, xs, z_ref = refs
    segments, height, cells = own_ref.shape
    rows = len(table)
    held = rows // segments
    kernels = f.shape[1]
    wide = [row for row, reach in enumerate(table) if reach == SMAX]
    ahead, others = rows_ahead(rows, wide, backward)
    collect(bands, merged, backward, filter_refs, f)
    lay_toeplitz(others, wide, lon_dev, merged, backward, f, t_ref, e_ref)

    def put(values, first):
        values = values.T
        count = values.shape[0] // lon_dev
        for shard in range(-SMAX, SMAX + 1):
            turned = pltpu.roll(values, -shard * share % height, 1) if shard else values
            at = pl.ds((shard + SMAX) * lon_dev, lon_dev)
            xs[pl.ds(first + 1, count), at, :] = turned.reshape(
                count, lon_dev, height
            )

    per_tile = LANES // lon_dev
    blank = jnp.zeros(xs.shape[1:], BF16)
    if halo_refs:
        band = lax.axis_index("lat")
        above = halo_refs[0][:, pl.ds(cells - LANES, LANES)]
        put(above, 0)
        edge = xs[per_tile].astype(jnp.float32)
        xs[0] = jnp.where(band > 0, edge, 0.0).astype(BF16)
        put(halo_refs[1][:, pl.ds(0, LANES)], 0)
        edge = xs[1].astype(jnp.float32)
        xs[rows + 1] = jnp.where(band < bands - 1, edge, 0.0).astype(BF16)
    else:
        xs[0] = blank
        xs[rows + 1] = blank
    for segment in range(segments):
        put(own_ref[segment], segment * held)
    span = 2 * LANES
    for row in range(rows):
        window = xs[row : row + 3, :span, :].reshape(3 * span, height)
        laid = ahead_ref[ahead.index(row)] if row in ahead else t_ref[others.index(row)]
        total = jnp.dot(laid, window, preferred_element_type=jnp.float32)
        if row in wide:
            beyond = []
            for tap in range(3):
                beyond += [xs[row + tap, span:, :], blank[: LANES - lon_dev]]
            total += jnp.dot(
                e_ref[wide.index(row)],
                jnp.concatenate(beyond, axis=0),
                preferred_element_type=jnp.float32,
            )
        total = total.astype(BF16)
        for k in range(kernels):
            z_ref[pl.ds(row * lon_dev, lon_dev), pl.ds(k * height, height)] = total[
                k * lon_dev : (k + 1) * lon_dev
            ]
    mixer = mixer_of(everyone, share, backward, w_ref, height)
    for segment in range(segments):
        part = z_ref[pl.ds(segment * cells, cells), :]
        mixed = lax.dot_general(mixer, part, ALONG, preferred_element_type=jnp.float32)
        o_ref[segment] = mixed.astype(o_ref.dtype)


def dense_kernel(m_ref, w_ref, g_ref, o_ref, d_ref):
    across = (((0,), (0,)), ((), ()))
    pre = lax.dot_general(m_ref[...], w_ref[...], across, preferred_element_type=jnp.float32)
    slope = 0.7978845608028654
    square = pre * pre
    bent = jnp.tanh(slope * (pre + 0.044715 * (square * pre)))
    half = 0.5 * (1.0 + bent)
    o_ref[...] = (pre * half).astype(o_ref.dtype)
    rise = half + 0.5 * pre * (1.0 - bent * bent) * (slope * (1.0 + 3.0 * 0.044715 * square))
    grad_pre = (g_ref[...].astype(jnp.float32) * rise).astype(BF16)
    d_ref[...] = lax.dot_general(
        w_ref[...], grad_pre, ALONG, preferred_element_type=jnp.float32
    ).astype(d_ref.dtype)


def from_bands(values):
    count = lax.axis_size("lat")
    up = [(i, i + 1) for i in range(count - 1)]
    down = [(j, i) for i, j in up]
    return [lax.ppermute(values, "lat", up), lax.ppermute(values, "lat", down)]


def body(inputs, psi_raw, widths, w_group, w_mix, grad_out):
    row_count, lon_dev, channels = inputs.shape
    kernels = psi_raw.shape[0]
    blocks, bands = lax.axis_size("lon"), lax.axis_size("lat")
    cells = row_count * lon_dev
    merged = bands == 2 and channels % (2 * GROUP * bands * blocks) == 0
    everyone = ("lat", "lon") if merged else ("lon",)
    segments = bands if merged else 1
    share = channels // (segments * blocks)
    height = blocks * share
    rows = segments * row_count
    tables = [
        tuple(max(table[row::rows]) for row in range(rows))
        for table in reaches(row_count, bands)
    ]
    square = jax.ShapeDtypeStruct((channels, cells), BF16)

    def exchange(values):
        parted = values.reshape(segments * blocks, share, cells)
        return lax.all_to_all(parted, everyone, 0, 0)

    turned, own_filters = pl.pallas_call(
        partial(enter_kernel, lon_dev),
        out_shape=(
            square,
            jax.ShapeDtypeStruct((kernels, 3, row_count, 3 * LANES), jnp.float32),
        ),
        in_specs=[
            pl.BlockSpec(memory_space=pltpu.SMEM),
            pl.BlockSpec(memory_space=pltpu.VMEM),
            pl.BlockSpec(memory_space=pltpu.VMEM),
        ],
    )(widths, inputs.reshape(cells, channels), psi_raw.transpose(0, 2, 1, 3))
    columns = exchange(turned)
    if merged:
        filters = [own_filters, lax.ppermute(own_filters, "lat", [(0, 1), (1, 0)])]
    else:
        above, below = from_bands(own_filters)
        filters = [above, own_filters, below]
    pool = (bands if merged else 3, *own_filters.shape)

    widest = [row for row in range(rows) if tables[0][row] == SMAX]
    ahead = len(rows_ahead(rows, widest, False)[0])
    laid = pl.pallas_call(
        partial(table_kernel, widest, rows, bands, lon_dev, merged),
        out_shape=jax.ShapeDtypeStruct((ahead, kernels * lon_dev, 6 * LANES), BF16),
        scratch_shapes=[pltpu.VMEM(pool, jnp.float32)],
        compiler_params=SMALL,
    )(*filters)

    def convolve(values, laid):
        backward = not laid
        values = values.reshape(segments, height, cells)
        halo = [] if merged else from_bands(values[0])
        return pl.pallas_call(
            partial(
                conv_kernel, tables[backward], bands, lon_dev, merged, everyone, share, backward
            ),
            out_shape=jax.ShapeDtypeStruct(values.shape, BF16),
            scratch_shapes=[
                pltpu.VMEM(pool, jnp.float32),
                pltpu.VMEM((rows - ahead * len(laid), kernels * lon_dev, 6 * LANES), BF16),
                pltpu.VMEM((tables[backward].count(SMAX), kernels * lon_dev, 3 * LANES), BF16),
                pltpu.VMEM((rows + 2, (2 * SMAX + 1) * lon_dev, height), BF16),
                pltpu.VMEM((rows * lon_dev, kernels * height), BF16),
            ],
            compiler_params=LARGE,
        )(w_group, values, *laid, *filters, *halo)

    mixed_in = exchange(convolve(columns, [laid]))
    outputs, grad_mixed = pl.pallas_call(
        dense_kernel,
        out_shape=(jax.ShapeDtypeStruct((cells, channels), BF16), square),
        compiler_params=SMALL,
    )(mixed_in.reshape(channels, cells), w_mix, grad_out.reshape(cells, channels))
    grad_in = exchange(convolve(exchange(grad_mixed), []))
    grad_in = transposed(grad_in.reshape(channels, cells))
    return outputs.reshape(inputs.shape), grad_in.reshape(inputs.shape)


def solution(mesh):
    return jax.shard_map(
        body,
        mesh=mesh,
        in_specs=(
            P("lat", "lon", None),
            P(None, "lat", None, None),
            P("lat"),
            P(),
            P(),
            P("lat", "lon", None),
        ),
        out_specs=(P("lat", "lon", None), P("lat", "lon", None)),
        check_vma=False,
    )
```

```python
from functools import partial

import jax
import jax.numpy as jnp
from jax import lax
from jax.experimental import pallas as pl
from jax.experimental.pallas import tpu as pltpu
from jax.sharding import PartitionSpec as P

GROUP = 4
SMAX = 4


LANES = 128
BF16 = jnp.bfloat16
ALONG = (((1,), (1,)), ((), ()))
SMALL = pltpu.CompilerParams(vmem_limit_bytes=4 * 2**20)
LARGE = pltpu.CompilerParams(vmem_limit_bytes=12 * 2**20)


def width_bound(row, row_total):
    pole = min(row, row_total - 1 - row)
    return min(SMAX, max(1, 2 * SMAX // (pole + 1)) + 1)


def reaches(row_count, bands):
    total = row_count * bands
    bound = [width_bound(row, total) for row in range(total)]
    near = [max(bound[max(0, row - 1) : row + 2]) for row in range(total)]
    return bound, near


def iota(shape, axis):
    return lax.broadcasted_iota(jnp.int32, shape, axis)


def transpose_kernel(x_ref, o_ref):
    o_ref[...] = x_ref[...].T


def transposed(values):
    return pl.pallas_call(
        transpose_kernel,
        out_shape=jax.ShapeDtypeStruct(values.shape[::-1], values.dtype),
        compiler_params=SMALL,
    )(values)


def enter_kernel(lon_dev, w_ref, x_ref, p_ref, o_ref, f_ref):
    o_ref[...] = x_ref[...].T
    kernels, taps, rows, cells = p_ref.shape
    shape = (rows, LANES)
    line, lane = iota(shape, 0), iota(shape, 1)
    reach = jnp.zeros(shape, jnp.int32)
    for row in range(rows):
        reach = jnp.where(line == row, w_ref[row] * lon_dev, reach)
    scale = lax.rsqrt(3.0 * (2.0 * reach.astype(jnp.float32) + 1.0))
    for tile in range(3):
        offset = lane + (tile * LANES - SMAX * lon_dev)
        keep = jnp.where(jnp.abs(offset) <= reach, scale, 0.0)
        for k in range(kernels):
            for tap in range(taps):
                if tile < 2:
                    values = p_ref[k, tap, :, pl.ds(tile * LANES, LANES)]
                else:
                    values = p_ref[k, tap, :, pl.ds(cells - 1, 1)]
                    values = jnp.where(lane == 0, values, 0.0)
                f_ref[k, tap, :, pl.ds(tile * LANES, LANES)] = (
                    (values * keep).astype(BF16).astype(jnp.float32)
                )


def collect(bands, merged, backward, filter_refs, f):
    if merged:
        band = lax.axis_index("lat")
        f[band] = filter_refs[0][...]
        f[1 - band] = filter_refs[1][...]
    else:
        for segment, ref in enumerate(filter_refs):
            f[segment] = ref[...]
    if backward:
        segments, kernels, taps, lines, width = f.shape
        shape = (width, width)
        mirror = jnp.where(iota(shape, 0) + iota(shape, 1) == 2 * LANES, 1.0, 0.0).astype(BF16)
        for segment in range(segments):
            values = f[segment].reshape(kernels * taps * lines, width).astype(BF16)
            values = jnp.dot(values, mirror, preferred_element_type=jnp.float32)
            f[segment] = values.reshape(kernels, taps, lines, width)


def lay_toeplitz(rows, wide, lon_dev, merged, backward, f, t_ref, e_ref=None):
    segments, kernels, _, held, _ = f.shape
    shape = (lon_dev, LANES)
    lane, line = iota(shape, 1), iota(shape, 0)
    upper = lane >= line
    corner = lane == line
    for place, row in enumerate(rows):
        for tap in range(3):
            source, column = (row + tap - 1, 2 - tap) if backward else (row, tap)
            source += 0 if merged else held
            segment, inner = divmod(source, held)
            present = 0 <= segment < segments
            for k in range(kernels):
                here = pl.ds(k * lon_dev, lon_dev)

                def turned(tile):
                    values = f[segment, k, column, pl.ds(inner, 1), pl.ds(tile * LANES, LANES)]
                    values = jnp.broadcast_to(values, shape)
                    return pltpu.roll(values, 0, 1, stride=1, stride_axis=0)

                if present:
                    first, second = turned(0), turned(1)
                    parts = [jnp.where(upper, first, 0.0), jnp.where(upper, second, first)]
                else:
                    parts = [jnp.zeros(shape, jnp.float32)] * 2
                for i, part in enumerate(parts):
                    t_ref[place, here, pl.ds((tap * 2 + i) * LANES, LANES)] = part.astype(BF16)
                if e_ref is not None and row in wide:
                    last = parts[0]
                    if present:
                        last = jnp.where(corner, turned(2), jnp.where(upper, 0.0, second))
                    at = pl.ds(tap * LANES, LANES)
                    e_ref[wide.index(row), here, at] = last.astype(BF16)


def mixer_of(everyone, share, backward, w_ref, height):
    kernels, group, channels = w_ref.shape
    first = lax.axis_index(everyone[0])
    for axis in everyone[1:]:
        first = first * lax.axis_size(axis) + lax.axis_index(axis)
    shape = (channels, height)
    chosen = iota(shape, 0) == first * share + iota(shape, 1) % share
    weights = jnp.concatenate([w_ref[k].astype(jnp.float32) for k in range(kernels)], axis=0)
    weights = jnp.dot(
        weights.astype(BF16),
        jnp.where(chosen, 1.0, 0.0).astype(BF16),
        preferred_element_type=jnp.float32,
    )
    if backward:
        spread = [
            jnp.concatenate([weights[k * group : (k + 1) * group]] * (height // group), axis=0)
            for k in range(kernels)
        ]
        spread = jnp.concatenate(spread, axis=1)
    else:
        shape = (kernels * group, kernels * height)
        line, lane = iota(shape, 0), iota(shape, 1)
        pick = line == (lane // height) * group + lane % group
        spread = lax.dot_general(
            weights.astype(BF16),
            jnp.where(pick, 1.0, 0.0).astype(BF16),
            (((0,), (0,)), ((), ())),
            preferred_element_type=jnp.float32,
        )
    shape = (height, kernels * height)
    same = iota(shape, 0) // group == (iota(shape, 1) % height) // group
    return jnp.where(same, spread, 0.0).astype(BF16)


def rows_ahead(rows, wide, backward):
    ahead = [] if backward else [row for row in range(rows) if row not in wide]
    return ahead, [row for row in range(rows) if row not in ahead]


def table_kernel(wide, rows, bands, lon_dev, merged, *refs):
    *filter_refs, t_ref, f = refs
    collect(bands, merged, False, filter_refs, f)
    lay_toeplitz(rows_ahead(rows, wide, False)[0], wide, lon_dev, merged, False, f, t_ref)


def conv_kernel(
    table, bands, lon_dev, merged, everyone, share, backward, w_ref, own_ref, *refs
):
    if not backward:
        ahead_ref, *refs = refs
    count = 2 if merged else 3
    filter_refs, refs = refs[:count], refs[count:]
    *halo_refs, o_ref, f, t_ref, e_ref, xs, z_ref = refs
    segments, height, cells = own_ref.shape
    rows = len(table)
    held = rows // segments
    kernels = f.shape[1]
    wide = [row for row, reach in enumerate(table) if reach == SMAX]
    ahead, others = rows_ahead(rows, wide, backward)
    collect(bands, merged, backward, filter_refs, f)
    lay_toeplitz(others, wide, lon_dev, merged, backward, f, t_ref, e_ref)

    def put(values, first):
        values = values.T
        count = values.shape[0] // lon_dev
        for shard in range(-SMAX, SMAX + 1):
            turned = pltpu.roll(values, -shard * share % height, 1) if shard else values
            at = pl.ds((shard + SMAX) * lon_dev, lon_dev)
            xs[pl.ds(first + 1, count), at, :] = turned.reshape(
                count, lon_dev, height
            )

    per_tile = LANES // lon_dev
    blank = jnp.zeros(xs.shape[1:], BF16)
    if halo_refs:
        band = lax.axis_index("lat")
        above = halo_refs[0][:, pl.ds(cells - LANES, LANES)]
        put(above, 0)
        edge = xs[per_tile].astype(jnp.float32)
        xs[0] = jnp.where(band > 0, edge, 0.0).astype(BF16)
        put(halo_refs[1][:, pl.ds(0, LANES)], 0)
        edge = xs[1].astype(jnp.float32)
        xs[rows + 1] = jnp.where(band < bands - 1, edge, 0.0).astype(BF16)
    else:
        xs[0] = blank
        xs[rows + 1] = blank
    for segment in range(segments):
        put(own_ref[segment], segment * held)
    span = 2 * LANES
    for row in range(rows):
        window = xs[row : row + 3, :span, :].reshape(3 * span, height)
        laid = ahead_ref[ahead.index(row)] if row in ahead else t_ref[others.index(row)]
        total = jnp.dot(laid, window, preferred_element_type=jnp.float32)
        if row in wide:
            beyond = []
            for tap in range(3):
                beyond += [xs[row + tap, span:, :], blank[: LANES - lon_dev]]
            total += jnp.dot(
                e_ref[wide.index(row)],
                jnp.concatenate(beyond, axis=0),
                preferred_element_type=jnp.float32,
            )
        total = total.astype(BF16)
        for k in range(kernels):
            z_ref[pl.ds(row * lon_dev, lon_dev), pl.ds(k * height, height)] = total[
                k * lon_dev : (k + 1) * lon_dev
            ]
    mixer = mixer_of(everyone, share, backward, w_ref, height)
    for segment in range(segments):
        part = z_ref[pl.ds(segment * cells, cells), :]
        mixed = lax.dot_general(mixer, part, ALONG, preferred_element_type=jnp.float32)
        o_ref[segment] = mixed.astype(o_ref.dtype)


def dense_kernel(m_ref, w_ref, g_ref, o_ref, d_ref):
    across = (((0,), (0,)), ((), ()))
    pre = lax.dot_general(m_ref[...], w_ref[...], across, preferred_element_type=jnp.float32)
    slope = 0.7978845608028654
    square = pre * pre
    bent = jnp.tanh(slope * (pre + 0.044715 * (square * pre)))
    half = 0.5 * (1.0 + bent)
    o_ref[...] = (pre * half).astype(o_ref.dtype)
    rise = half + 0.5 * pre * (1.0 - bent * bent) * (slope * (1.0 + 3.0 * 0.044715 * square))
    grad_pre = (g_ref[...].astype(jnp.float32) * rise).astype(BF16)
    d_ref[...] = lax.dot_general(
        w_ref[...], grad_pre, ALONG, preferred_element_type=jnp.float32
    ).astype(d_ref.dtype)


def from_bands(values):
    count = lax.axis_size("lat")
    up = [(i, i + 1) for i in range(count - 1)]
    down = [(j, i) for i, j in up]
    return [lax.ppermute(values, "lat", up), lax.ppermute(values, "lat", down)]


def body(inputs, psi_raw, widths, w_group, w_mix, grad_out):
    row_count, lon_dev, channels = inputs.shape
    kernels = psi_raw.shape[0]
    blocks, bands = lax.axis_size("lon"), lax.axis_size("lat")
    cells = row_count * lon_dev
    merged = bands == 2 and channels % (2 * GROUP * bands * blocks) == 0
    everyone = ("lat", "lon") if merged else ("lon",)
    segments = bands if merged else 1
    share = channels // (segments * blocks)
    height = blocks * share
    rows = segments * row_count
    tables = [
        tuple(max(table[row::rows]) for row in range(rows))
        for table in reaches(row_count, bands)
    ]
    square = jax.ShapeDtypeStruct((channels, cells), BF16)

    def exchange(values):
        parted = values.reshape(segments * blocks, share, cells)
        return lax.all_to_all(parted, everyone, 0, 0)

    turned, own_filters = pl.pallas_call(
        partial(enter_kernel, lon_dev),
        out_shape=(
            square,
            jax.ShapeDtypeStruct((kernels, 3, row_count, 3 * LANES), jnp.float32),
        ),
        in_specs=[
            pl.BlockSpec(memory_space=pltpu.SMEM),
            pl.BlockSpec(memory_space=pltpu.VMEM),
            pl.BlockSpec(memory_space=pltpu.VMEM),
        ],
    )(widths, inputs.reshape(cells, channels), psi_raw.transpose(0, 2, 1, 3))
    columns = exchange(turned)
    if merged:
        filters = [own_filters, lax.ppermute(own_filters, "lat", [(0, 1), (1, 0)])]
    else:
        above, below = from_bands(own_filters)
        filters = [above, own_filters, below]
    pool = (bands if merged else 3, *own_filters.shape)

    widest = [row for row in range(rows) if tables[0][row] == SMAX]
    ahead = len(rows_ahead(rows, widest, False)[0])
    laid = pl.pallas_call(
        partial(table_kernel, widest, rows, bands, lon_dev, merged),
        out_shape=jax.ShapeDtypeStruct((ahead, kernels * lon_dev, 6 * LANES), BF16),
        scratch_shapes=[pltpu.VMEM(pool, jnp.float32)],
        compiler_params=SMALL,
    )(*filters)

    def convolve(values, laid):
        backward = not laid
        values = values.reshape(segments, height, cells)
        halo = [] if merged else from_bands(values[0])
        return pl.pallas_call(
            partial(
                conv_kernel, tables[backward], bands, lon_dev, merged, everyone, share, backward
            ),
            out_shape=jax.ShapeDtypeStruct(values.shape, BF16),
            scratch_shapes=[
                pltpu.VMEM(pool, jnp.float32),
                pltpu.VMEM((rows - ahead * len(laid), kernels * lon_dev, 6 * LANES), BF16),
                pltpu.VMEM((tables[backward].count(SMAX), kernels * lon_dev, 3 * LANES), BF16),
                pltpu.VMEM((rows + 2, (2 * SMAX + 1) * lon_dev, height), BF16),
                pltpu.VMEM((rows * lon_dev, kernels * height), BF16),
            ],
            compiler_params=LARGE,
        )(w_group, values, *laid, *filters, *halo)

    mixed_in = exchange(convolve(columns, [laid]))
    outputs, grad_mixed = pl.pallas_call(
        dense_kernel,
        out_shape=(jax.ShapeDtypeStruct((cells, channels), BF16), square),
        compiler_params=SMALL,
    )(mixed_in.reshape(channels, cells), w_mix, grad_out.reshape(cells, channels))
    grad_in = exchange(convolve(exchange(grad_mixed), []))
    grad_in = transposed(grad_in.reshape(channels, cells))
    return outputs.reshape(inputs.shape), grad_in.reshape(inputs.shape)


def solution(mesh):
    return jax.shard_map(
        body,
        mesh=mesh,
        in_specs=(
            P("lat", "lon", None),
            P(None, "lat", None, None),
            P("lat"),
            P(),
            P(),
            P("lat", "lon", None),
        ),
        out_specs=(P("lat", "lon", None), P("lat", "lon", None)),
        check_vma=False,
    )
```
